32 devices in a mesh: dp: 8 (over y, x, core), mlp: 4 (over z).
Axes of the slice: x: 2, y: 2, z: 4, core: 2. Of those that a mesh axis runs over, the one named last changes fastest.
Arguments:
- tokens: float32 [16384, 1024], P(('dp', 'mlp')), may hold values from -6 to 6
- cotangent: float32 [16384, 1024], P(('dp', 'mlp')), may hold values from -6 to 6
- positions: int32 [16384], P(('dp', 'mlp')), may hold values from 0 to 511, as said below
- owners: int32 [4, 192], P('mlp'), may hold values from 0 to 191, as said below
- masters: float32 [4, 192, 128, 128], P('mlp', 'dp')
- basis_left: float32 [4, 192, 128, 128], P('mlp', 'dp'), as said below
- basis_right: float32 [4, 192, 128, 128], P('mlp', 'dp'), as said below
- moment1: float32 [4, 192, 128, 128], P('mlp', 'dp')
- moment2: float32 [4, 192, 128, 128], P('mlp', 'dp'), as said below
- ema: float32 [4, 192, 128, 128], P('mlp', 'dp')
- vectors: float32 [9, 1024], replicated, as said below
- vector_moment1: float32 [9, 1024], replicated
- vector_moment2: float32 [9, 1024], replicated, as said below
- hidden_bias: float32 [4096], replicated, may hold values from -1.8 to 1.8
- hidden_moment1: float32 [4096], replicated
- hidden_moment2: float32 [4096], replicated, as said below
Outputs:
- result: float32 [16384, 1024], P(('dp', 'mlp'))
- grad_tokens: float32 [16384, 1024], P(('dp', 'mlp'))
- block_grad: float32 [4, 192, 128, 128], P('mlp', 'dp')
- moment1_new: float32 [4, 192, 128, 128], P('mlp', 'dp')
- moment2_new: float32 [4, 192, 128, 128], P('mlp', 'dp')
- master_new: float32 [4, 192, 128, 128], P('mlp', 'dp')
- weight_copy: bfloat16 [4, 192, 128, 128], P('mlp', 'dp')
- ema_new: float32 [4, 192, 128, 128], P('mlp', 'dp')
- vector_grad: float32 [9, 1024], replicated
- vector_moment1_new: float32 [9, 1024], replicated
- vector_moment2_new: float32 [9, 1024], replicated
- vectors_new: float32 [9, 1024], replicated
- hidden_grad: float32 [4096], replicated
- hidden_moment1_new: float32 [4096], replicated
- hidden_moment2_new: float32 [4096], replicated
- hidden_new: float32 [4096], replicated
The draws below stay inside these ranges and needn't reach their ends.
Inputs may be any that keep to these rules, and one draw needn't show every extreme that they name: Each row of owners names every slot of 0 to 191 once. Each sequence of 512 tokens is packed with documents; positions count from 0 at the first token of each document and rise by one from token to token within it; the first sequence is one document. `basis_left`: each slot is an orthogonal 128 x 128 matrix. `basis_right`: each slot is an orthogonal 128 x 128 matrix. `moment2`: positive. `vector_moment2`: positive. `hidden_moment2`: positive. `vectors`: rows 0 and 2 lie between 0.5 and 1.5.
All inputs are finite; a program needn't handle non-finite values.
Results may differ from the reference program's by a relative error of at most 0.0095.
Values may be sent and summed in bfloat16 or wider, within the bound.
A program may use at most 192 MiB of HBM per device.

```python
import math
import jax
import jax.numpy as jnp
from jax import lax

D = 1024
HEADS = 16
HDIM = 64
ROT = 16
FF = 4096
LEN = 512
BLK = 128
STEP = 5
COLUMNS = 4
TOKENS = 16384
ABLK = 256
UNITS = 192


grad_coeffs = (0.3, 0.3, 0.3, 0.35, 0.3, 0.65)


vector_coeffs = (0.5, 0.5, 0.6, 0.6, 0.3, 0.3, 0.3, 1.0, 1.0)


def owner_table(key):
    keys = jax.random.split(jax.random.fold_in(key, 101), COLUMNS)
    return jax.vmap(lambda single: jax.random.permutation(single, UNITS))(keys).astype(jnp.int32)


def slot_kinds(key):
    table = owner_table(key)
    per_att = ABLK // COLUMNS
    square = (D // BLK) ** 2
    hidden_tiles = D // BLK * (FF // COLUMNS // BLK)
    unit_ids = jnp.arange(UNITS, dtype=jnp.int32)[None, :]
    column_ids = jnp.arange(COLUMNS, dtype=jnp.int32)[:, None]
    attn_kind = (column_ids * per_att + unit_ids) // square
    kinds = jnp.where(unit_ids < per_att, attn_kind, jnp.where(unit_ids < per_att + hidden_tiles, 4, 5))
    kinds = jnp.broadcast_to(kinds, (COLUMNS, UNITS)).astype(jnp.int32)
    rows_all = jnp.broadcast_to(column_ids, (COLUMNS, UNITS))
    return jnp.zeros((COLUMNS, UNITS), jnp.int32).at[rows_all, table].set(kinds)


def kind_scale(key, scales):
    return jnp.asarray(scales, jnp.float32)[slot_kinds(key)][:, :, None, None]


def weight_stds():
    return (D ** (-0.5), D ** (-0.5), D ** (-0.5), 4.0 * D ** (-0.5), D ** (-0.5), FF ** (-0.5))


def grad_sizes():
    root = math.sqrt(TOKENS)
    return tuple((coeff * root for coeff in grad_coeffs))


def orthogonal(key):
    count_all = COLUMNS * UNITS
    keys = jax.random.split(key, count_all)
    freq = jnp.arange(BLK, dtype=jnp.float32)[:, None]
    place = jnp.arange(BLK, dtype=jnp.float32)[None, :]
    table = jnp.cos(math.pi * (2.0 * place + 1.0) * freq / (2.0 * BLK)) * math.sqrt(2.0 / BLK)
    table = jnp.where(freq == 0.0, table * math.sqrt(0.5), table)

    def one_slot(single):
        first_key, second_key, third_key, fourth_key = jax.random.split(single, 4)
        row_perm = jax.random.permutation(first_key, BLK)
        col_perm = jax.random.permutation(second_key, BLK)
        row_sign = (2 * jax.random.randint(third_key, (BLK,), 0, 2) - 1).astype(jnp.float32)
        col_sign = (2 * jax.random.randint(fourth_key, (BLK,), 0, 2) - 1).astype(jnp.float32)
        return table[row_perm][:, col_perm] * row_sign[:, None] * col_sign[None, :]
    return jax.vmap(one_slot)(keys).reshape(COLUMNS, UNITS, BLK, BLK)


def draw_owners(key, part):
    return owner_table(key)


def draw_positions(key, part):
    seq_count = TOKENS // LEN
    place = jnp.arange(LEN, dtype=jnp.int32)[None, :]
    picks = jax.random.randint(jax.random.fold_in(key, 8), (seq_count, LEN), 0, max(2, LEN // 4))
    starts = (picks == 0) | (place == 0)
    seq_ids = jnp.arange(seq_count, dtype=jnp.int32)[:, None]
    starts = jnp.where(seq_ids == 0, place == 0, starts)
    marks = jnp.where(starts, place, 0).astype(jnp.int32)
    begin = lax.cummax(marks, axis=1)
    return (place - begin).reshape(TOKENS).astype(jnp.int32)


def draw_masters(key, part):
    noise = jax.random.truncated_normal(jax.random.fold_in(key, 1), -4.0, 4.0, (COLUMNS, UNITS, BLK, BLK), jnp.float32)
    return kind_scale(key, weight_stds()) * noise


def draw_ema(key, part):
    noise = jax.random.truncated_normal(jax.random.fold_in(key, 2), -4.0, 4.0, (COLUMNS, UNITS, BLK, BLK), jnp.float32)
    return kind_scale(key, weight_stds()) * noise


def draw_moment1(key, part):
    noise = jax.random.truncated_normal(jax.random.fold_in(key, 3), -4.0, 4.0, (COLUMNS, UNITS, BLK, BLK), jnp.float32)
    return kind_scale(key, grad_sizes()) * noise


def draw_moment2(key, part):
    sizes_sq = kind_scale(key, tuple((size * size for size in grad_sizes())))
    per_slot = jax.random.uniform(jax.random.fold_in(key, 4), (COLUMNS, UNITS, 1, 1), jnp.float32, 1.0, 4.0)
    per_entry = jax.random.uniform(jax.random.fold_in(key, 5), (COLUMNS, UNITS, BLK, BLK), jnp.float32, 0.5, 2.0)
    return sizes_sq * per_slot * per_entry


def draw_basis_left(key, part):
    return orthogonal(jax.random.fold_in(key, 6))


def draw_basis_right(key, part):
    return orthogonal(jax.random.fold_in(key, 7))


def draw_vectors(key, part):
    row_ids = jnp.arange(9, dtype=jnp.int32)[:, None]
    gains = 1.0 + 0.5 * jax.random.uniform(jax.random.fold_in(key, 9), (9, D), jnp.float32, -1.0, 1.0)
    biases = 0.3 * jax.random.truncated_normal(jax.random.fold_in(key, 10), -4.0, 4.0, (9, D), jnp.float32)
    return jnp.where((row_ids == 0) | (row_ids == 2), gains, biases)


def draw_vector_moment1(key, part):
    coeffs = jnp.asarray(vector_coeffs, jnp.float32)[:, None] * math.sqrt(TOKENS)
    return coeffs * jax.random.truncated_normal(jax.random.fold_in(key, 11), -4.0, 4.0, (9, D), jnp.float32)


def draw_vector_moment2(key, part):
    coeffs = jnp.asarray(vector_coeffs, jnp.float32)[:, None]
    per_row = jax.random.uniform(jax.random.fold_in(key, 12), (9, 1), jnp.float32, 1.0, 4.0)
    per_entry = jax.random.uniform(jax.random.fold_in(key, 13), (9, D), jnp.float32, 0.5, 2.0)
    return coeffs * coeffs * TOKENS * per_row * per_entry


def draw_hidden_moment1(key, part):
    return 0.3 * math.sqrt(TOKENS) * jax.random.truncated_normal(jax.random.fold_in(key, 14), -4.0, 4.0, (FF,), jnp.float32)


def draw_hidden_moment2(key, part):
    return 0.09 * TOKENS * jax.random.uniform(jax.random.fold_in(key, 15), (FF,), jnp.float32, 0.5, 8.0)


def shard_levels(own_key, extent, cuts, low, top_value):
    def one(position, parts):
        heights = jax.random.uniform(jax.random.fold_in(jax.random.fold_in(own_key, 6), position), (parts,), jnp.float32, low / len(cuts), top_value / len(cuts))
        return jnp.repeat(jnp.exp(heights), extent[position] // parts).reshape((-1,) + (1,) * (len(extent) - position - 1))

    factor_of = one(*cuts[0])
    for cut in cuts[1:]:
        factor_of = factor_of * one(*cut)
    return factor_of


def normal_values(key, shape, scale, limit, cuts=(), kind=jnp.bfloat16):
    gain = shard_levels(key, shape, cuts, -0.22, 0.18) if cuts else 1.0
    drawn = jax.random.normal(key, shape, jnp.float32) * scale * gain
    return jnp.minimum(jnp.maximum(drawn, -limit), limit).astype(kind)


def setup_inputs(seed: int = 0) -> dict:
    key_list = jax.random.split(jax.random.key(seed), 17)
    tokens = normal_values(key_list[0], (TOKENS, D), 1.0, 6.0, ((0, 32),), jnp.float32)
    cotangent = normal_values(key_list[1], (TOKENS, D), 1.0, 6.0, ((0, 32),), jnp.float32)
    positions = draw_positions(jax.random.fold_in(key_list[16], 71), 0)
    owners = draw_owners(jax.random.fold_in(key_list[16], 71), 0)
    masters = draw_masters(jax.random.fold_in(key_list[16], 71), 0)
    basis_left = draw_basis_left(jax.random.fold_in(key_list[16], 71), 0)
    basis_right = draw_basis_right(jax.random.fold_in(key_list[16], 71), 0)
    moment1 = draw_moment1(jax.random.fold_in(key_list[16], 71), 0)
    moment2 = draw_moment2(jax.random.fold_in(key_list[16], 71), 0)
    ema = draw_ema(jax.random.fold_in(key_list[16], 71), 0)
    vectors = draw_vectors(jax.random.fold_in(key_list[16], 71), 0)
    vector_moment1 = draw_vector_moment1(jax.random.fold_in(key_list[16], 71), 0)
    vector_moment2 = draw_vector_moment2(jax.random.fold_in(key_list[16], 71), 0)
    hidden_bias = normal_values(key_list[13], (FF,), 0.3, 1.8, (), jnp.float32)
    hidden_moment1 = draw_hidden_moment1(jax.random.fold_in(key_list[16], 71), 0)
    hidden_moment2 = draw_hidden_moment2(jax.random.fold_in(key_list[16], 71), 0)
    return {"tokens": tokens, "cotangent": cotangent, "positions": positions, "owners": owners, "masters": masters, "basis_left": basis_left, "basis_right": basis_right, "moment1": moment1, "moment2": moment2, "ema": ema, "vectors": vectors, "vector_moment1": vector_moment1, "vector_moment2": vector_moment2, "hidden_bias": hidden_bias, "hidden_moment1": hidden_moment1, "hidden_moment2": hidden_moment2}


PRECISE = lax.Precision.HIGHEST
eps_norm = 1e-05
eps_adam = 1e-08
lr_matrix = 0.05
lr_vector = 0.5
ema_keep = 0.8

@jax.custom_vjp
def low(v):
    return lax.optimization_barrier(v.astype(jnp.bfloat16)).astype(jnp.float32)

@jax.custom_vjp
def low_back(v):
    return v

def low_keep(v):
    return (low(v), None)

def low_pass(kept, grad):
    return (grad,)

def back_keep(v):
    return (v, None)

def back_low(kept, grad):
    return (low(grad),)
low.defvjp(low_keep, low_pass)
low_back.defvjp(back_keep, back_low)

def layer_norm(values, gain_vec, shift_vec):
    centered = values - lax.optimization_barrier(jnp.mean(values, axis=-1, keepdims=True))
    variance = lax.optimization_barrier(jnp.mean(centered * centered, axis=-1, keepdims=True))
    return centered * lax.rsqrt(variance + eps_norm) * gain_vec + shift_vec

def rotate(values, cos_table, sin_table):
    half_rot = ROT // 2
    first_half = values[..., :half_rot]
    second_half = values[..., half_rot:ROT]
    return jnp.concatenate([first_half * cos_table - second_half * sin_table, second_half * cos_table + first_half * sin_table, values[..., ROT:]], axis=-1)

def angle_tables(positions):
    inverse_freq = 10000.0 ** (-(jnp.arange(ROT // 2, dtype=jnp.float32) * 2.0) / ROT)
    angles = positions.astype(jnp.float32)[..., None] * inverse_freq
    return (jnp.cos(angles)[..., None, :], jnp.sin(angles)[..., None, :])

def to_matrix(tiles, rows_count, cols_count):
    size_tile = tiles.shape[1]
    return tiles.reshape(rows_count, cols_count, size_tile, size_tile).transpose(0, 2, 1, 3).reshape(rows_count * size_tile, cols_count * size_tile)

def to_tiles(matrix, size_tile):
    rows_count = matrix.shape[0] // size_tile
    cols_count = matrix.shape[1] // size_tile
    return matrix.reshape(rows_count, size_tile, cols_count, size_tile).transpose(0, 2, 1, 3).reshape(rows_count * cols_count, size_tile, size_tile)

def attend(queries, key_low, values):
    rows_per = min(512, LEN)
    count_blocks = LEN // rows_per
    scale = HDIM ** (-0.5)
    key_place = jnp.arange(LEN, dtype=jnp.int32)

    def one_block(step_index):
        query_rows = lax.dynamic_slice_in_dim(queries, step_index * rows_per, rows_per, 0)
        scores = jnp.einsum('qhd,khd->hqk', query_rows, key_low, precision=PRECISE)
        scores = low_back(scores * scale)
        row_place = step_index * rows_per + jnp.arange(rows_per, dtype=jnp.int32)
        scores = jnp.where(key_place[None, None, :] <= row_place[None, :, None], scores, -1e+30)
        peak = lax.optimization_barrier(jnp.max(scores, axis=-1, keepdims=True))
        raised = jnp.exp(scores - peak)
        attn_prob = low(raised / lax.optimization_barrier(jnp.sum(raised, axis=-1, keepdims=True)))
        return jnp.einsum('hqk,khd->qhd', attn_prob, values, precision=PRECISE)
    outputs = lax.map(jax.checkpoint(one_block), jnp.arange(count_blocks, dtype=jnp.int32))
    return outputs.reshape(LEN, HEADS, HDIM)

def forward(group_tokens, cos_table, sin_table, weights, vectors, hidden_bias):
    w_query, w_key, w_value, w_output, w_up, w_down = weights
    groups = group_tokens.shape[0]
    flat = group_tokens.reshape(groups * LEN, D)
    normed = low(layer_norm(flat, vectors[0], vectors[1]))
    query_pre = low_back(jnp.dot(normed, w_query, precision=PRECISE) + vectors[4])
    key_pre = low_back(jnp.dot(normed, w_key, precision=PRECISE) + vectors[5])
    values = low(low_back(jnp.dot(normed, w_value, precision=PRECISE) + vectors[6]))
    queries = low(rotate(query_pre.reshape(groups, LEN, HEADS, HDIM), cos_table, sin_table))
    key_low = low(rotate(key_pre.reshape(groups, LEN, HEADS, HDIM), cos_table, sin_table))
    attended = jax.vmap(attend)(queries, key_low, values.reshape(groups, LEN, HEADS, HDIM))
    attended = low(low_back(attended.reshape(groups * LEN, D)))
    branch_attn = low_back(jnp.dot(attended, w_output, precision=PRECISE) + vectors[7])
    normed_ff = low(layer_norm(flat, vectors[2], vectors[3]))
    pre_act = low_back(jnp.dot(normed_ff, w_up, precision=PRECISE) + hidden_bias)
    hidden_act = low(jax.nn.gelu(pre_act, approximate=False))
    branch_ff = low_back(jnp.dot(hidden_act, w_down, precision=PRECISE) + vectors[8])
    return (flat + branch_attn + branch_ff).reshape(groups, LEN, D)

def soap_step(grad, left, right, first, second, master, average):
    bias_fix = 1.0 - 0.5 ** STEP
    turned = jnp.einsum('...ji,...jk->...ik', left, grad, precision=PRECISE)
    turned = jnp.einsum('...ik,...kl->...il', turned, right, precision=PRECISE)
    first_new = 0.5 * first + 0.5 * turned
    second_new = 0.5 * second + 0.5 * turned * turned
    scaled = first_new / bias_fix / (jnp.sqrt(second_new / bias_fix) + eps_adam)
    back = jnp.einsum('...ij,...jk->...ik', left, scaled, precision=PRECISE)
    back = jnp.einsum('...ik,...lk->...il', back, right, precision=PRECISE)
    master_new = master - lr_matrix * back
    return (first_new, second_new, master_new, master_new.astype(jnp.bfloat16), ema_keep * average + (1.0 - ema_keep) * master_new)

def adam_step(grad, first, second, param):
    bias_fix = 1.0 - 0.5 ** STEP
    first_new = 0.5 * first + 0.5 * grad
    second_new = 0.5 * second + 0.5 * grad * grad
    return (first_new, second_new, param - lr_vector * (first_new / bias_fix) / (jnp.sqrt(second_new / bias_fix) + eps_adam))

def reference(tokens, cotangent, positions, owners, masters, basis_left, basis_right, moment1, moment2, ema, vectors, vector_moment1, vector_moment2, hidden_bias, hidden_moment1, hidden_moment2):
    tiles_row = D // BLK
    tiles_hidden = FF // COLUMNS // BLK
    hidden_tiles = tiles_row * tiles_hidden
    per_att = ABLK // COLUMNS
    square = tiles_row * tiles_row
    ordered = jax.vmap(lambda slot_table, slot_order: jnp.take(slot_table, slot_order, axis=0))(masters, owners)
    ordered = low(ordered)
    attn_tiles = ordered[:, :per_att].reshape(ABLK, BLK, BLK)
    w_query = to_matrix(attn_tiles[0:square], tiles_row, tiles_row)
    w_key = to_matrix(attn_tiles[square:2 * square], tiles_row, tiles_row)
    w_value = to_matrix(attn_tiles[2 * square:3 * square], tiles_row, tiles_row)
    w_output = to_matrix(attn_tiles[3 * square:], tiles_row, tiles_row)
    w_up = ordered[:, per_att:per_att + hidden_tiles].reshape(COLUMNS, tiles_row, tiles_hidden, BLK, BLK).transpose(1, 3, 0, 2, 4).reshape(D, FF)
    w_down = ordered[:, per_att + hidden_tiles:].reshape(COLUMNS, tiles_hidden, tiles_row, BLK, BLK).transpose(0, 1, 3, 2, 4).reshape(FF, D)
    seq_count = TOKENS // LEN
    group_size = min(seq_count, max(1, 4096 // LEN))
    step_count = seq_count // group_size
    cos_table, sin_table = angle_tables(positions.reshape(step_count, group_size, LEN))
    params = ((w_query, w_key, w_value, w_output, w_up, w_down), vectors, hidden_bias)

    def run_group(carried, pieces):
        part_tokens, part_grad, part_cos, part_sin = pieces

        def apply(values_in, params_all):
            return forward(values_in, part_cos, part_sin, params_all[0], params_all[1], params_all[2])
        output, pull = jax.vjp(apply, part_tokens, params)
        grad_in, grad_params = pull(part_grad)
        carried = jax.tree.map(lambda left_part, right_part: left_part + right_part, carried, grad_params)
        return (carried, (output, grad_in))
    zeros_all = jax.tree.map(jnp.zeros_like, params)
    grads, (outputs, grads_in) = lax.scan(run_group, zeros_all, (tokens.reshape(step_count, group_size, LEN, D), cotangent.reshape(step_count, group_size, LEN, D), cos_table, sin_table))
    result = outputs.reshape(TOKENS, D)
    grad_tokens = grads_in.reshape(TOKENS, D)
    (grad_q, grad_k, grad_v, grad_o, grad_up, grad_down), vector_grad, hidden_grad = grads
    attn_grad = jnp.concatenate([to_tiles(grad_q, BLK), to_tiles(grad_k, BLK), to_tiles(grad_v, BLK), to_tiles(grad_o, BLK)], axis=0).reshape(COLUMNS, per_att, BLK, BLK)
    up_grad = grad_up.reshape(tiles_row, BLK, COLUMNS, tiles_hidden, BLK).transpose(2, 0, 3, 1, 4).reshape(COLUMNS, hidden_tiles, BLK, BLK)
    down_grad = grad_down.reshape(COLUMNS, tiles_hidden, BLK, tiles_row, BLK).transpose(0, 1, 3, 2, 4).reshape(COLUMNS, hidden_tiles, BLK, BLK)
    unit_grad = jnp.concatenate([attn_grad, up_grad, down_grad], axis=1)
    inverse = jax.vmap(lambda slot_order: jnp.zeros((UNITS,), jnp.int32).at[slot_order].set(jnp.arange(UNITS, dtype=jnp.int32)))(owners)
    block_grad = jax.vmap(lambda unit_table, unit_order: jnp.take(unit_table, unit_order, axis=0))(unit_grad, inverse)
    first_new, second_new, master_new, weight_copy, ema_new = soap_step(block_grad, basis_left, basis_right, moment1, moment2, masters, ema)
    vec_first, vec_second, vectors_new = adam_step(vector_grad, vector_moment1, vector_moment2, vectors)
    hid_first, hid_second, hidden_new = adam_step(hidden_grad, hidden_moment1, hidden_moment2, hidden_bias)
    return (result, grad_tokens, block_grad, first_new, second_new, master_new, weight_copy, ema_new, vector_grad, vec_first, vec_second, vectors_new, hidden_grad, hid_first, hid_second, hidden_new)
```

```python
import functools

import jax
import jax.numpy as jnp
from jax import lax
from jax.experimental import pallas as pl
from jax.experimental.pallas import tpu as pltpu
from jax.sharding import PartitionSpec as P

HEADS = 16
HDIM = 64
ROT = 16
FF = 4096
STEP = 5
TILE = 128
LANES = 128
GROUP = 4

PRECISE = lax.Precision.HIGHEST
eps_norm = 1e-05
eps_adam = 1e-08
lr_matrix = 0.05
lr_vector = 0.5
ema_keep = 0.8

F32 = jnp.float32
BF16 = jnp.bfloat16
ANY = pl.BlockSpec(memory_space=pl.ANY)
VMEM = pl.BlockSpec(memory_space=pltpu.VMEM)
SMEM = pl.BlockSpec(memory_space=pltpu.SMEM)


def dot_nn(left, right):
    return jnp.dot(left, right, preferred_element_type=F32)


def dot_nt(left, right):
    return lax.dot_general(left, right, (((1,), (1,)), ((), ())), preferred_element_type=F32)


def dot_tn(left, right):
    return lax.dot_general(left, right, (((0,), (0,)), ((), ())), preferred_element_type=F32)


def precise(left, right, left_dim, right_dim):
    return lax.dot_general(
        left,
        right,
        (((left_dim,), (right_dim,)), ((), ())),
        precision=PRECISE,
        preferred_element_type=F32,
    )


def swap_dp(value, bit):
    count = lax.axis_size("dp")
    return lax.ppermute(value, "dp", [(i, i ^ bit) for i in range(count)])


def swap_z(value, bit):
    count = lax.axis_size("mlp")
    return lax.ppermute(value, "mlp", [(i, i ^ bit) for i in range(count)])


def gather_dp(block):
    count = lax.axis_size("dp")
    bits = [1 << i for i in range(1, count.bit_length() - 1)]
    rows = block.shape[0]
    half = rows // 2
    held = [{0: block[:half]}, {0: block[half:]}]
    for step in range(len(bits)):
        for place, order in ((0, bits), (1, bits[::-1])):
            bit = order[step]
            for at in list(held[place]):
                held[place][at ^ bit] = swap_dp(held[place][at], bit)
    parts = []
    for place in (0, 1):
        for at in list(held[place]):
            held[place][at ^ 1] = swap_dp(held[place][at], 1)
        parts += [(at * rows + place * half, held[place][at]) for at in sorted(held[place])]
    return parts


def gather_q(block):
    count = lax.axis_size("dp") // 2
    return [block] + [swap_dp(block, at << 1) for at in range(1, count)]


def reduce_q(stacked):
    total = stacked[0].astype(F32)
    for at in range(1, stacked.shape[0]):
        total = total + swap_dp(stacked[at], at << 1).astype(F32)
    return total


def gather_group(block):
    core = swap_dp(block, 1)
    along = swap_z(block, 1)
    return [block, core, along, swap_dp(along, 1)]


def all_sum(value):
    for i in range(lax.axis_size("dp").bit_length() - 1):
        value = value + swap_dp(value, 1 << i)
    for i in range(lax.axis_size("mlp").bit_length() - 1):
        value = value + swap_z(value, 1 << i)
    return value


def attn_unit(column, rank, place):
    by_columns = (place // 2) * 8 + 2 * rank + place % 2
    by_rows = (2 * rank + place // 8) * 8 + place % 8
    return jnp.where(column == 3, by_rows, by_columns)


def ff_unit(core, place):
    later = place - 32
    up = 64 + (place // 4) * 8 + core * 4 + place % 4
    down = 128 + (core * 4 + later // 8) * 8 + later % 8
    return jnp.where(place < 32, up, down)


def load_parts(offsets, part_refs, slab, sems):
    copies = []
    for number, (offset, ref) in enumerate(zip(offsets, part_refs)):
        copies.append(
            pltpu.make_async_copy(ref, slab.at[pl.ds(offset, ref.shape[0]), :], sems.at[number])
        )
    for copy in copies:
        copy.start()
    for copy in copies:
        copy.wait()


def pick_kernel(offsets, slots, replicas, place_ref, owner_ref, *refs):
    count = len(offsets)
    part_refs = refs[:count]
    own_attn, send1, send2, send3, own_ff, send_ff, slab, sems = refs[count:]
    me, column = place_ref[0], place_ref[1]
    core, quarter = me % 2, me // 2
    low = column % 2
    load_parts(offsets, part_refs, slab, sems)

    def tile_row(unit):
        slot = owner_ref[unit]
        return pl.multiple_of((((slot // slots) ^ me) * slots + slot % slots) * TILE, TILE)

    def fill(out_ref, first_row, unit_of):
        rows = out_ref.shape[0]
        size = min(TILE, rows)

        def body(step, carry):
            row = first_row + step * size
            source = pl.multiple_of(tile_row(unit_of(row // TILE)) + row % TILE, size)
            out_ref[pl.ds(pl.multiple_of(step * size, size), size), :] = slab[
                pl.ds(source, size), :
            ]
            return carry

        lax.fori_loop(0, rows // size, body, 0)

    for bit, out_ref in ((1, send1), (2, send2), (3, send3)):
        rank = 2 * (low ^ (bit & 1)) + core
        fill(
            out_ref,
            quarter * out_ref.shape[0],
            functools.partial(attn_unit, column, rank),
        )
    fill(send_ff, quarter * send_ff.shape[0], functools.partial(ff_unit, core))
    fill(own_attn, 0, functools.partial(attn_unit, column, 2 * low + core))
    fill(own_ff, 0, functools.partial(ff_unit, core))


def pick(place, owner_row, parts, slots, replicas):
    offsets = [offset for offset, _ in parts]
    total = sum(part.shape[0] for _, part in parts)
    shapes = [16 * TILE] + [16 * TILE // replicas] * 3 + [64 * TILE, 64 * TILE // replicas]
    return pl.pallas_call(
        functools.partial(pick_kernel, offsets, slots, replicas),
        out_shape=[jax.ShapeDtypeStruct((rows, LANES), BF16) for rows in shapes],
        in_specs=[SMEM, SMEM] + [ANY] * len(parts),
        out_specs=[VMEM] * len(shapes),
        scratch_shapes=[
            pltpu.VMEM((total, LANES), BF16),
            pltpu.SemaphoreType.DMA((len(parts),)),
        ],
        compiler_params=pltpu.CompilerParams(vmem_limit_bytes=24 << 20),
        cost_estimate=pl.CostEstimate(flops=0, bytes_accessed=16 << 20, transcendentals=0),
        name="pick",
    )(place, owner_row, *[part for _, part in parts])


def erf_f32(value):
    value = jnp.clip(value, -3.832506856900711, 3.832506856900711)
    square = value * value
    top = jnp.full_like(square, 0.00022905065861350646)
    for coeff in (
        0.0034082910107109506,
        0.050955695062380861,
        0.18520832239976145,
        1.128379143519084,
    ):
        top = top * square + coeff
    low = jnp.full_like(square, -1.1791602954361697e-7)
    for coeff in (
        0.000023547966471313185,
        0.0010179625278914885,
        0.014070470171167667,
        0.11098505178285362,
        0.49746925110067538,
        1.0,
    ):
        low = low * square + coeff
    return value * top / low


def ff_kernel(count, has_acc, replicas, *refs):
    refs = list(refs)
    take = lambda number: [refs.pop(0) for _ in range(number)]
    place_ref, norm_ref, bias_ref = take(3)
    h_refs, c_refs, part_refs = take(4), take(4), take(count)
    acc_refs = take(2) if has_acc else None
    out_ref, gd_ref, dw_ref, vec_ref, hid_ref = take(5)
    h_all, c_all, tiles, up, down, up_acc, down_acc, sems = take(8)
    quarter = place_ref[2]
    copies = []
    for number in range(4):
        copies.append(pltpu.make_async_copy(h_refs[number], h_all.at[number], sems.at[number]))
        copies.append(pltpu.make_async_copy(c_refs[number], c_all.at[number], sems.at[4 + number]))
    for copy in copies:
        copy.start()
    rows_part = part_refs[0].shape[0]
    for at in range(count):
        where = (at ^ quarter) if count > 1 else 0
        tiles[pl.ds(pl.multiple_of(where * rows_part, TILE), rows_part), :] = part_refs[at][...]
    for at in range(32):
        up[(at // 4) * TILE : (at // 4 + 1) * TILE, (at % 4) * TILE : (at % 4 + 1) * TILE] = tiles[
            at * TILE : (at + 1) * TILE, :
        ]
        down[(at // 8) * TILE : (at // 8 + 1) * TILE, (at % 8) * TILE : (at % 8 + 1) * TILE] = (
            tiles[(32 + at) * TILE : (33 + at) * TILE, :]
        )
    up_acc[...] = jnp.zeros_like(up_acc)
    down_acc[...] = jnp.zeros_like(down_acc)
    vec_ref[...] = jnp.zeros_like(vec_ref)
    hid_ref[...] = jnp.zeros_like(hid_ref)
    for copy in copies:
        copy.wait()

    def body(at, carry):
        hat = h_all[at].astype(F32)
        normed = (hat * norm_ref[2:3, :] + norm_ref[3:4, :]).astype(BF16)
        cot = c_all[at]
        pre = dot_nn(normed, up[...]) + bias_ref[...]
        cdf = 0.5 + 0.5 * erf_f32(pre * 0.7071067811865476)
        hidden = (pre * cdf).astype(BF16)
        grad = dot_nt(cot, down[...])
        grad = grad * (cdf + pre * (jnp.exp(-0.5 * pre * pre) * 0.3989422804014327))
        grad = grad.astype(BF16)
        hid_ref[...] += jnp.sum(grad.astype(F32), axis=0, keepdims=True)
        out = dot_nn(hidden, down[...])
        back = dot_nt(grad, up[...])
        vec_ref[0:1, :] += jnp.sum(back * hat, axis=0, keepdims=True)
        vec_ref[1:2, :] += jnp.sum(back, axis=0, keepdims=True)
        back = back * norm_ref[2:3, :]
        if acc_refs is not None:
            out = out + acc_refs[0][at].astype(F32)
            back = back + acc_refs[1][at].astype(F32)
        out_ref[at] = out.astype(BF16)
        gd_ref[at] = back.astype(BF16)
        up_acc[...] += dot_tn(normed, grad)
        down_acc[...] += dot_tn(hidden, cot)
        return carry

    lax.fori_loop(0, 4, body, 0)
    rows_out = dw_ref.shape[1]
    per = rows_out // TILE
    for at in range(64):
        if at < 32:
            tile = up_acc[
                (at // 4) * TILE : (at // 4 + 1) * TILE, (at % 4) * TILE : (at % 4 + 1) * TILE
            ]
        else:
            low = at - 32
            tile = down_acc[
                (low // 8) * TILE : (low // 8 + 1) * TILE, (low % 8) * TILE : (low % 8 + 1) * TILE
            ]
        dw_ref[(at // per) ^ quarter, (at % per) * TILE : (at % per + 1) * TILE, :] = tile.astype(
            BF16
        )


def feed_forward(place, vectors, bias, hats, cots, parts, acc, replicas):
    length, width = hats[0].shape
    hidden = 4 * TILE
    rows_out = 64 * TILE // replicas
    acc_list = list(acc) if acc is not None else []
    return pl.pallas_call(
        functools.partial(ff_kernel, len(parts), acc is not None, replicas),
        out_shape=[
            jax.ShapeDtypeStruct((4, length, width), BF16),
            jax.ShapeDtypeStruct((4, length, width), BF16),
            jax.ShapeDtypeStruct((replicas, rows_out, LANES), BF16),
            jax.ShapeDtypeStruct((2, width), F32),
            jax.ShapeDtypeStruct((1, hidden), F32),
        ],
        in_specs=[SMEM, VMEM, VMEM] + [ANY] * 8 + [VMEM] * (len(parts) + len(acc_list)),
        out_specs=[VMEM] * 5,
        scratch_shapes=[
            pltpu.VMEM((4, length, width), BF16),
            pltpu.VMEM((4, length, width), BF16),
            pltpu.VMEM((64 * TILE, LANES), BF16),
            pltpu.VMEM((width, hidden), BF16),
            pltpu.VMEM((hidden, width), BF16),
            pltpu.VMEM((width, hidden), F32),
            pltpu.VMEM((hidden, width), F32),
            pltpu.SemaphoreType.DMA((8,)),
        ],
        compiler_params=pltpu.CompilerParams(vmem_limit_bytes=56 << 20),
        cost_estimate=pl.CostEstimate(
            flops=12 * 4 * length * width * hidden, bytes_accessed=20 << 20, transcendentals=0
        ),
        name="feed_forward",
    )(place, vectors, bias, *hats, *cots, *parts, *acc_list)


def attn_kernel(count, replicas, *refs):
    refs = list(refs)
    take = lambda number: [refs.pop(0) for _ in range(number)]
    place_ref, norm_ref, bias_ref, spread_ref = take(4)
    tab_refs, h_refs, c_refs = take(4), take(4), take(4)
    (own_ref,) = take(1)
    part_refs = take(count)
    acc_refs = take(2)
    out_ref, gd_ref, dw_ref, vec_ref, sum_ref = take(5)
    h_all, c_all, tab_all, tiles, w_in, w_out, in_acc, out_acc = take(8)
    q_all, k_all, v_all, g_all, o_all, dq_all, dk_all, dv_all, sems = take(9)
    me, column, quarter = place_ref[0], place_ref[1], place_ref[2]
    copies = []
    for number in range(4):
        copies.append(pltpu.make_async_copy(h_refs[number], h_all.at[number], sems.at[number]))
        copies.append(pltpu.make_async_copy(c_refs[number], c_all.at[number], sems.at[4 + number]))
    for copy in copies:
        copy.start()
    for number in range(4):
        tab_all[number] = tab_refs[number][...]
    tiles[column] = own_ref[...]
    rows_part = 16 * TILE // count
    for at in range(count):
        first = pl.multiple_of((at ^ quarter) * rows_part, rows_part)
        for bit in (1, 2, 3):
            tiles[column ^ bit, pl.ds(first, rows_part), :] = part_refs[at][
                (bit - 1) * rows_part : bit * rows_part, :
            ]
    for matrix in range(3):
        for at in range(16):
            w_in[
                (at // 2) * TILE : (at // 2 + 1) * TILE,
                (2 * matrix + at % 2) * TILE : (2 * matrix + at % 2 + 1) * TILE,
            ] = tiles[matrix, at * TILE : (at + 1) * TILE, :]
    for at in range(16):
        w_out[(at // 8) * TILE : (at // 8 + 1) * TILE, (at % 8) * TILE : (at % 8 + 1) * TILE] = (
            tiles[3, at * TILE : (at + 1) * TILE, :]
        )
    in_acc[...] = jnp.zeros_like(in_acc)
    out_acc[...] = jnp.zeros_like(out_acc)
    vec_ref[...] = jnp.zeros_like(vec_ref)
    sum_ref[...] = jnp.zeros_like(sum_ref)
    for copy in copies:
        copy.wait()
    length = h_all.shape[1]
    wide = 4 * HDIM
    block = 256
    half = ROT // 2
    lane = lax.broadcasted_iota(jnp.int32, (1, LANES), 1) % (2 * HDIM)
    keep_low = lane < HDIM
    scale = HDIM ** (-0.5)

    def body(at, carry):
        hat = h_all[at].astype(F32)
        normed = (hat * norm_ref[0:1, :] + norm_ref[1:2, :]).astype(BF16)
        cot = c_all[at]
        table = precise(tab_all[at], spread_ref[...], 0, 0)
        within = lane % HDIM
        cos_w = table[:, 0:LANES] + (within >= ROT).astype(F32)
        sin_a = table[:, LANES : 2 * LANES]
        sin_b = table[:, 2 * LANES : 3 * LANES]
        proj = dot_nn(normed, w_in[...]) + bias_ref[...]
        g_all[...] = dot_nt(cot, w_out[...]).astype(BF16)
        for pair in range(2):
            cols = slice(pair * LANES, (pair + 1) * LANES)
            query = proj[:, pair * LANES : (pair + 1) * LANES]
            key = proj[:, wide + pair * LANES : wide + (pair + 1) * LANES]

            def turn(value):
                return (
                    value * cos_w
                    - pltpu.roll(value, LANES - half, 1) * sin_a
                    + pltpu.roll(value, half, 1) * sin_b
                )

            q_all[:, cols] = (turn(query).astype(BF16) * scale).astype(BF16)
            k_all[:, cols] = turn(key).astype(BF16)
            v_all[:, cols] = proj[:, 2 * wide + pair * LANES : 2 * wide + (pair + 1) * LANES].astype(
                BF16
            )
        dk_all[...] = jnp.zeros_like(dk_all)
        dv_all[...] = jnp.zeros_like(dv_all)
        for pair in range(2):
            cols = slice(pair * LANES, (pair + 1) * LANES)
            for first in range(0, length, block):
                rows = slice(first, first + block)
                keys = slice(0, first + block)
                out_rows = None
                dq_rows = None
                for head in range(2):
                    mask = keep_low if head == 0 else jnp.logical_not(keep_low)
                    zero = jnp.zeros((), BF16)
                    query = jnp.where(mask, q_all[rows, cols], zero)
                    grad = jnp.where(mask, g_all[rows, cols], zero)
                    key = jnp.where(mask, k_all[keys, cols], zero)
                    value = jnp.where(mask, v_all[keys, cols], zero)
                    scores = dot_nt(query, key)
                    row_at = first + lax.broadcasted_iota(jnp.int32, scores.shape, 0)
                    col_at = lax.broadcasted_iota(jnp.int32, scores.shape, 1)
                    scores = jnp.where(col_at <= row_at, scores, -1e30)
                    peak = jnp.max(scores, axis=-1, keepdims=True)
                    raised = jnp.exp(scores - peak)
                    prob = raised * (1.0 / jnp.sum(raised, axis=-1, keepdims=True))
                    prob_low = prob.astype(BF16)
                    piece = dot_nn(prob_low, value)
                    out_rows = piece if out_rows is None else out_rows + piece
                    grad_prob = dot_nt(grad, value)
                    delta = jnp.sum(prob * grad_prob, axis=-1, keepdims=True)
                    grad_scores = (prob * (grad_prob - delta)).astype(BF16)
                    piece = dot_nn(grad_scores, key)
                    dq_rows = piece if dq_rows is None else dq_rows + piece
                    dk_all[keys, cols] += dot_tn(grad_scores, query)
                    dv_all[keys, cols] += dot_tn(prob_low, grad)
                o_all[rows, cols] = out_rows.astype(BF16)
                dq_all[rows, cols] = dq_rows * scale

        def turn_back(value):
            return (
                value * cos_w
                + pltpu.roll(value, LANES - half, 1) * sin_a
                - pltpu.roll(value, half, 1) * sin_b
            ).astype(BF16)

        pieces = [turn_back(dq_all[:, 0:LANES]), turn_back(dq_all[:, LANES : 2 * LANES])]
        pieces += [turn_back(dk_all[:, 0:LANES]), turn_back(dk_all[:, LANES : 2 * LANES])]
        pieces += [dv_all[...].astype(BF16)]
        grads = jnp.concatenate(pieces, axis=1)
        sum_ref[...] += jnp.sum(grads.astype(F32), axis=0, keepdims=True)
        out = dot_nn(o_all[...], w_out[...]) + acc_refs[0][at].astype(F32)
        out_ref[at] = out.astype(BF16)
        back = dot_nt(grads, w_in[...])
        vec_ref[0:1, :] += jnp.sum(back * hat, axis=0, keepdims=True)
        vec_ref[1:2, :] += jnp.sum(back, axis=0, keepdims=True)
        back = back * norm_ref[0:1, :] + acc_refs[1][at].astype(F32)
        gd_ref[at] = back.astype(BF16)
        in_acc[...] += dot_tn(normed, grads)
        out_acc[...] += dot_tn(o_all[...], cot)
        return carry

    lax.fori_loop(0, 4, body, 0)
    rows_out = dw_ref.shape[2]
    size = min(TILE, rows_out)
    for matrix in range(4):
        for at in range(16):
            for piece in range(TILE // size):
                row = at * TILE + piece * size
                if matrix < 3:
                    top, left = (at // 2) * TILE, (2 * matrix + at % 2) * TILE
                    tile = in_acc[top + piece * size : top + (piece + 1) * size, left : left + TILE]
                else:
                    top, left = (at // 8) * TILE, (at % 8) * TILE
                    tile = out_acc[
                        top + piece * size : top + (piece + 1) * size, left : left + TILE
                    ]
                inner = row % rows_out
                dw_ref[(row // rows_out) ^ quarter, column ^ matrix, inner : inner + size, :] = (
                    tile.astype(BF16)
                )


def attention(place, vectors, bias, spread, tables, hats, cots, own, parts, acc, replicas):
    length, width = hats[0].shape
    wide = 4 * HDIM
    rows_out = 16 * TILE // replicas
    return pl.pallas_call(
        functools.partial(attn_kernel, len(parts), replicas),
        out_shape=[
            jax.ShapeDtypeStruct((4, length, width), BF16),
            jax.ShapeDtypeStruct((4, length, width), BF16),
            jax.ShapeDtypeStruct((replicas, 4, rows_out, LANES), BF16),
            jax.ShapeDtypeStruct((2, width), F32),
            jax.ShapeDtypeStruct((1, 3 * wide), F32),
        ],
        in_specs=[SMEM, VMEM, VMEM, VMEM] + [VMEM] * 4 + [ANY] * 8 + [VMEM] * (1 + len(parts) + 2),
        out_specs=[VMEM] * 5,
        scratch_shapes=[
            pltpu.VMEM((4, length, width), BF16),
            pltpu.VMEM((4, length, width), BF16),
            pltpu.VMEM((4, ROT, length), F32),
            pltpu.VMEM((4, 16 * TILE, LANES), BF16),
            pltpu.VMEM((width, 3 * wide), BF16),
            pltpu.VMEM((wide, width), BF16),
            pltpu.VMEM((width, 3 * wide), F32),
            pltpu.VMEM((wide, width), F32),
            pltpu.VMEM((length, wide), BF16),
            pltpu.VMEM((length, wide), BF16),
            pltpu.VMEM((length, wide), BF16),
            pltpu.VMEM((length, wide), BF16),
            pltpu.VMEM((length, wide), BF16),
            pltpu.VMEM((length, wide), F32),
            pltpu.VMEM((length, wide), F32),
            pltpu.VMEM((length, wide), F32),
            pltpu.SemaphoreType.DMA((8,)),
        ],
        compiler_params=pltpu.CompilerParams(vmem_limit_bytes=56 << 20),
        cost_estimate=pl.CostEstimate(
            flops=30 * 10**9, bytes_accessed=20 << 20, transcendentals=0
        ),
        name="attention",
    )(place, vectors, bias, spread, *tables, *hats, *cots, own, *parts, *acc)


def soap_kernel(offsets, slots, replicas, per_step, *refs):
    refs = list(refs)
    take = lambda number: [refs.pop(0) for _ in range(number)]
    place_ref, owner_ref = take(2)
    part_refs = take(len(offsets))
    left_ref, right_ref, first_ref, second_ref, master_ref, ema_ref = take(6)
    grad_ref, first_out, second_out, master_out, copy_out, ema_out = take(6)
    slab, inverse, sems = take(3)
    me, column = place_ref[0], place_ref[1]
    step = pl.program_id(0)
    bias_fix = 1.0 - 0.5**STEP

    @pl.when(step == 0)
    def _():
        def note(unit, carry):
            inverse[owner_ref[unit]] = unit
            return carry

        lax.fori_loop(0, owner_ref.shape[0], note, 0)
        load_parts(offsets, part_refs, slab, sems)

    rows_ff = 64 * TILE // replicas
    rows_attn = 16 * TILE // replicas
    rows_all = slots * TILE
    size = min(TILE, rows_attn)
    for number in range(per_step):
        unit = inverse[me * slots + step * per_step + number]
        row, col = (unit % 64) // 8, unit % 8
        by_rows = column == 3
        rank = jnp.where(by_rows, row // 2, col // 2)
        attn_place = jnp.where(by_rows, (row % 2) * 8 + col, row * 2 + col % 2)
        up_place = row * 4 + col % 4
        down_place = 32 + (row % 4) * 8 + col
        is_attn, is_up = unit < 64, unit < 128
        core = jnp.where(is_attn, rank % 2, jnp.where(is_up, col // 4, row // 4))
        other = ((rank // 2) != (column % 2)).astype(jnp.int32)
        pieces = []
        for piece in range(TILE // size):
            attn_row = attn_place * TILE + piece * size
            ff_row = jnp.where(is_up, up_place, down_place) * TILE + piece * size
            holder = jnp.where(is_attn, attn_row // rows_attn, ff_row // rows_ff)
            inner = jnp.where(
                is_attn, rows_ff + other * rows_attn + attn_row % rows_attn, ff_row % rows_ff
            )
            start = ((holder * 2 + core) ^ me) * rows_all + inner
            pieces.append(slab[pl.ds(pl.multiple_of(start, size), size), :].astype(F32))
        grad = pieces[0] if len(pieces) == 1 else jnp.concatenate(pieces, axis=0)
        left, right = left_ref[number], right_ref[number]
        grad_ref[number] = grad
        turned = precise(precise(left, grad, 0, 0), right, 1, 0)
        first = 0.5 * first_ref[number] + 0.5 * turned
        second = 0.5 * second_ref[number] + 0.5 * turned * turned
        first_out[number] = first
        second_out[number] = second
        scaled = first / bias_fix / (jnp.sqrt(second / bias_fix) + eps_adam)
        back = precise(precise(left, scaled, 1, 0), right, 1, 1)
        master = master_ref[number] - lr_matrix * back
        master_out[number] = master
        copy_out[number] = master.astype(BF16)
        ema_out[number] = ema_keep * ema_ref[number] + (1.0 - ema_keep) * master


def soap(place, owner_row, parts, state, replicas):
    slots = state[0].shape[0]
    per_step = 4 if slots % 4 == 0 else 1
    offsets = [offset for offset, _ in parts]
    total = sum(part.shape[0] for _, part in parts)
    spec = pl.BlockSpec((per_step, TILE, TILE), lambda i: (i, 0, 0))
    shape = (slots, TILE, TILE)
    return pl.pallas_call(
        functools.partial(soap_kernel, offsets, slots, replicas, per_step),
        grid=(slots // per_step,),
        out_shape=[jax.ShapeDtypeStruct(shape, F32)] * 4
        + [jax.ShapeDtypeStruct(shape, BF16), jax.ShapeDtypeStruct(shape, F32)],
        in_specs=[SMEM, SMEM] + [ANY] * len(parts) + [spec] * 6,
        out_specs=[spec] * 6,
        scratch_shapes=[
            pltpu.VMEM((total, LANES), BF16),
            pltpu.SMEM((owner_row.shape[0],), jnp.int32),
            pltpu.SemaphoreType.DMA((len(parts),)),
        ],
        compiler_params=pltpu.CompilerParams(vmem_limit_bytes=32 << 20),
        cost_estimate=pl.CostEstimate(
            flops=24 * slots * 2 * TILE**3, bytes_accessed=26 << 20, transcendentals=0
        ),
        name="soap",
    )(place, owner_row, *[part for _, part in parts], *state)


def adam_step(grad, first, second, param):
    bias_fix = 1.0 - 0.5**STEP
    first_new = 0.5 * first + 0.5 * grad
    second_new = 0.5 * second + 0.5 * grad * grad
    return (
        first_new,
        second_new,
        param - lr_vector * (first_new / bias_fix) / (jnp.sqrt(second_new / bias_fix) + eps_adam),
    )


def spread_table():
    lane = jnp.arange(LANES, dtype=jnp.int32) % HDIM
    row = jnp.arange(ROT, dtype=jnp.int32)[:, None]
    half = ROT // 2
    cos_part = (lane < ROT) & (row == lane % half)
    sin_first = (lane < half) & (row == half + lane)
    sin_second = (lane >= half) & (lane < ROT) & (row == lane)
    return jnp.concatenate([cos_part, sin_first, sin_second], axis=1).astype(F32)


def local(
    tokens,
    cotangent,
    positions,
    owners,
    masters,
    basis_left,
    basis_right,
    moment1,
    moment2,
    ema,
    vectors,
    vector_moment1,
    vector_moment2,
    hidden_bias,
    hidden_moment1,
    hidden_moment2,
):
    length, width = tokens.shape
    slots = masters.shape[1]
    me = lax.axis_index("dp")
    column = lax.axis_index("mlp")
    replicas = lax.axis_size("dp") // 2
    core, low = me % 2, column % 2
    rank = 2 * low + core
    place = jnp.stack([me, column, me // 2]).astype(jnp.int32)
    owner_row = owners[0]

    parts = gather_dp(masters[0].astype(BF16).reshape(slots * TILE, LANES))

    centered = tokens - jnp.mean(tokens, axis=-1, keepdims=True)
    spread_inv = lax.rsqrt(jnp.mean(centered * centered, axis=-1, keepdims=True) + eps_norm)
    hats = gather_group((centered * spread_inv).astype(BF16))
    grad_low = cotangent.astype(BF16)
    cots = gather_group(grad_low)
    inverse_freq = 10000.0 ** (-(jnp.arange(ROT // 2, dtype=F32) * 2.0) / ROT)
    angles = inverse_freq[:, None] * positions.astype(F32)[None, :]
    tables = gather_group(jnp.concatenate([jnp.cos(angles), jnp.sin(angles)], axis=0))

    own_attn, send1, send2, send3, own_ff, send_ff = pick(place, owner_row, parts, slots, replicas)
    others = jnp.concatenate([swap_z(send1, 1), swap_z(send2, 2), swap_z(send3, 3)], axis=0)
    attn_parts = gather_q(others)
    ff_parts = gather_q(swap_z(send_ff, 2))

    hidden = FF // (2 * GROUP)
    start_own = column * (2 * hidden) + core * hidden
    start_other = (column ^ 2) * (2 * hidden) + core * hidden
    bias_own = lax.dynamic_slice_in_dim(hidden_bias, start_own, hidden, 0)[None]
    bias_other = lax.dynamic_slice_in_dim(hidden_bias, start_other, hidden, 0)[None]
    wide = width // GROUP
    bias_qkv = lax.dynamic_slice(vectors, (4, rank * wide), (3, wide)).reshape(1, 3 * wide)

    out, back, dw_own, vec_own, hid_own = feed_forward(
        place, vectors, bias_own, hats, cots, [own_ff], None, replicas
    )
    sum_own = reduce_q(dw_own)
    out, back, dw_attn, vec_attn, sums = attention(
        place,
        vectors,
        bias_qkv,
        spread_table(),
        tables,
        hats,
        cots,
        own_attn,
        attn_parts,
        (out, back),
        replicas,
    )
    sum_attn = reduce_q(dw_attn)
    attn_low = sum_attn.astype(BF16)
    attn_same = sum_attn[0] + swap_z(attn_low[2], 2).astype(F32)
    attn_other = swap_z(attn_low[1], 1).astype(F32) + swap_z(attn_low[3], 3).astype(F32)
    out, back, dw_other, vec_other, hid_other = feed_forward(
        place, vectors, bias_other, hats, cots, ff_parts, (out, back), replicas
    )
    sum_other = reduce_q(dw_other)
    sum_ff = sum_own + swap_z(sum_other.astype(BF16), 2).astype(F32)
    block = jnp.concatenate([sum_ff, attn_same, attn_other], axis=0).astype(BF16)
    grad_parts = gather_dp(block)
    state = [item[0] for item in (basis_left, basis_right, moment1, moment2, masters, ema)]
    own_grad, first_new, second_new, master_new, weight_copy, ema_new = soap(
        place, owner_row, grad_parts, state, replicas
    )

    def scatter(value):
        mine = value[0].astype(F32) + swap_dp(value[1], 1).astype(F32)
        along = value[2].astype(F32) + swap_dp(value[3], 1).astype(F32)
        return mine + swap_z(along.astype(BF16), 1).astype(F32)

    result = tokens + (scatter(out) + (vectors[7] + vectors[8]))
    grad_hat = scatter(back)
    hat = centered * spread_inv
    grad_tokens = cotangent + spread_inv * (
        grad_hat
        - jnp.mean(grad_hat, axis=-1, keepdims=True)
        - hat * jnp.mean(grad_hat * hat, axis=-1, keepdims=True)
    )

    grad_bias_out = jnp.sum(grad_low.astype(F32), axis=0)
    sums = jnp.zeros((3, width), F32) + lax.dynamic_update_slice(
        jnp.zeros((3, width), F32), sums.reshape(3, wide), (0, rank * wide)
    )
    vector_part = jnp.concatenate(
        [vec_attn, vec_own + vec_other, sums, grad_bias_out[None]], axis=0
    )
    hidden_part = lax.dynamic_update_slice_in_dim(
        jnp.zeros((FF,), F32), hid_own[0], start_own, 0
    )
    hidden_part = lax.dynamic_update_slice_in_dim(hidden_part, hid_other[0], start_other, 0)
    reduced = all_sum(jnp.concatenate([vector_part, hidden_part.reshape(-1, width)], axis=0))
    vector_grad = jnp.concatenate([reduced[:8], reduced[7:8]], axis=0)
    hidden_grad = reduced[8:].reshape(FF)
    vec_first, vec_second, vectors_new = adam_step(
        vector_grad, vector_moment1, vector_moment2, vectors
    )
    hid_first, hid_second, hidden_new = adam_step(
        hidden_grad, hidden_moment1, hidden_moment2, hidden_bias
    )
    return (
        result,
        grad_tokens,
        own_grad[None],
        first_new[None],
        second_new[None],
        master_new[None],
        weight_copy[None],
        ema_new[None],
        vector_grad,
        vec_first,
        vec_second,
        vectors_new,
        hidden_grad,
        hid_first,
        hid_second,
        hidden_new,
    )


def solution(mesh):
    split = P(("dp", "mlp"), None)
    tiled = P("mlp", "dp", None, None)
    return jax.shard_map(
        local,
        mesh=mesh,
        in_specs=(split, split, P(("dp", "mlp")), P("mlp", None)) + (tiled,) * 6 + (P(),) * 6,
        out_specs=(split, split) + (tiled,) * 6 + (P(),) * 8,
        check_vma=False,
    )
```

```python
import functools

import jax
import jax.numpy as jnp
from jax import lax
from jax.experimental import pallas as pl
from jax.experimental.pallas import tpu as pltpu
from jax.sharding import PartitionSpec as P

HEADS = 16
HDIM = 64
ROT = 16
FF = 4096
STEP = 5
TILE = 128
LANES = 128
GROUP = 4

PRECISE = lax.Precision.HIGHEST
eps_norm = 1e-05
eps_adam = 1e-08
lr_matrix = 0.05
lr_vector = 0.5
ema_keep = 0.8

F32 = jnp.float32
BF16 = jnp.bfloat16
ANY = pl.BlockSpec(memory_space=pl.ANY)
VMEM = pl.BlockSpec(memory_space=pltpu.VMEM)
SMEM = pl.BlockSpec(memory_space=pltpu.SMEM)


def dot_nn(left, right):
    return jnp.dot(left, right, preferred_element_type=F32)


def dot_nt(left, right):
    return lax.dot_general(left, right, (((1,), (1,)), ((), ())), preferred_element_type=F32)


def dot_tn(left, right):
    return lax.dot_general(left, right, (((0,), (0,)), ((), ())), preferred_element_type=F32)


def precise(left, right, left_dim, right_dim):
    return lax.dot_general(
        left,
        right,
        (((left_dim,), (right_dim,)), ((), ())),
        precision=PRECISE,
        preferred_element_type=F32,
    )


MESH = pl.DeviceIdType.MESH


def flip(index, mask):
    bit = 1
    while bit <= mask:
        if mask & bit:
            index = index + bit - 2 * bit * ((index // bit) % 2)
        bit *= 2
    return index


def differ(left, right, count):
    total, bit = 0, 1
    while bit < count:
        one, two = (left // bit) % 2, (right // bit) % 2
        total = total + bit * (one + two - 2 * one * two)
        bit *= 2
    return total


class Links:
    def __init__(self, send_sems, recv_sems):
        self.send_sems, self.recv_sems = send_sems, recv_sems
        self.number = 0
        self.all = []

    def send(self, source, target, device):
        copy = pltpu.make_async_remote_copy(
            src_ref=source,
            dst_ref=target,
            send_sem=self.send_sems.at[self.number],
            recv_sem=self.recv_sems.at[self.number],
            device_id=device,
            device_id_type=MESH,
        )
        self.number += 1
        copy.start()
        entry = [copy, False]
        self.all.append(entry)
        return entry

    def arrived(self, entry):
        if not entry[1]:
            entry[0].wait_recv()
            entry[1] = True

    def finish(self):
        for entry in self.all:
            self.arrived(entry)
            entry[0].wait_send()


def greet(me, column, masks_dp, masks_z):
    barrier = pltpu.get_barrier_semaphore()
    for mask in masks_dp:
        pl.semaphore_signal(barrier, inc=1, device_id={"dp": flip(me, mask)}, device_id_type=MESH)
    for mask in masks_z:
        pl.semaphore_signal(
            barrier, inc=1, device_id={"mlp": flip(column, mask)}, device_id_type=MESH
        )
    pl.semaphore_wait(barrier, len(masks_dp) + len(masks_z))


def start_side(moves, send_sems, recv_sems):
    me, column = lax.axis_index("dp"), lax.axis_index("mlp")
    masks_dp = sorted({mask for _, _, axis, mask in moves if axis == "dp"})
    masks_z = sorted({mask for _, _, axis, mask in moves if axis == "mlp"})
    greet(me, column, masks_dp, masks_z)
    links = Links(send_sems, recv_sems)
    for source, target, axis, mask in moves:
        links.send(source, target, {axis: flip(me if axis == "dp" else column, mask)})
    return links


def side_shapes(moves):
    return [pltpu.SemaphoreType.DMA((moves,)), pltpu.SemaphoreType.DMA((moves,))]


class Spread:
    def __init__(self, links, slab, me, count, rows, first, size, backward):
        self.links, self.slab, self.me = links, slab, me
        self.rows, self.first, self.size = rows, first, size
        self.bits = [1 << i for i in range(1, count.bit_length() - 1)]
        if backward:
            self.bits = self.bits[::-1]
        self.came = {}
        self.order = []

    def part(self, at):
        return self.slab.at[pl.ds(at * self.rows + self.first, self.size)]

    def forward(self, at, step, source=None):
        source = self.part(at) if source is None else source
        for later in range(step, len(self.bits)):
            bit = self.bits[later]
            entry = self.links.send(source, self.part(at ^ bit), {"dp": flip(self.me, bit)})
            self.came[at ^ bit] = (entry, later + 1)
            self.order.append(at ^ bit)
        self.links.send(source, self.part(at ^ 1), {"dp": flip(self.me, 1)})

    def relay(self):
        while self.order:
            at = min(self.order, key=lambda index: (self.came[index][1], index.bit_count()))
            self.order.remove(at)
            entry, step = self.came[at]
            self.links.arrived(entry)
            self.forward(at, step)


def attn_unit(column, rank, place):
    by_columns = (place // 2) * 8 + 2 * rank + place % 2
    by_rows = (2 * rank + place // 8) * 8 + place % 8
    return jnp.where(column == 3, by_rows, by_columns)


def ff_unit(core, place):
    later = place - 32
    up = 64 + (place // 4) * 8 + core * 4 + place % 4
    down = 128 + (core * 4 + later // 8) * 8 + later % 8
    return jnp.where(place < 32, up, down)


def front_kernel(slots, devices, tokens, cot, table, masters, tile_ref, *refs):
    (hats, cots, tables, attn_parts, own_attn, own_ff, send_ff) = refs[:7]
    (slab, own_hat, own_cot, send_attn, send_sems, recv_sems, local_sems) = refs[7:]
    me, column = lax.axis_index("dp"), lax.axis_index("mlp")
    replicas = devices // 2
    core, quarter, low = me % 2, me // 2, column % 2
    links = Links(send_sems, recv_sems)
    half = slots // 2
    greet(me, column, [1] + [at << 1 for at in range(1, replicas)], [1, 2, 3])
    slab[0:slots] = masters[...].astype(BF16)
    spreads = [
        Spread(links, slab, me, devices, slots, 0, half, False),
        Spread(links, slab, me, devices, slots, half, slots - half, True),
    ]
    for spread in spreads:
        spread.forward(0, 0)

    length = tokens.shape[0]
    step_rows = 128

    def normalize(step, carry):
        where = pl.ds(pl.multiple_of(step * step_rows, step_rows), step_rows)
        value = tokens[where, :]
        value = value - jnp.mean(value, axis=-1, keepdims=True)
        value = value * lax.rsqrt(jnp.mean(value * value, axis=-1, keepdims=True) + eps_norm)
        own_hat[where, :] = value.astype(BF16)
        own_cot[where, :] = cot[where, :].astype(BF16)
        return carry

    lax.fori_loop(0, length // step_rows, normalize, 0)
    own = []
    along = []
    for number, (source, target) in enumerate(
        ((own_hat, hats), (table, tables), (own_cot, cots))
    ):
        along.append((target, links.send(source, target.at[2], {"mlp": flip(column, 1)})))
        links.send(source, target.at[1], {"dp": flip(me, 1)})
        copy = pltpu.make_async_copy(source, target.at[0], local_sems.at[number])
        copy.start()
        own.append(copy)
    for spread in spreads:
        spread.relay()
    for entry in links.all:
        if not any(entry is item for _, item in along):
            links.arrived(entry)

    def fill(out_ref, base, rows_out, first_row, unit_of):
        size = min(TILE, rows_out)

        def body(step, carry):
            row = first_row + step * size
            tile = tile_ref[unit_of(row // TILE)]
            where = pl.ds(pl.multiple_of(base + step * size, size), size)
            if size == TILE:
                out_ref[where, :] = slab[tile]
            else:
                out_ref[where, :] = slab[tile, pl.ds(pl.multiple_of(row % TILE, size), size), :]
            return carry

        lax.fori_loop(0, rows_out // size, body, 0)

    rows_attn = 16 * TILE // replicas
    across = []
    for bit in (3, 2, 1):
        rank = 2 * (flip(low, 1) if bit & 1 else low) + core
        base = (bit - 1) * rows_attn
        fill(
            send_attn,
            base,
            rows_attn,
            quarter * rows_attn,
            functools.partial(attn_unit, column, rank),
        )
        piece = pl.ds(base, rows_attn)
        across.append(
            (
                piece,
                links.send(
                    send_attn.at[piece, :],
                    attn_parts.at[0, piece, :],
                    {"mlp": flip(column, bit)},
                ),
            )
        )
    rows_ff = 64 * TILE // replicas
    fill(own_attn, 0, 16 * TILE, 0, functools.partial(attn_unit, column, 2 * low + core))
    for piece, entry in across[::-1]:
        links.arrived(entry)
        for at in range(1, replicas):
            links.send(
                attn_parts.at[0, piece, :],
                attn_parts.at[at, piece, :],
                {"dp": flip(me, at << 1)},
            )
    fill(send_ff, 0, rows_ff, quarter * rows_ff, functools.partial(ff_unit, core))
    fill(own_ff, 0, 64 * TILE, 0, functools.partial(ff_unit, core))
    for target, entry in along:
        links.arrived(entry)
        links.send(target.at[2], target.at[3], {"dp": flip(me, 1)})
    for copy in own:
        copy.wait()
    links.finish()


def front(tokens, cot, table, masters, tile_row):
    length, width = tokens.shape
    slots = masters.shape[0]
    devices = lax.axis_size("dp")
    replicas = devices // 2
    rows_attn = 16 * TILE // replicas
    count = 2 * (replicas - 1) + 2 * replicas + 9 + 3 * replicas + 3
    block = jax.ShapeDtypeStruct((4, length, width), BF16)
    flat = lambda number: jax.ShapeDtypeStruct((number, LANES), BF16)
    return pl.pallas_call(
        functools.partial(front_kernel, slots, devices),
        out_shape=[
            block,
            block,
            jax.ShapeDtypeStruct((4,) + table.shape, F32),
            jax.ShapeDtypeStruct((replicas, 3 * rows_attn, LANES), BF16),
            flat(16 * TILE),
            flat(64 * TILE),
            flat(64 * TILE // replicas),
        ],
        in_specs=[VMEM] * 4 + [SMEM],
        out_specs=[ANY] * 4 + [VMEM] * 3,
        scratch_shapes=[
            pltpu.VMEM((devices * slots, TILE, LANES), BF16),
            pltpu.VMEM((length, width), BF16),
            pltpu.VMEM((length, width), BF16),
            pltpu.VMEM((3 * rows_attn, LANES), BF16),
            pltpu.SemaphoreType.DMA((count,)),
            pltpu.SemaphoreType.DMA((count,)),
            pltpu.SemaphoreType.DMA((3,)),
        ],
        compiler_params=pltpu.CompilerParams(
            vmem_limit_bytes=32 << 20, collective_id=0, has_side_effects=True
        ),
        cost_estimate=pl.CostEstimate(flops=0, bytes_accessed=200 << 20, transcendentals=0),
        name="front",
    )(tokens, cot, table, masters, tile_row)


def back_kernel(slots, devices, *refs):
    refs = list(refs)
    take = lambda number: [refs.pop(0) for _ in range(number)]
    dw, dw_own, own_land, dw_attn, attn_side, out, back, tokens, cot, bias, vec = take(11)
    slab, result, grad_tokens, reduced = take(4)
    dw_land, z_send, z_land, attn_send, attn_land, block, attn_sum = take(7)
    core_land, along_send, along_land, vec_land, vec_send = take(5)
    send_sems, recv_sems, local_sems = take(3)
    me, column = lax.axis_index("dp"), lax.axis_index("mlp")
    replicas = devices // 2
    links = Links(send_sems, recv_sems)
    rows = slots * TILE
    rows_ff, rows_attn = 64 * TILE // replicas, 16 * TILE // replicas
    chunks = 4
    size = rows_ff // chunks
    greet(
        me,
        column,
        [1] + [at << 1 for at in range(1, replicas)],
        [1, 2, 3],
    )
    for bit in range(4):
        total = dw_attn[0, bit].astype(F32)
        for at in range(1, replicas):
            total = total + attn_side[at - 1, bit].astype(F32)
        if bit == 0:
            attn_sum[...] = total
        else:
            attn_send[bit - 1] = total.astype(BF16)
    attn_came = [
        links.send(attn_send.at[bit - 1], attn_land.at[bit - 1], {"mlp": flip(column, bit)})
        for bit in (1, 2, 3)
    ]
    dw_came = []
    for chunk in range(chunks):
        piece = pl.ds(chunk * size, size)
        dw_came.append(
            [
                links.send(dw.at[at, piece, :], dw_land.at[at - 1, piece, :], {"dp": flip(me, at << 1)})
                for at in range(1, replicas)
            ]
        )
    core_came = []
    for number, source in ((1, back), (0, out)):
        for at in (3, 1):
            core_came.append(
                links.send(source.at[at], core_land.at[number, at // 2], {"dp": flip(me, 1)})
            )
    masks = [1 << i for i in range(devices.bit_length() - 1)]
    hops = [("dp", mask) for mask in masks] + [("mlp", 1), ("mlp", 2)]
    vec_send[0] = vec[...]
    state = {"hop": 0, "entry": None}

    def vec_step():
        hop = state["hop"]
        if hop > len(hops):
            return
        if state["entry"] is not None:
            links.arrived(state["entry"])
            value = vec_send[hop - 1] + vec_land[hop - 1]
            if hop == len(hops):
                reduced[...] = value
            else:
                vec_send[hop] = value
        if hop < len(hops):
            axis, mask = hops[hop]
            own = me if axis == "dp" else column
            state["entry"] = links.send(
                vec_send.at[hop], vec_land.at[hop], {axis: flip(own, mask)}
            )
        state["hop"] = hop + 1

    vec_step()
    step_rows = 128
    length = tokens.shape[0]

    def by_rows(function):
        def body(step, carry):
            function(pl.ds(pl.multiple_of(step * step_rows, step_rows), step_rows))
            return carry

        lax.fori_loop(0, length // step_rows, body, 0)

    along_came = {}
    for place, (number, source) in enumerate(((1, back), (0, out))):
        links.arrived(core_came[2 * place])

        def add(where, number=number, source=source):
            along_send[number, where, :] = (
                source[2, where, :].astype(F32) + core_land[number, 1, where, :].astype(F32)
            ).astype(BF16)

        by_rows(add)
        along_came[number] = links.send(
            along_send.at[number], along_land.at[number], {"mlp": flip(column, 1)}
        )
    vec_step()
    local_copies = []
    spreads = []

    def publish(first, count):
        backward = len(spreads) % 2 == 1
        spread = Spread(links, slab, me, devices, rows, first, count, backward)
        source = block.at[pl.ds(first, count), :]
        spread.forward(0, 0, source)
        copy = pltpu.make_async_copy(source, spread.part(0), local_sems.at[len(spreads)])
        copy.start()
        local_copies.append(copy)
        spreads.append(spread)

    def add_chunk(chunk):
        piece = slice(chunk * size, (chunk + 1) * size)
        for entry in dw_came[chunk]:
            links.arrived(entry)
        total = dw[0, piece, :].astype(F32)
        for at in range(1, replicas):
            total = total + dw_land[at - 1, piece, :].astype(F32)
        z_send[piece, :] = total.astype(BF16)
        where = pl.ds(chunk * size, size)
        return links.send(z_send.at[where, :], z_land.at[where, :], {"mlp": flip(column, 2)})

    z_came = [add_chunk(0)]
    for entry in attn_came:
        links.arrived(entry)
    block[rows_ff : rows_ff + rows_attn, :] = (
        attn_sum[...] + attn_land[1].astype(F32)
    ).astype(BF16)
    publish(rows_ff, rows_attn)
    block[rows_ff + rows_attn : rows, :] = (
        attn_land[0].astype(F32) + attn_land[2].astype(F32)
    ).astype(BF16)
    publish(rows_ff + rows_attn, rows_attn)
    vec_step()
    for chunk in range(1, chunks):
        z_came.append(add_chunk(chunk))
    vec_step()
    for spread in spreads[:2]:
        spread.relay()
    for chunk in range(chunks):
        links.arrived(z_came[chunk])
        piece = slice(chunk * size, (chunk + 1) * size)
        total = z_land[piece, :].astype(F32) + dw_own[0, piece, :].astype(F32)
        for at in range(1, replicas):
            total = total + own_land[at - 1, piece, :].astype(F32)
        block[piece, :] = total.astype(BF16)
        publish(chunk * size, size)
        vec_step()
        if chunk > 0:
            spreads[1 + chunk].relay()
    spreads[1 + chunks].relay()

    links.arrived(core_came[1])
    links.arrived(along_came[1])

    def finish_back(where):
        value = tokens[where, :]
        value = value - jnp.mean(value, axis=-1, keepdims=True)
        inverse = lax.rsqrt(jnp.mean(value * value, axis=-1, keepdims=True) + eps_norm)
        hat = value * inverse
        grad = back[0, where, :].astype(F32) + core_land[1, 0, where, :].astype(F32)
        grad = grad + along_land[1, where, :].astype(F32)
        grad_tokens[where, :] = cot[where, :] + inverse * (
            grad
            - jnp.mean(grad, axis=-1, keepdims=True)
            - hat * jnp.mean(grad * hat, axis=-1, keepdims=True)
        )

    by_rows(finish_back)
    links.arrived(core_came[3])
    links.arrived(along_came[0])

    def finish_out(where):
        value = out[0, where, :].astype(F32) + core_land[0, 0, where, :].astype(F32)
        value = value + along_land[0, where, :].astype(F32)
        result[where, :] = tokens[where, :] + (value + (bias[7:8, :] + bias[8:9, :]))

    by_rows(finish_out)
    while state["hop"] <= len(hops):
        vec_step()
    for copy in local_copies:
        copy.wait()
    links.finish()


def send_back(dw, own, attn, out, back, tokens, cot, vectors, vec, slots):
    length, width = tokens.shape
    devices = lax.axis_size("dp")
    replicas = devices // 2
    rows_ff, rows_attn = 64 * TILE // replicas, 16 * TILE // replicas
    rows = slots * TILE
    pieces = 6
    hops = devices.bit_length() + 1
    count = 3 + 4 * (replicas - 1) + 4 + 2 + hops + 4 + pieces * (2 * replicas - 1)
    return pl.pallas_call(
        functools.partial(back_kernel, slots, devices),
        out_shape=[
            jax.ShapeDtypeStruct((devices * rows, LANES), BF16),
            jax.ShapeDtypeStruct((length, width), F32),
            jax.ShapeDtypeStruct((length, width), F32),
            jax.ShapeDtypeStruct(vec.shape, F32),
        ],
        in_specs=[VMEM] * 11,
        out_specs=[ANY] + [VMEM] * 3,
        scratch_shapes=[
            pltpu.VMEM((replicas - 1, rows_ff, LANES), BF16),
            pltpu.VMEM((rows_ff, LANES), BF16),
            pltpu.VMEM((rows_ff, LANES), BF16),
            pltpu.VMEM((3, rows_attn, LANES), BF16),
            pltpu.VMEM((3, rows_attn, LANES), BF16),
            pltpu.VMEM((rows, LANES), BF16),
            pltpu.VMEM((rows_attn, LANES), F32),
            pltpu.VMEM((2, 2, length, width), BF16),
            pltpu.VMEM((2, length, width), BF16),
            pltpu.VMEM((2, length, width), BF16),
            pltpu.VMEM((hops,) + vec.shape, F32),
            pltpu.VMEM((hops,) + vec.shape, F32),
            pltpu.SemaphoreType.DMA((count,)),
            pltpu.SemaphoreType.DMA((count,)),
            pltpu.SemaphoreType.DMA((pieces,)),
        ],
        compiler_params=pltpu.CompilerParams(
            vmem_limit_bytes=60 << 20, collective_id=1, has_side_effects=True
        ),
        cost_estimate=pl.CostEstimate(flops=0, bytes_accessed=200 << 20, transcendentals=0),
        name="send_back",
    )(dw, *own, *attn, out, back, tokens, cot, vectors, vec)


def erf_f32(value):
    value = jnp.clip(value, -3.832506856900711, 3.832506856900711)
    square = value * value
    top = jnp.full_like(square, 0.00022905065861350646)
    for coeff in (
        0.0034082910107109506,
        0.050955695062380861,
        0.18520832239976145,
        1.128379143519084,
    ):
        top = top * square + coeff
    low = jnp.full_like(square, -1.1791602954361697e-7)
    for coeff in (
        0.000023547966471313185,
        0.0010179625278914885,
        0.014070470171167667,
        0.11098505178285362,
        0.49746925110067538,
        1.0,
    ):
        low = low * square + coeff
    return value * top / low


def ff_kernel(count, has_acc, replicas, *refs):
    refs = list(refs)
    take = lambda number: [refs.pop(0) for _ in range(number)]
    norm_ref, bias_ref, side_ref = take(3)
    h_ref, c_ref = take(2)
    part_refs = take(count)
    acc_refs = take(2) if has_acc else None
    out_ref, gd_ref, dw_ref, vec_ref, hid_ref, land_ref = take(6)
    h_all, c_all, tiles, up, down, up_acc, down_acc, sems, send_sems, recv_sems = take(10)
    quarter = lax.axis_index("dp") // 2
    if has_acc:
        moves = [
            (side_ref.at[at], land_ref.at[at - 1], "dp", at << 1) for at in range(1, replicas)
        ]
    else:
        moves = [(side_ref, land_ref, "mlp", 2)]
    links = start_side(moves, send_sems, recv_sems)
    copies = []
    for number in range(4):
        copies.append(pltpu.make_async_copy(h_ref.at[number], h_all.at[number], sems.at[number]))
        copies.append(
            pltpu.make_async_copy(c_ref.at[number], c_all.at[number], sems.at[4 + number])
        )
    for copy in copies:
        copy.start()
    rows_part = part_refs[0].shape[0]
    for at in range(replicas if count > 1 else 1):
        where = differ(at, quarter, replicas) if count > 1 else 0
        tiles[pl.ds(pl.multiple_of(where * rows_part, TILE), rows_part), :] = (
            part_refs[0][...] if at == 0 else part_refs[1][at - 1]
        )
    for at in range(32):
        up[(at // 4) * TILE : (at // 4 + 1) * TILE, (at % 4) * TILE : (at % 4 + 1) * TILE] = tiles[
            at * TILE : (at + 1) * TILE, :
        ]
        down[(at // 8) * TILE : (at // 8 + 1) * TILE, (at % 8) * TILE : (at % 8 + 1) * TILE] = (
            tiles[(32 + at) * TILE : (33 + at) * TILE, :]
        )
    up_acc[...] = jnp.zeros_like(up_acc)
    down_acc[...] = jnp.zeros_like(down_acc)
    vec_ref[...] = jnp.zeros_like(vec_ref)
    hid_ref[...] = jnp.zeros_like(hid_ref)
    for copy in copies:
        copy.wait()

    def body(at, carry):
        hat = h_all[at].astype(F32)
        normed = (hat * norm_ref[2:3, :] + norm_ref[3:4, :]).astype(BF16)
        cot = c_all[at]
        pre = dot_nn(normed, up[...]) + bias_ref[...]
        cdf = 0.5 + 0.5 * erf_f32(pre * 0.7071067811865476)
        hidden = (pre * cdf).astype(BF16)
        grad = dot_nt(cot, down[...])
        grad = grad * (cdf + pre * (jnp.exp(-0.5 * pre * pre) * 0.3989422804014327))
        grad = grad.astype(BF16)
        hid_ref[...] += jnp.sum(grad.astype(F32), axis=0, keepdims=True)
        out = dot_nn(hidden, down[...])
        back = dot_nt(grad, up[...])
        vec_ref[0:1, :] += jnp.sum(back * hat, axis=0, keepdims=True)
        vec_ref[1:2, :] += jnp.sum(back, axis=0, keepdims=True)
        back = back * norm_ref[2:3, :]
        if acc_refs is not None:
            out = out + acc_refs[0][at].astype(F32)
            back = back + acc_refs[1][at].astype(F32)
        out_ref[at] = out.astype(BF16)
        gd_ref[at] = back.astype(BF16)
        up_acc[...] += dot_tn(normed, grad)
        down_acc[...] += dot_tn(hidden, cot)
        return carry

    lax.fori_loop(0, 4, body, 0)
    rows_out = dw_ref.shape[1]
    per = rows_out // TILE
    for at in range(64):
        if at < 32:
            tile = up_acc[
                (at // 4) * TILE : (at // 4 + 1) * TILE, (at % 4) * TILE : (at % 4 + 1) * TILE
            ]
        else:
            low = at - 32
            tile = down_acc[
                (low // 8) * TILE : (low // 8 + 1) * TILE, (low % 8) * TILE : (low % 8 + 1) * TILE
            ]
        dw_ref[
            differ(at // per, quarter, replicas), (at % per) * TILE : (at % per + 1) * TILE, :
        ] = tile.astype(BF16)
    links.finish()


def feed_forward(vectors, bias, side, hats, cots, parts, acc, replicas):
    length, width = hats.shape[1:]
    hidden = 4 * TILE
    rows_out = 64 * TILE // replicas
    acc_list = list(acc) if acc is not None else []
    land = side.shape if acc is None else (replicas - 1,) + side.shape[1:]
    moves = 1 if acc is None else replicas - 1
    return pl.pallas_call(
        functools.partial(ff_kernel, len(parts), acc is not None, replicas),
        out_shape=[
            jax.ShapeDtypeStruct((4, length, width), BF16),
            jax.ShapeDtypeStruct((4, length, width), BF16),
            jax.ShapeDtypeStruct((replicas, rows_out, LANES), BF16),
            jax.ShapeDtypeStruct((2, width), F32),
            jax.ShapeDtypeStruct((1, hidden), F32),
            jax.ShapeDtypeStruct(land, BF16),
        ],
        in_specs=[VMEM, VMEM] + [ANY] * 3 + [VMEM] * (len(parts) + len(acc_list)),
        out_specs=[VMEM] * 5 + [ANY],
        scratch_shapes=[
            pltpu.VMEM((4, length, width), BF16),
            pltpu.VMEM((4, length, width), BF16),
            pltpu.VMEM((64 * TILE, LANES), BF16),
            pltpu.VMEM((width, hidden), BF16),
            pltpu.VMEM((hidden, width), BF16),
            pltpu.VMEM((width, hidden), F32),
            pltpu.VMEM((hidden, width), F32),
            pltpu.SemaphoreType.DMA((8,)),
        ]
        + side_shapes(moves),
        compiler_params=pltpu.CompilerParams(
            vmem_limit_bytes=60 << 20,
            collective_id=2 if acc is None else 3,
            has_side_effects=True,
        ),
        cost_estimate=pl.CostEstimate(
            flops=12 * 4 * length * width * hidden, bytes_accessed=20 << 20, transcendentals=0
        ),
        name="feed_forward",
    )(vectors, bias, side, hats, cots, *parts, *acc_list)


def attn_kernel(count, replicas, *refs):
    refs = list(refs)
    take = lambda number: [refs.pop(0) for _ in range(number)]
    norm_ref, bias_ref, spread_ref, side_ff, side_dw = take(5)
    tab_ref, h_ref, c_ref, own_ref, part_ref = take(5)
    acc_refs = take(2)
    out_ref, gd_ref, dw_ref, vec_ref, sum_ref, land_ff, land_dw = take(7)
    h_all, c_all, tiles, w_in, w_out, in_acc, out_acc = take(7)
    q_all, k_all, v_all, g_all, o_all, dq_all, dk_all, dv_all, sems = take(9)
    send_sems, recv_sems = take(2)
    me, column = lax.axis_index("dp"), lax.axis_index("mlp")
    quarter = me // 2
    moves = []
    for at in range(1, replicas):
        moves.append((side_ff, land_ff.at[at - 1], "dp", at << 1))
        moves.append((side_dw.at[at], land_dw.at[at - 1], "dp", at << 1))
    links = start_side(moves, send_sems, recv_sems)
    copies = []
    for number in range(4):
        copies.append(pltpu.make_async_copy(h_ref.at[number], h_all.at[number], sems.at[number]))
        copies.append(
            pltpu.make_async_copy(c_ref.at[number], c_all.at[number], sems.at[4 + number])
        )
    for copy in copies:
        copy.start()
    tiles[column] = own_ref[...]
    rows_part = 16 * TILE // count
    for at in range(count):
        first = pl.multiple_of(differ(at, quarter, replicas) * rows_part, rows_part)
        for bit in (1, 2, 3):
            tiles[flip(column, bit), pl.ds(first, rows_part), :] = part_ref[
                at, (bit - 1) * rows_part : bit * rows_part, :
            ]
    for matrix in range(3):
        for at in range(16):
            w_in[
                (at // 2) * TILE : (at // 2 + 1) * TILE,
                (2 * matrix + at % 2) * TILE : (2 * matrix + at % 2 + 1) * TILE,
            ] = tiles[matrix, at * TILE : (at + 1) * TILE, :]
    for at in range(16):
        w_out[(at // 8) * TILE : (at // 8 + 1) * TILE, (at % 8) * TILE : (at % 8 + 1) * TILE] = (
            tiles[3, at * TILE : (at + 1) * TILE, :]
        )
    in_acc[...] = jnp.zeros_like(in_acc)
    out_acc[...] = jnp.zeros_like(out_acc)
    vec_ref[...] = jnp.zeros_like(vec_ref)
    sum_ref[...] = jnp.zeros_like(sum_ref)
    for copy in copies:
        copy.wait()
    length = h_all.shape[1]
    wide = 4 * HDIM
    block = 256
    half = ROT // 2
    lane = lax.broadcasted_iota(jnp.int32, (1, LANES), 1) % (2 * HDIM)
    keep_low = lane < HDIM
    scale = HDIM ** (-0.5)

    def body(at, carry):
        hat = h_all[at].astype(F32)
        normed = (hat * norm_ref[0:1, :] + norm_ref[1:2, :]).astype(BF16)
        cot = c_all[at]
        table = precise(tab_ref[at], spread_ref[...], 0, 0)
        within = lane % HDIM
        cos_w = table[:, 0:LANES] + (within >= ROT).astype(F32)
        sin_a = table[:, LANES : 2 * LANES]
        sin_b = table[:, 2 * LANES : 3 * LANES]
        proj = dot_nn(normed, w_in[...]) + bias_ref[...]
        g_all[...] = dot_nt(cot, w_out[...]).astype(BF16)
        for pair in range(2):
            cols = slice(pair * LANES, (pair + 1) * LANES)
            query = proj[:, pair * LANES : (pair + 1) * LANES]
            key = proj[:, wide + pair * LANES : wide + (pair + 1) * LANES]

            def turn(value):
                return (
                    value * cos_w
                    - pltpu.roll(value, LANES - half, 1) * sin_a
                    + pltpu.roll(value, half, 1) * sin_b
                )

            q_all[:, cols] = (turn(query).astype(BF16) * scale).astype(BF16)
            k_all[:, cols] = turn(key).astype(BF16)
            v_all[:, cols] = proj[:, 2 * wide + pair * LANES : 2 * wide + (pair + 1) * LANES].astype(
                BF16
            )
        dk_all[...] = jnp.zeros_like(dk_all)
        dv_all[...] = jnp.zeros_like(dv_all)
        for pair in range(2):
            cols = slice(pair * LANES, (pair + 1) * LANES)
            for first in range(0, length, block):
                rows = slice(first, first + block)
                keys = slice(0, first + block)
                out_rows = None
                dq_rows = None
                for head in range(2):
                    mask = keep_low if head == 0 else jnp.logical_not(keep_low)
                    zero = jnp.zeros((), BF16)
                    query = jnp.where(mask, q_all[rows, cols], zero)
                    grad = jnp.where(mask, g_all[rows, cols], zero)
                    key = jnp.where(mask, k_all[keys, cols], zero)
                    value = jnp.where(mask, v_all[keys, cols], zero)
                    scores = dot_nt(query, key)
                    row_at = first + lax.broadcasted_iota(jnp.int32, scores.shape, 0)
                    col_at = lax.broadcasted_iota(jnp.int32, scores.shape, 1)
                    scores = jnp.where(col_at <= row_at, scores, -1e30)
                    peak = jnp.max(scores, axis=-1, keepdims=True)
                    raised = jnp.exp(scores - peak)
                    prob = raised * (1.0 / jnp.sum(raised, axis=-1, keepdims=True))
                    prob_low = prob.astype(BF16)
                    piece = dot_nn(prob_low, value)
                    out_rows = piece if out_rows is None else out_rows + piece
                    grad_prob = dot_nt(grad, value)
                    delta = jnp.sum(prob * grad_prob, axis=-1, keepdims=True)
                    grad_scores = (prob * (grad_prob - delta)).astype(BF16)
                    piece = dot_nn(grad_scores, key)
                    dq_rows = piece if dq_rows is None else dq_rows + piece
                    dk_all[keys, cols] += dot_tn(grad_scores, query)
                    dv_all[keys, cols] += dot_tn(prob_low, grad)
                o_all[rows, cols] = out_rows.astype(BF16)
                dq_all[rows, cols] = dq_rows * scale

        def turn_back(value):
            return (
                value * cos_w
                + pltpu.roll(value, LANES - half, 1) * sin_a
                - pltpu.roll(value, half, 1) * sin_b
            ).astype(BF16)

        pieces = [turn_back(dq_all[:, 0:LANES]), turn_back(dq_all[:, LANES : 2 * LANES])]
        pieces += [turn_back(dk_all[:, 0:LANES]), turn_back(dk_all[:, LANES : 2 * LANES])]
        pieces += [dv_all[...].astype(BF16)]
        grads = jnp.concatenate(pieces, axis=1)
        sum_ref[...] += jnp.sum(grads.astype(F32), axis=0, keepdims=True)
        out = dot_nn(o_all[...], w_out[...]) + acc_refs[0][at].astype(F32)
        out_ref[at] = out.astype(BF16)
        back = dot_nt(grads, w_in[...])
        vec_ref[0:1, :] += jnp.sum(back * hat, axis=0, keepdims=True)
        vec_ref[1:2, :] += jnp.sum(back, axis=0, keepdims=True)
        back = back * norm_ref[0:1, :] + acc_refs[1][at].astype(F32)
        gd_ref[at] = back.astype(BF16)
        in_acc[...] += dot_tn(normed, grads)
        out_acc[...] += dot_tn(o_all[...], cot)
        return carry

    lax.fori_loop(0, 4, body, 0)
    rows_out = dw_ref.shape[2]
    size = min(TILE, rows_out)
    for matrix in range(4):
        for at in range(16):
            for piece in range(TILE // size):
                row = at * TILE + piece * size
                if matrix < 3:
                    top, left = (at // 2) * TILE, (2 * matrix + at % 2) * TILE
                    tile = in_acc[top + piece * size : top + (piece + 1) * size, left : left + TILE]
                else:
                    top, left = (at // 8) * TILE, (at % 8) * TILE
                    tile = out_acc[
                        top + piece * size : top + (piece + 1) * size, left : left + TILE
                    ]
                inner = row % rows_out
                dw_ref[
                    differ(row // rows_out, quarter, replicas),
                    flip(column, matrix),
                    inner : inner + size,
                    :,
                ] = tile.astype(BF16)
    links.finish()


def attention(vectors, bias, spread, side_ff, side_dw, tables, hats, cots, own, parts, acc, replicas):
    length, width = hats.shape[1:]
    wide = 4 * HDIM
    rows_out = 16 * TILE // replicas
    return pl.pallas_call(
        functools.partial(attn_kernel, replicas, replicas),
        out_shape=[
            jax.ShapeDtypeStruct((4, length, width), BF16),
            jax.ShapeDtypeStruct((4, length, width), BF16),
            jax.ShapeDtypeStruct((replicas, 4, rows_out, LANES), BF16),
            jax.ShapeDtypeStruct((2, width), F32),
            jax.ShapeDtypeStruct((1, 3 * wide), F32),
            jax.ShapeDtypeStruct((replicas - 1,) + side_ff.shape, BF16),
            jax.ShapeDtypeStruct((replicas - 1,) + side_dw.shape[1:], BF16),
        ],
        in_specs=[VMEM, VMEM, VMEM, ANY, ANY, VMEM, ANY, ANY] + [VMEM] * 4,
        out_specs=[VMEM] * 5 + [ANY] * 2,
        scratch_shapes=[
            pltpu.VMEM((4, length, width), BF16),
            pltpu.VMEM((4, length, width), BF16),
            pltpu.VMEM((4, 16 * TILE, LANES), BF16),
            pltpu.VMEM((width, 3 * wide), BF16),
            pltpu.VMEM((wide, width), BF16),
            pltpu.VMEM((width, 3 * wide), F32),
            pltpu.VMEM((wide, width), F32),
            pltpu.VMEM((length, wide), BF16),
            pltpu.VMEM((length, wide), BF16),
            pltpu.VMEM((length, wide), BF16),
            pltpu.VMEM((length, wide), BF16),
            pltpu.VMEM((length, wide), BF16),
            pltpu.VMEM((length, wide), F32),
            pltpu.VMEM((length, wide), F32),
            pltpu.VMEM((length, wide), F32),
            pltpu.SemaphoreType.DMA((8,)),
        ]
        + side_shapes(2 * (replicas - 1)),
        compiler_params=pltpu.CompilerParams(
            vmem_limit_bytes=60 << 20, collective_id=4, has_side_effects=True
        ),
        cost_estimate=pl.CostEstimate(
            flops=30 * 10**9, bytes_accessed=20 << 20, transcendentals=0
        ),
        name="attention",
    )(vectors, bias, spread, side_ff, side_dw, tables, hats, cots, own, parts, *acc)


def soap_kernel(slots, replicas, per_step, *refs):
    refs = list(refs)
    take = lambda number: [refs.pop(0) for _ in range(number)]
    place_ref, owner_ref, slab = take(3)
    left_ref, right_ref, first_ref, second_ref, master_ref, ema_ref = take(6)
    grad_ref, first_out, second_out, master_out, copy_out, ema_out = take(6)
    mine, inverse, sem = take(3)
    me, column = place_ref[0], place_ref[1]
    step = pl.program_id(0)
    bias_fix = 1.0 - 0.5**STEP
    rows_ff = 64 * TILE // replicas
    rows_attn = 16 * TILE // replicas
    rows_all = slots * TILE
    size = min(TILE, rows_attn)

    @pl.when(step == 0)
    def _():
        def note(unit, carry):
            inverse[owner_ref[unit]] = unit
            return carry

        lax.fori_loop(0, owner_ref.shape[0], note, 0)

        def fetch(number, carry):
            unit = inverse[me * slots + number]
            row, col = (unit % 64) // 8, unit % 8
            by_rows = column == 3
            rank = jnp.where(by_rows, row // 2, col // 2)
            attn_place = jnp.where(by_rows, (row % 2) * 8 + col, row * 2 + col % 2)
            up_place = row * 4 + col % 4
            down_place = 32 + (row % 4) * 8 + col
            is_attn, is_up = unit < 64, unit < 128
            core = jnp.where(is_attn, rank % 2, jnp.where(is_up, col // 4, row // 4))
            other = ((rank // 2) != (column % 2)).astype(jnp.int32)
            for piece in range(TILE // size):
                attn_row = attn_place * TILE + piece * size
                ff_row = jnp.where(is_up, up_place, down_place) * TILE + piece * size
                holder = jnp.where(is_attn, attn_row // rows_attn, ff_row // rows_ff)
                inner = jnp.where(
                    is_attn, rows_ff + other * rows_attn + attn_row % rows_attn, ff_row % rows_ff
                )
                start = ((holder * 2 + core) ^ me) * rows_all + inner
                pltpu.make_async_copy(
                    slab.at[pl.ds(pl.multiple_of(start, size), size), :],
                    mine.at[number, pl.ds(piece * size, size), :],
                    sem,
                ).start()
            return carry

        lax.fori_loop(0, slots, fetch, 0)
        pltpu.make_async_copy(mine, mine, sem).wait()

    for number in range(per_step):
        grad = mine[step * per_step + number].astype(F32)
        left, right = left_ref[number], right_ref[number]
        grad_ref[number] = grad
        turned = precise(precise(left, grad, 0, 0), right, 1, 0)
        first = 0.5 * first_ref[number] + 0.5 * turned
        second = 0.5 * second_ref[number] + 0.5 * turned * turned
        first_out[number] = first
        second_out[number] = second
        scaled = first / bias_fix / (jnp.sqrt(second / bias_fix) + eps_adam)
        back = precise(precise(left, scaled, 1, 0), right, 1, 1)
        master = master_ref[number] - lr_matrix * back
        master_out[number] = master
        copy_out[number] = master.astype(BF16)
        ema_out[number] = ema_keep * ema_ref[number] + (1.0 - ema_keep) * master


def soap(place, owner_row, slab, state, replicas):
    slots = state[0].shape[0]
    per_step = 4 if slots % 4 == 0 else 1
    spec = pl.BlockSpec((per_step, TILE, TILE), lambda i: (i, 0, 0))
    shape = (slots, TILE, TILE)
    return pl.pallas_call(
        functools.partial(soap_kernel, slots, replicas, per_step),
        grid=(slots // per_step,),
        out_shape=[jax.ShapeDtypeStruct(shape, F32)] * 4
        + [jax.ShapeDtypeStruct(shape, BF16), jax.ShapeDtypeStruct(shape, F32)],
        in_specs=[SMEM, SMEM, ANY] + [spec] * 6,
        out_specs=[spec] * 6,
        scratch_shapes=[
            pltpu.VMEM(shape, BF16),
            pltpu.SMEM((owner_row.shape[0],), jnp.int32),
            pltpu.SemaphoreType.DMA,
        ],
        compiler_params=pltpu.CompilerParams(vmem_limit_bytes=32 << 20),
        cost_estimate=pl.CostEstimate(
            flops=24 * slots * 2 * TILE**3, bytes_accessed=20 << 20, transcendentals=0
        ),
        name="soap",
    )(place, owner_row, slab, *state)


def adam_step(grad, first, second, param):
    bias_fix = 1.0 - 0.5**STEP
    first_new = 0.5 * first + 0.5 * grad
    second_new = 0.5 * second + 0.5 * grad * grad
    return (
        first_new,
        second_new,
        param - lr_vector * (first_new / bias_fix) / (jnp.sqrt(second_new / bias_fix) + eps_adam),
    )


def spread_table():
    lane = jnp.arange(LANES, dtype=jnp.int32) % HDIM
    row = jnp.arange(ROT, dtype=jnp.int32)[:, None]
    half = ROT // 2
    cos_part = (lane < ROT) & (row == lane % half)
    sin_first = (lane < half) & (row == half + lane)
    sin_second = (lane >= half) & (lane < ROT) & (row == lane)
    return jnp.concatenate([cos_part, sin_first, sin_second], axis=1).astype(F32)


def local(
    tokens,
    cotangent,
    positions,
    owners,
    masters,
    basis_left,
    basis_right,
    moment1,
    moment2,
    ema,
    vectors,
    vector_moment1,
    vector_moment2,
    hidden_bias,
    hidden_moment1,
    hidden_moment2,
):
    length, width = tokens.shape
    slots = masters.shape[1]
    me = lax.axis_index("dp")
    column = lax.axis_index("mlp")
    replicas = lax.axis_size("dp") // 2
    core, low = me % 2, column % 2
    rank = 2 * low + core
    place = jnp.stack([me, column, me // 2]).astype(jnp.int32)
    owner_row = owners[0]

    inverse_freq = 10000.0 ** (-(jnp.arange(ROT // 2, dtype=F32) * 2.0) / ROT)
    angles = inverse_freq[:, None] * positions.astype(F32)[None, :]
    table = jnp.concatenate([jnp.cos(angles), jnp.sin(angles)], axis=0)
    hats, cots, tables, attn_parts, own_attn, own_ff, send_ff = front(
        tokens, cotangent, table, masters[0], (owner_row // slots ^ me) * slots + owner_row % slots
    )

    hidden = FF // (2 * GROUP)
    start_own = column * (2 * hidden) + core * hidden
    start_other = (column ^ 2) * (2 * hidden) + core * hidden
    bias_own = lax.dynamic_slice_in_dim(hidden_bias, start_own, hidden, 0)[None]
    bias_other = lax.dynamic_slice_in_dim(hidden_bias, start_other, hidden, 0)[None]
    wide = width // GROUP
    bias_qkv = lax.dynamic_slice(vectors, (4, rank * wide), (3, wide)).reshape(1, 3 * wide)

    out, back, dw_own, vec_own, hid_own, other_ff = feed_forward(
        vectors, bias_own, send_ff, hats, cots, [own_ff], None, replicas
    )
    out, back, dw_attn, vec_attn, sums, ff_land, own_land = attention(
        vectors,
        bias_qkv,
        spread_table(),
        other_ff,
        dw_own,
        tables,
        hats,
        cots,
        own_attn,
        attn_parts,
        (out, back),
        replicas,
    )
    out, back, dw_other, vec_other, hid_other, attn_side = feed_forward(
        vectors, bias_other, dw_attn, hats, cots, [other_ff, ff_land], (out, back), replicas
    )
    grad_bias_out = jnp.sum(cotangent.astype(BF16).astype(F32), axis=0)
    sums = lax.dynamic_update_slice(
        jnp.zeros((3, width), F32), sums.reshape(3, wide), (0, rank * wide)
    )
    hidden_part = lax.dynamic_update_slice_in_dim(
        jnp.zeros((FF,), F32), hid_own[0], start_own, 0
    )
    hidden_part = lax.dynamic_update_slice_in_dim(hidden_part, hid_other[0], start_other, 0)
    vector_part = jnp.concatenate(
        [
            vec_attn,
            vec_own + vec_other,
            sums,
            grad_bias_out[None],
            hidden_part.reshape(-1, width),
        ],
        axis=0,
    )
    slab, result, grad_tokens, reduced = send_back(
        dw_other,
        (dw_own, own_land),
        (dw_attn, attn_side),
        out,
        back,
        tokens,
        cotangent,
        vectors,
        vector_part,
        slots,
    )
    state = [item[0] for item in (basis_left, basis_right, moment1, moment2, masters, ema)]
    own_grad, first_new, second_new, master_new, weight_copy, ema_new = soap(
        place, owner_row, slab, state, replicas
    )
    vector_grad = jnp.concatenate([reduced[:8], reduced[7:8]], axis=0)
    hidden_grad = reduced[8:].reshape(FF)
    vec_first, vec_second, vectors_new = adam_step(
        vector_grad, vector_moment1, vector_moment2, vectors
    )
    hid_first, hid_second, hidden_new = adam_step(
        hidden_grad, hidden_moment1, hidden_moment2, hidden_bias
    )
    return (
        result,
        grad_tokens,
        own_grad[None],
        first_new[None],
        second_new[None],
        master_new[None],
        weight_copy[None],
        ema_new[None],
        vector_grad,
        vec_first,
        vec_second,
        vectors_new,
        hidden_grad,
        hid_first,
        hid_second,
        hidden_new,
    )


def solution(mesh):
    split = P(("dp", "mlp"), None)
    tiled = P("mlp", "dp", None, None)
    return jax.shard_map(
        local,
        mesh=mesh,
        in_specs=(split, split, P(("dp", "mlp")), P("mlp", None)) + (tiled,) * 6 + (P(),) * 6,
        out_specs=(split, split) + (tiled,) * 6 + (P(),) * 8,
        check_vma=False,
    )
```

```python
import functools

import jax
import jax.numpy as jnp
from jax import lax
from jax.experimental import pallas as pl
from jax.experimental.pallas import tpu as pltpu
from jax.sharding import PartitionSpec as P

HEADS = 16
HDIM = 64
ROT = 16
FF = 4096
STEP = 5
TILE = 128
LANES = 128
GROUP = 4

PRECISE = lax.Precision.HIGHEST
eps_norm = 1e-05
eps_adam = 1e-08
lr_matrix = 0.05
lr_vector = 0.5
ema_keep = 0.8

F32 = jnp.float32
BF16 = jnp.bfloat16
ANY = pl.BlockSpec(memory_space=pl.ANY)
VMEM = pl.BlockSpec(memory_space=pltpu.VMEM)
SMEM = pl.BlockSpec(memory_space=pltpu.SMEM)


def dot_nn(left, right):
    return jnp.dot(left, right, preferred_element_type=F32)


def dot_nt(left, right):
    return lax.dot_general(left, right, (((1,), (1,)), ((), ())), preferred_element_type=F32)


def dot_tn(left, right):
    return lax.dot_general(left, right, (((0,), (0,)), ((), ())), preferred_element_type=F32)


def precise(left, right, left_dim, right_dim):
    return lax.dot_general(
        left,
        right,
        (((left_dim,), (right_dim,)), ((), ())),
        precision=PRECISE,
        preferred_element_type=F32,
    )


MESH = pl.DeviceIdType.MESH


def flip(index, mask):
    bit = 1
    while bit <= mask:
        if mask & bit:
            index = index + bit - 2 * bit * ((index // bit) % 2)
        bit *= 2
    return index


def differ(left, right, count):
    total, bit = 0, 1
    while bit < count:
        one, two = (left // bit) % 2, (right // bit) % 2
        total = total + bit * (one + two - 2 * one * two)
        bit *= 2
    return total


class Links:
    def __init__(self, send_sems, recv_sems):
        self.send_sems, self.recv_sems = send_sems, recv_sems
        self.number = 0
        self.all = []

    def send(self, source, target, device):
        copy = pltpu.make_async_remote_copy(
            src_ref=source,
            dst_ref=target,
            send_sem=self.send_sems.at[self.number],
            recv_sem=self.recv_sems.at[self.number],
            device_id=device,
            device_id_type=MESH,
        )
        self.number += 1
        copy.start()
        entry = [copy, False, False]
        self.all.append(entry)
        return entry

    def arrived(self, entry):
        if not entry[1]:
            entry[0].wait_recv()
            entry[1] = True

    def left(self, entry):
        if not entry[2]:
            entry[0].wait_send()
            entry[2] = True

    def finish(self):
        for entry in self.all:
            self.arrived(entry)
            self.left(entry)


def greet(me, column, masks_dp, masks_z):
    barrier = pltpu.get_barrier_semaphore()
    for mask in masks_dp:
        pl.semaphore_signal(barrier, inc=1, device_id={"dp": flip(me, mask)}, device_id_type=MESH)
    for mask in masks_z:
        pl.semaphore_signal(
            barrier, inc=1, device_id={"mlp": flip(column, mask)}, device_id_type=MESH
        )
    pl.semaphore_wait(barrier, len(masks_dp) + len(masks_z))


class Spread:
    def __init__(self, links, slab, me, count, rows, first, size, backward, pairs=True):
        self.links, self.slab, self.me, self.pairs = links, slab, me, pairs
        self.rows, self.first, self.size = rows, first, size
        self.bits = [1 << i for i in range(1, count.bit_length() - 1)]
        if backward:
            self.bits = self.bits[::-1]
        self.came = {}
        self.order = []

    def part(self, at):
        place = at if self.pairs else at // 2
        return self.slab.at[pl.ds(place * self.rows + self.first, self.size)]

    def forward(self, at, step, source=None):
        source = self.part(at) if source is None else source
        for later in range(step, len(self.bits)):
            bit = self.bits[later]
            entry = self.links.send(source, self.part(at ^ bit), {"dp": flip(self.me, bit)})
            self.came[at ^ bit] = (entry, later + 1)
            self.order.append(at ^ bit)
        if self.pairs:
            self.links.send(source, self.part(at ^ 1), {"dp": flip(self.me, 1)})

    def relay(self):
        while self.order:
            at = min(self.order, key=lambda index: (self.came[index][1], index.bit_count()))
            self.order.remove(at)
            entry, step = self.came[at]
            self.links.arrived(entry)
            self.forward(at, step)


def attn_unit(column, rank, place):
    by_columns = (place // 2) * 8 + 2 * rank + place % 2
    by_rows = (2 * rank + place // 8) * 8 + place % 8
    return jnp.where(column == 3, by_rows, by_columns)


def ff_unit(core, place):
    later = place - 32
    up = 64 + (place // 4) * 8 + core * 4 + place % 4
    down = 128 + (core * 4 + later // 8) * 8 + later % 8
    return jnp.where(place < 32, up, down)


def front_kernel(slots, devices, tokens, cot, table, masters, tile_ref, *refs):
    (hats, cots, tables, attn_parts, own_attn, own_ff, send_ff) = refs[:7]
    (slab, own_hat, own_cot, send_attn, send_sems, recv_sems, local_sems) = refs[7:]
    me, column = lax.axis_index("dp"), lax.axis_index("mlp")
    replicas = devices // 2
    core, quarter, low = me % 2, me // 2, column % 2
    links = Links(send_sems, recv_sems)
    half = slots // 2
    greet(me, column, [1] + [at << 1 for at in range(1, replicas)], [1, 2, 3])
    slab[0:slots] = masters[...].astype(BF16)
    spreads = [
        Spread(links, slab, me, devices, slots, 0, half, False),
        Spread(links, slab, me, devices, slots, half, slots - half, True),
    ]
    for spread in spreads:
        spread.forward(0, 0)

    length = tokens.shape[0]
    step_rows = 128

    def normalize(step, carry):
        where = pl.ds(pl.multiple_of(step * step_rows, step_rows), step_rows)
        value = tokens[where, :]
        value = value - jnp.mean(value, axis=-1, keepdims=True)
        value = value * lax.rsqrt(jnp.mean(value * value, axis=-1, keepdims=True) + eps_norm)
        own_hat[where, :] = value.astype(BF16)
        own_cot[where, :] = cot[where, :].astype(BF16)
        return carry

    lax.fori_loop(0, length // step_rows, normalize, 0)
    own = []
    along = []

    def send_along(source, target, where):
        entry = links.send(source.at[where], target.at[2].at[where], {"mlp": flip(column, 1)})
        along.append((target, where, entry))

    for number, (source, target) in enumerate(
        ((own_hat, hats), (table, tables), (own_cot, cots))
    ):
        send_along(source, target, pl.ds(0, source.shape[0] // (2 if number == 2 else 1)))
        links.send(source, target.at[1], {"dp": flip(me, 1)})
        copy = pltpu.make_async_copy(source, target.at[0], local_sems.at[number])
        copy.start()
        own.append(copy)
    for spread in spreads:
        spread.relay()
    for entry in links.all:
        if not any(entry is item[2] for item in along):
            links.arrived(entry)

    def fill(out_ref, base, rows_out, first_row, unit_of):
        size = min(TILE, rows_out)

        def body(step, carry):
            row = first_row + step * size
            tile = tile_ref[unit_of(row // TILE)]
            where = pl.ds(pl.multiple_of(base + step * size, size), size)
            if size == TILE:
                out_ref[where, :] = slab[tile]
            else:
                out_ref[where, :] = slab[tile, pl.ds(pl.multiple_of(row % TILE, size), size), :]
            return carry

        lax.fori_loop(0, rows_out // size, body, 0)

    rows_attn = 16 * TILE // replicas
    across = []
    for bit in (3, 2, 1):
        rank = 2 * (flip(low, 1) if bit & 1 else low) + core
        base = (bit - 1) * rows_attn
        fill(
            send_attn,
            base,
            rows_attn,
            quarter * rows_attn,
            functools.partial(attn_unit, column, rank),
        )
        piece = pl.ds(base, rows_attn)
        across.append(
            (
                piece,
                links.send(
                    send_attn.at[piece, :],
                    attn_parts.at[piece, :],
                    {"mlp": flip(column, bit)},
                ),
            )
        )
    send_along(own_cot, cots, pl.ds(length // 2, length // 2))
    rows_ff = 64 * TILE // replicas
    fill(own_attn, 0, 16 * TILE, 0, functools.partial(attn_unit, column, 2 * low + core))
    spreads = []
    for number, (piece, entry) in enumerate(across[::-1]):
        links.arrived(entry)
        pieces = [(number * rows_attn, rows_attn, number == 1)]
        if number == 2:
            cut = rows_attn // 32 * 16
            pieces = [
                (2 * rows_attn, cut, False),
                (2 * rows_attn + cut, rows_attn - cut, True),
            ]
        for first, size, backward in pieces:
            spreads.append(
                Spread(links, attn_parts, me, devices, 3 * rows_attn, first, size, backward, False)
            )
            spreads[-1].forward(0, 0)
    fill(send_ff, 0, rows_ff, quarter * rows_ff, functools.partial(ff_unit, core))
    fill(own_ff, 0, 64 * TILE, 0, functools.partial(ff_unit, core))
    for spread in spreads:
        spread.relay()
    for target, where, entry in along:
        links.arrived(entry)
        links.send(target.at[2].at[where], target.at[3].at[where], {"dp": flip(me, 1)})
    for copy in own:
        copy.wait()
    links.finish()


def front(tokens, cot, table, masters, tile_row):
    length, width = tokens.shape
    slots = masters.shape[0]
    devices = lax.axis_size("dp")
    replicas = devices // 2
    rows_attn = 16 * TILE // replicas
    count = 2 * (2 * replicas - 1) + 11 + 3 + 4 * (replicas - 1)
    block = jax.ShapeDtypeStruct((4, length, width), BF16)
    flat = lambda number: jax.ShapeDtypeStruct((number, LANES), BF16)
    return pl.pallas_call(
        functools.partial(front_kernel, slots, devices),
        out_shape=[
            block,
            block,
            jax.ShapeDtypeStruct((4,) + table.shape, F32),
            jax.ShapeDtypeStruct((replicas * 3 * rows_attn, LANES), BF16),
            flat(16 * TILE),
            flat(64 * TILE),
            flat(64 * TILE // replicas),
        ],
        in_specs=[VMEM] * 4 + [SMEM],
        out_specs=[ANY] * 4 + [VMEM] * 3,
        scratch_shapes=[
            pltpu.VMEM((devices * slots, TILE, LANES), BF16),
            pltpu.VMEM((length, width), BF16),
            pltpu.VMEM((length, width), BF16),
            pltpu.VMEM((3 * rows_attn, LANES), BF16),
            pltpu.SemaphoreType.DMA((count,)),
            pltpu.SemaphoreType.DMA((count,)),
            pltpu.SemaphoreType.DMA((3,)),
        ],
        compiler_params=pltpu.CompilerParams(
            vmem_limit_bytes=60 << 20, collective_id=0, has_side_effects=True
        ),
        cost_estimate=pl.CostEstimate(flops=0, bytes_accessed=200 << 20, transcendentals=0),
        name="front",
    )(tokens, cot, table, masters, tile_row)


def erf_f32(value):
    value = jnp.clip(value, -3.832506856900711, 3.832506856900711)
    square = value * value
    top = jnp.full_like(square, 0.00022905065861350646)
    for coeff in (
        0.0034082910107109506,
        0.050955695062380861,
        0.18520832239976145,
        1.128379143519084,
    ):
        top = top * square + coeff
    low = jnp.full_like(square, -1.1791602954361697e-7)
    for coeff in (
        0.000023547966471313185,
        0.0010179625278914885,
        0.014070470171167667,
        0.11098505178285362,
        0.49746925110067538,
        1.0,
    ):
        low = low * square + coeff
    return value * top / low


def row_sum(value):
    return dot_nn(jnp.ones((16, value.shape[0]), BF16), value)[0:1, :]


def transpose_tile(value):
    return jnp.swapaxes(value, 0, 1)


def middle_kernel(slots, devices, *refs):
    refs = list(refs)
    take = lambda number: [refs.pop(0) for _ in range(number)]
    norm_ref, hidden_ref, table_ref, hats, cots = take(5)
    own_attn, attn_parts, own_ff, send_ff = take(4)
    mine, across, slab, reduced = take(4)
    h_all, c_all, out_acc, back_acc = take(4)
    tiles, up, down, up_acc, down_acc = take(5)
    w_in, w_out, in_acc, proj_acc = take(4)
    q_all, k_all, v_all, g_all, o_all, dq_all, dk_all, dv_all = take(8)
    dw, own_land, attn_land, z_ff, core_land = take(5)
    own_sum, attn_keep, attn_send, attn_back, z_send, z_land, block_all = take(7)
    vec, vec_land, vec_sum = take(3)
    local_sems, tile_sems, send_sems, recv_sems = take(4)
    me, column = lax.axis_index("dp"), lax.axis_index("mlp")
    replicas = devices // 2
    core, quarter = me % 2, me // 2
    rank = 2 * (column % 2) + core
    length, width = h_all.shape[1:]
    hidden = up.shape[1]
    wide = 4 * HDIM
    rows_ff, rows_attn = 64 * TILE // replicas, 16 * TILE // replicas
    loads = []
    tile_load = pltpu.make_async_copy(own_ff, tiles, local_sems.at[8])
    tile_load.start()
    for number in range(4):
        pair = []
        for source, target, sem in ((hats, h_all, number), (cots, c_all, 4 + number)):
            copy = pltpu.make_async_copy(source.at[number], target.at[number], local_sems.at[sem])
            copy.start()
            pair.append(copy)
        loads.append(pair)
    links = Links(send_sems, recv_sems)
    greet(me, column, [1] + [at << 1 for at in range(1, replicas)], [1, 2, 3])
    came_ff = [links.send(send_ff, z_ff.at[0], {"mlp": flip(column, 2)})]
    vec[...] = jnp.zeros_like(vec)

    def set_ff_weights():
        for at in range(32):
            up[
                (at // 4) * TILE : (at // 4 + 1) * TILE, (at % 4) * TILE : (at % 4 + 1) * TILE
            ] = tiles[at * TILE : (at + 1) * TILE, :]
            down[
                (at // 8) * TILE : (at // 8 + 1) * TILE, (at % 8) * TILE : (at % 8 + 1) * TILE
            ] = tiles[(32 + at) * TILE : (33 + at) * TILE, :]
        up_acc[...] = jnp.zeros_like(up_acc)
        down_acc[...] = jnp.zeros_like(down_acc)

    def ff_block(at, ff_column, first, store):
        hat = h_all[at].astype(F32)
        normed = (hat * norm_ref[2:3, :] + norm_ref[3:4, :]).astype(BF16)
        cot = c_all[at]
        pre = dot_nn(normed, up[...]) + hidden_ref[pl.ds(2 * ff_column + core, 1), :]
        cdf = 0.5 + 0.5 * erf_f32(pre * 0.7071067811865476)
        act = (pre * cdf).astype(BF16)
        grad = dot_nt(cot, down[...])
        grad = grad * (cdf + pre * (jnp.exp(-0.5 * pre * pre) * 0.3989422804014327))
        grad = grad.astype(BF16)
        where = pl.ds(pl.multiple_of(core * hidden, hidden), hidden)
        vec[pl.ds(8 + ff_column, 1), where] += row_sum(grad)
        out = dot_nn(act, down[...])
        back = dot_nt(grad, up[...])
        vec[2:3, :] += jnp.sum(back * hat, axis=0, keepdims=True)
        vec[3:4, :] += jnp.sum(back, axis=0, keepdims=True)
        back = back * norm_ref[2:3, :]
        if not first:
            out = out + out_acc[at].astype(F32)
            back = back + back_acc[at].astype(F32)
        store(out, back)
        up_acc[...] += dot_tn(normed, grad)
        down_acc[...] += dot_tn(act, cot)

    def store_ff(target):
        per = rows_ff // TILE
        for at in range(64):
            if at < 32:
                tile = up_acc[
                    (at // 4) * TILE : (at // 4 + 1) * TILE, (at % 4) * TILE : (at % 4 + 1) * TILE
                ]
            else:
                low = at - 32
                tile = down_acc[
                    (low // 8) * TILE : (low // 8 + 1) * TILE,
                    (low % 8) * TILE : (low % 8 + 1) * TILE,
                ]
            target[
                differ(at // per, quarter, replicas), (at % per) * TILE : (at % per + 1) * TILE, :
            ] = tile.astype(BF16)

    def attn_rows(matrix):
        return pl.multiple_of(matrix * (16 * TILE), TILE)

    tile_load.wait()
    set_ff_weights()
    tile_loads = [
        pltpu.make_async_copy(
            own_attn, tiles.at[pl.ds(attn_rows(column), 16 * TILE), :], tile_sems.at[0]
        )
    ]
    for at in range(replicas):
        for bit in (1, 2, 3):
            first = attn_rows(flip(column, bit)) + differ(at, quarter, replicas) * rows_attn
            tile_loads.append(
                pltpu.make_async_copy(
                    attn_parts.at[pl.ds((3 * at + bit - 1) * rows_attn, rows_attn), :],
                    tiles.at[pl.ds(pl.multiple_of(first, rows_attn), rows_attn), :],
                    tile_sems.at[len(tile_loads)],
                )
            )
    for copy in tile_loads:
        copy.start()
    for at in range(4):
        for copy in loads[at]:
            copy.wait()
    vec[7:8, :] = row_sum(c_all[0])

    def own_block(at, carry):
        def store(out, back):
            out_acc[at] = out.astype(BF16)
            back_acc[at] = back.astype(BF16)

        ff_block(at, column, True, store)
        return carry

    lax.fori_loop(0, 4, own_block, 0)
    store_ff(dw)
    own_sum[...] = dw[0].astype(F32)
    own_came = [
        links.send(dw.at[at], own_land.at[at - 1], {"dp": flip(me, at << 1)})
        for at in range(1, replicas)
    ]
    links.arrived(came_ff[0])
    for at in range(1, replicas):
        came_ff.append(links.send(z_ff.at[0], z_ff.at[at], {"dp": flip(me, at << 1)}))

    for copy in tile_loads:
        copy.wait()
    for matrix in range(3):
        for at in range(16):
            row = (16 * matrix + at) * TILE
            w_in[
                (at // 2) * TILE : (at // 2 + 1) * TILE,
                (2 * matrix + at % 2) * TILE : (2 * matrix + at % 2 + 1) * TILE,
            ] = tiles[row : row + TILE, :]
    for at in range(16):
        w_out[(at // 8) * TILE : (at // 8 + 1) * TILE, (at % 8) * TILE : (at % 8 + 1) * TILE] = (
            tiles[(48 + at) * TILE : (49 + at) * TILE, :]
        )
    in_acc[...] = jnp.zeros_like(in_acc)
    proj_acc[...] = jnp.zeros_like(proj_acc)
    half = ROT // 2
    block = BLOCK
    scale = HDIM ** (-0.5)
    lane = lax.broadcasted_iota(jnp.int32, (1, LANES), 1)
    within = lane % HDIM
    keep_low = lane < HDIM
    wave = lax.broadcasted_iota(jnp.int32, (ROT, LANES), 0)
    spot = lax.broadcasted_iota(jnp.int32, (ROT, LANES), 1) % HDIM
    pick_cos = ((spot < ROT) & (wave == spot % half)).astype(F32)
    pick_first = ((spot < half) & (wave == half + spot)).astype(F32)
    pick_second = ((spot >= half) & (spot < ROT) & (wave == spot)).astype(F32)
    plain = (within >= ROT).astype(F32)

    def attn_block(at, carry):
        hat = h_all[at].astype(F32)
        normed = (hat * norm_ref[0:1, :] + norm_ref[1:2, :]).astype(BF16)
        cot = c_all[at]
        table = table_ref[at]
        cos_w = precise(table, pick_cos, 0, 0) + plain
        sin_a = precise(table, pick_first, 0, 0)
        sin_b = precise(table, pick_second, 0, 0)
        proj = dot_nn(normed, w_in[...])
        g_all[...] = dot_nt(cot, w_out[...]).astype(BF16)

        def turn(value):
            return (
                value * cos_w
                - pltpu.roll(value, LANES - half, 1) * sin_a
                + pltpu.roll(value, half, 1) * sin_b
            )

        for pair in range(2):
            cols = slice(pair * LANES, (pair + 1) * LANES)
            where = pl.ds(pl.multiple_of(rank * wide + pair * LANES, LANES), LANES)
            query = proj[:, pair * LANES : (pair + 1) * LANES] + norm_ref[4:5, where]
            key = proj[:, wide + pair * LANES : wide + (pair + 1) * LANES] + norm_ref[5:6, where]
            value = proj[:, 2 * wide + pair * LANES : 2 * wide + (pair + 1) * LANES]
            q_all[:, cols] = (turn(query).astype(BF16) * scale).astype(BF16)
            k_all[:, cols] = turn(key).astype(BF16)
            v_all[:, cols] = (value + norm_ref[6:7, where]).astype(BF16)
        zero = jnp.zeros((), BF16)
        for pair in range(2):
            cols = slice(pair * LANES, (pair + 1) * LANES)
            query, key = q_all[:, cols], k_all[:, cols]
            value, grad = v_all[:, cols], g_all[:, cols]
            key_t, value_t = transpose_tile(key), transpose_tile(value)
            out_t, dq_t = [], []
            dk_all[:, cols] = jnp.zeros((length, LANES), F32)
            dv_all[:, cols] = jnp.zeros((length, LANES), F32)
            for head in range(2):
                mask = keep_low if head == 0 else jnp.logical_not(keep_low)
                key_m, value_m = jnp.where(mask, key, zero), jnp.where(mask, value, zero)
                query_m, grad_m = jnp.where(mask, query, zero), jnp.where(mask, grad, zero)
                part = slice(head * HDIM, (head + 1) * HDIM)
                out_row, dq_row = [], []
                for first in range(0, length, block):
                    last = first + block
                    scores = dot_nt(key_m[:last], query[first:last])
                    key_at = lax.broadcasted_iota(jnp.int32, scores.shape, 0)
                    query_at = first + lax.broadcasted_iota(jnp.int32, scores.shape, 1)
                    scores = jnp.where(key_at <= query_at, scores, -1e30)
                    peak = jnp.max(scores, axis=0, keepdims=True)
                    raised = jnp.exp(scores - peak)
                    prob = raised * (1.0 / jnp.sum(raised, axis=0, keepdims=True))
                    prob_low = prob.astype(BF16)
                    grad_prob = dot_nt(value_m[:last], grad[first:last])
                    delta = jnp.sum(prob * grad_prob, axis=0, keepdims=True)
                    grad_scores = (prob * (grad_prob - delta)).astype(BF16)
                    out_row.append(dot_nn(value_t[part, :last], prob_low))
                    dq_row.append(dot_nn(key_t[part, :last], grad_scores))
                    dv_all[:last, cols] += dot_nn(prob_low, grad_m[first:last])
                    dk_all[:last, cols] += dot_nn(grad_scores, query_m[first:last])
                out_t.append(jnp.concatenate(out_row, axis=1))
                dq_t.append(jnp.concatenate(dq_row, axis=1))
            o_all[:, cols] = transpose_tile(jnp.concatenate(out_t, axis=0)).astype(BF16)
            dq_all[:, cols] = transpose_tile(jnp.concatenate(dq_t, axis=0)) * scale

        def turn_back(value):
            return (
                value * cos_w
                + pltpu.roll(value, LANES - half, 1) * sin_a
                - pltpu.roll(value, half, 1) * sin_b
            ).astype(BF16)

        pieces = [turn_back(dq_all[:, 0:LANES]), turn_back(dq_all[:, LANES : 2 * LANES])]
        pieces += [turn_back(dk_all[:, 0:LANES]), turn_back(dk_all[:, LANES : 2 * LANES])]
        pieces += [dv_all[...].astype(BF16)]
        grads = jnp.concatenate(pieces, axis=1)
        sums = row_sum(grads)
        where = pl.ds(pl.multiple_of(rank * wide, LANES), wide)
        for matrix in range(3):
            vec[4 + matrix : 5 + matrix, where] += sums[:, matrix * wide : (matrix + 1) * wide]
        out = dot_nn(o_all[...], w_out[...])
        out_acc[at] = (out_acc[at].astype(F32) + out).astype(BF16)
        back = dot_nt(grads, w_in[...])
        vec[0:1, :] += jnp.sum(back * hat, axis=0, keepdims=True)
        vec[1:2, :] += jnp.sum(back, axis=0, keepdims=True)
        back_acc[at] = (back_acc[at].astype(F32) + back * norm_ref[0:1, :]).astype(BF16)
        in_acc[...] += dot_tn(normed, grads)
        proj_acc[...] += dot_tn(o_all[...], cot)
        return carry

    lax.fori_loop(0, 4, attn_block, 0)
    for entry in own_came:
        links.arrived(entry)
        links.left(entry)
    for at in range(1, replicas):
        own_sum[...] += own_land[at - 1].astype(F32)
    size = min(TILE, rows_attn)
    for matrix in range(4):
        for at in range(16):
            for piece in range(TILE // size):
                row = at * TILE + piece * size
                if matrix < 3:
                    top, left = (at // 2) * TILE, (2 * matrix + at % 2) * TILE
                    tile = in_acc[top + piece * size : top + (piece + 1) * size, left : left + TILE]
                else:
                    top, left = (at // 8) * TILE, (at % 8) * TILE
                    tile = proj_acc[
                        top + piece * size : top + (piece + 1) * size, left : left + TILE
                    ]
                inner = row % rows_attn
                dw[
                    differ(row // rows_attn, quarter, replicas),
                    pl.ds(
                        pl.multiple_of(flip(column, matrix) * rows_attn + inner, size), size
                    ),
                    :,
                ] = tile.astype(BF16)
    attn_came = [
        links.send(dw.at[at], attn_land.at[at - 1], {"dp": flip(me, at << 1)})
        for at in range(1, replicas)
    ]
    attn_keep[...] = dw[0, 0:rows_attn, :].astype(F32)
    attn_send[...] = dw[0, rows_attn : 4 * rows_attn, :]

    other = flip(column, 2)
    for entry in came_ff:
        links.arrived(entry)
    for at in range(replicas):
        first = differ(at, quarter, replicas) * rows_ff
        tiles[pl.ds(pl.multiple_of(first, TILE), rows_ff), :] = z_ff[at]
    set_ff_weights()
    core_came = {}
    outs = []
    waiting = []

    def pump(count):
        for number, source, where in waiting[:count]:
            links.send(
                source.at[2, where, :], across.at[number, where, :], {"mlp": flip(column, 1)}
            )
        del waiting[:count]

    def send_core(at):
        def store(out, back):
            out_acc[at] = out.astype(BF16)
            back_acc[at] = back.astype(BF16)
            for number, source in ((0, out_acc), (1, back_acc)):
                core_came[number, at // 2] = links.send(
                    source.at[at], core_land.at[number, at // 2], {"dp": flip(me, 1)}
                )

        return store

    def keep(at):
        def store(out, back):
            for number, value, source in ((0, out, out_acc), (1, back, back_acc)):
                links.arrived(core_came[number, at // 2])
                value = value + core_land[number, at // 2].astype(F32)
                source[at] = value.astype(BF16)
                if at == 0:
                    copy = pltpu.make_async_copy(
                        source.at[at], mine.at[number], local_sems.at[number]
                    )
                    copy.start()
                    outs.append(copy)
                else:
                    for first in range(0, length, length // 4):
                        waiting.append((number, source, pl.ds(first, length // 4)))

        return store

    for at in (3, 2, 1, 0):
        ff_block(at, other, False, send_core(at) if at % 2 else keep(at))
        pump(1)
    for entry in attn_came:
        links.arrived(entry)
        links.left(entry)

    store_ff(dw)
    chunks = 4
    size = rows_ff // chunks
    dw_came = []
    for chunk in range(chunks):
        piece = pl.ds(chunk * size, size)
        dw_came.append(
            [
                links.send(
                    dw.at[at, piece, :], own_land.at[at - 1, piece, :], {"dp": flip(me, at << 1)}
                )
                for at in range(1, replicas)
            ]
        )
    vec_came = [
        links.send(vec, vec_land.at[bit], {"mlp": flip(column, bit)}) for bit in (1, 2, 3)
    ]
    for at in range(1, replicas):
        attn_keep[...] += attn_land[at - 1, 0:rows_attn, :].astype(F32)
    total = attn_send[...].astype(F32)
    for at in range(1, replicas):
        total = total + attn_land[at - 1, rows_attn : 4 * rows_attn, :].astype(F32)
    attn_send[...] = total.astype(BF16)
    back_came = []
    for bit in (1, 2, 3):
        piece = pl.ds((bit - 1) * rows_attn, rows_attn)
        back_came.append(
            links.send(attn_send.at[piece, :], attn_back.at[bit - 1], {"mlp": flip(column, bit)})
        )
    pump(1)
    rows = slots * TILE
    spreads = []

    def publish(first, count):
        backward = len(spreads) % 2 == 1
        spread = Spread(links, slab, me, devices, rows, first, count, backward)
        source = block_all.at[pl.ds(first, count), :]
        spread.forward(0, 0, source)
        copy = pltpu.make_async_copy(source, spread.part(0), local_sems.at[2 + len(spreads)])
        copy.start()
        outs.append(copy)
        spreads.append(spread)

    def add_chunk(chunk):
        piece = slice(chunk * size, (chunk + 1) * size)
        for entry in dw_came[chunk]:
            links.arrived(entry)
        total = dw[0, piece, :].astype(F32)
        for at in range(1, replicas):
            total = total + own_land[at - 1, piece, :].astype(F32)
        z_send[piece, :] = total.astype(BF16)
        where = pl.ds(chunk * size, size)
        return links.send(z_send.at[where, :], z_land.at[where, :], {"mlp": flip(column, 2)})

    for entry in vec_came:
        links.arrived(entry)
    vec_sum[0] = (vec[...] + vec_land[1]) + (vec_land[2] + vec_land[3])
    vec_core = links.send(vec_sum.at[0], vec_land.at[0], {"dp": flip(me, 1)})
    z_came = [add_chunk(0)]
    pump(1)
    for entry in back_came:
        links.arrived(entry)
    block_all[rows_ff : rows_ff + rows_attn, :] = (
        attn_keep[...] + attn_back[1].astype(F32)
    ).astype(BF16)
    publish(rows_ff, rows_attn)
    block_all[rows_ff + rows_attn : rows, :] = (
        attn_back[0].astype(F32) + attn_back[2].astype(F32)
    ).astype(BF16)
    publish(rows_ff + rows_attn, rows_attn)
    links.arrived(vec_core)
    vec_sum[1] = vec_sum[0] + vec_land[0]
    vec_came = [
        links.send(vec_sum.at[1], vec_land.at[3 + at], {"dp": flip(me, at << 1)})
        for at in range(1, replicas)
    ]
    for chunk in range(1, chunks):
        z_came.append(add_chunk(chunk))
        pump(1)
    for spread in spreads[:2]:
        spread.relay()
    for chunk in range(chunks):
        links.arrived(z_came[chunk])
        piece = slice(chunk * size, (chunk + 1) * size)
        block_all[piece, :] = (own_sum[piece, :] + z_land[piece, :].astype(F32)).astype(BF16)
        publish(chunk * size, size)
        pump(1)
        if chunk > 0:
            spreads[1 + chunk].relay()
    pump(len(waiting))
    spreads[1 + chunks].relay()
    for entry in vec_came:
        links.arrived(entry)
    values = [vec_sum[1]] + [vec_land[3 + at] for at in range(1, replicas)]
    while len(values) > 1:
        values = [values[i] + values[i + 1] for i in range(0, len(values), 2)]
    reduced[...] = values[0]
    for copy in outs:
        copy.wait()
    links.finish()


BLOCK = 256


def middle(vectors, hidden_bias, tables, hats, cots, own_attn, attn_parts, own_ff, send_ff, slots):
    length, width = hats.shape[1:]
    devices = lax.axis_size("dp")
    replicas = devices // 2
    hidden = 4 * TILE
    wide = 4 * HDIM
    rows_ff, rows_attn = 64 * TILE // replicas, 16 * TILE // replicas
    count = 1 + 3 * (replicas - 1) + 4 + 8 + 4 * (replicas - 1) + 3 + 3 + 4 + 1 + replicas - 1
    count += 6 * (2 * replicas - 1)
    rows = slots * TILE
    vmem = lambda *shape: pltpu.VMEM(shape, BF16)
    vmem32 = lambda *shape: pltpu.VMEM(shape, F32)
    return pl.pallas_call(
        functools.partial(middle_kernel, slots, devices),
        out_shape=[
            jax.ShapeDtypeStruct((2, length, width), BF16),
            jax.ShapeDtypeStruct((2, length, width), BF16),
            jax.ShapeDtypeStruct((devices * rows, LANES), BF16),
            jax.ShapeDtypeStruct((12, width), F32),
        ],
        in_specs=[VMEM] * 3 + [ANY] * 6,
        out_specs=[ANY] * 3 + [VMEM],
        scratch_shapes=[
            vmem(4, length, width),
            vmem(4, length, width),
            vmem(4, length, width),
            vmem(4, length, width),
            vmem(64 * TILE, LANES),
            vmem(width, hidden),
            vmem(hidden, width),
            vmem32(width, hidden),
            vmem32(hidden, width),
            vmem(width, 3 * wide),
            vmem(wide, width),
            vmem32(width, 3 * wide),
            vmem32(wide, width),
            vmem(length, wide),
            vmem(length, wide),
            vmem(length, wide),
            vmem(length, wide),
            vmem(length, wide),
            vmem32(length, wide),
            vmem32(length, wide),
            vmem32(length, wide),
            vmem(replicas, rows_ff, LANES),
            vmem(replicas - 1, rows_ff, LANES),
            vmem(replicas - 1, 4 * rows_attn, LANES),
            vmem(replicas, rows_ff, LANES),
            vmem(2, 2, length, width),
            vmem32(rows_ff, LANES),
            vmem32(rows_attn, LANES),
            vmem(3 * rows_attn, LANES),
            vmem(3, rows_attn, LANES),
            vmem(rows_ff, LANES),
            vmem(rows_ff, LANES),
            vmem(rows, LANES),
            vmem32(12, width),
            vmem32(3 + replicas, 12, width),
            vmem32(2, 12, width),
            pltpu.SemaphoreType.DMA((9,)),
            pltpu.SemaphoreType.DMA((3 * replicas + 1,)),
            pltpu.SemaphoreType.DMA((count,)),
            pltpu.SemaphoreType.DMA((count,)),
        ],
        compiler_params=pltpu.CompilerParams(
            vmem_limit_bytes=63 << 20, collective_id=2, has_side_effects=True
        ),
        cost_estimate=pl.CostEstimate(
            flops=60 * 10**9, bytes_accessed=40 << 20, transcendentals=0
        ),
        name="middle",
    )(vectors, hidden_bias, tables, hats, cots, own_attn, attn_parts, own_ff, send_ff)


def split(value):
    high = value.astype(BF16)
    return high, (value - high.astype(F32)).astype(BF16)


def soap_kernel(slots, replicas, per_step, *refs):
    refs = list(refs)
    take = lambda number: [refs.pop(0) for _ in range(number)]
    place_ref, owner_ref, slab = take(3)
    left_ref, right_ref, first_ref, second_ref, master_ref, ema_ref = take(6)
    grad_ref, first_out, second_out, master_out, copy_out, ema_out = take(6)
    mine, inverse, sem = take(3)
    me, column = place_ref[0], place_ref[1]
    step = pl.program_id(0)
    bias_fix = 1.0 - 0.5**STEP
    rows_ff = 64 * TILE // replicas
    rows_attn = 16 * TILE // replicas
    rows_all = slots * TILE
    size = min(TILE, rows_attn)

    @pl.when(step == 0)
    def _():
        def note(unit, carry):
            inverse[owner_ref[unit]] = unit
            return carry

        lax.fori_loop(0, owner_ref.shape[0], note, 0)

        def fetch(number, carry):
            unit = inverse[me * slots + number]
            row, col = (unit % 64) // 8, unit % 8
            by_rows = column == 3
            rank = jnp.where(by_rows, row // 2, col // 2)
            attn_place = jnp.where(by_rows, (row % 2) * 8 + col, row * 2 + col % 2)
            up_place = row * 4 + col % 4
            down_place = 32 + (row % 4) * 8 + col
            is_attn, is_up = unit < 64, unit < 128
            core = jnp.where(is_attn, rank % 2, jnp.where(is_up, col // 4, row // 4))
            other = ((rank // 2) != (column % 2)).astype(jnp.int32)
            for piece in range(TILE // size):
                attn_row = attn_place * TILE + piece * size
                ff_row = jnp.where(is_up, up_place, down_place) * TILE + piece * size
                holder = jnp.where(is_attn, attn_row // rows_attn, ff_row // rows_ff)
                inner = jnp.where(
                    is_attn, rows_ff + other * rows_attn + attn_row % rows_attn, ff_row % rows_ff
                )
                start = ((holder * 2 + core) ^ me) * rows_all + inner
                pltpu.make_async_copy(
                    slab.at[pl.ds(pl.multiple_of(start, size), size), :],
                    mine.at[number, pl.ds(piece * size, size), :],
                    sem,
                ).start()
            return carry

        lax.fori_loop(0, slots, fetch, 0)
        pltpu.make_async_copy(mine, mine, sem).wait()

    every = range(per_step)
    grads = [mine[step * per_step + number] for number in every]
    left = [split(left_ref[number]) for number in every]
    right = [split(right_ref[number]) for number in every]
    twice = lambda value, axis: jnp.concatenate([value, value], axis=axis)
    both = lambda pair, axis: jnp.concatenate(pair, axis=axis)
    turned = [dot_tn(both(left[n], 0), twice(grads[n], 0)) for n in every]
    parts = [split(turned[n]) for n in every]
    turned = [
        dot_nn(parts[n][0], right[n][1]) + dot_nn(both(parts[n], 1), twice(right[n][0], 0))
        for n in every
    ]
    scaled = []
    for n in every:
        grad_ref[n] = grads[n].astype(F32)
        first = 0.5 * first_ref[n] + 0.5 * turned[n]
        second = 0.5 * second_ref[n] + 0.5 * turned[n] * turned[n]
        first_out[n] = first
        second_out[n] = second
        scaled.append(first / bias_fix / (jnp.sqrt(second / bias_fix) + eps_adam))
    parts = [split(scaled[n]) for n in every]
    back = [
        dot_nn(left[n][0], parts[n][1]) + dot_nn(both(left[n], 1), twice(parts[n][0], 0))
        for n in every
    ]
    parts = [split(back[n]) for n in every]
    back = [
        dot_nt(parts[n][0], right[n][1]) + dot_nt(both(parts[n], 1), twice(right[n][0], 1))
        for n in every
    ]
    for n in every:
        master = master_ref[n] - lr_matrix * back[n]
        master_out[n] = master
        copy_out[n] = master.astype(BF16)
        ema_out[n] = ema_keep * ema_ref[n] + (1.0 - ema_keep) * master


def soap(place, owner_row, slab, state, replicas):
    slots = state[0].shape[0]
    per_step = 4 if slots % 4 == 0 else 1
    spec = pl.BlockSpec((per_step, TILE, TILE), lambda i: (i, 0, 0))
    shape = (slots, TILE, TILE)
    return pl.pallas_call(
        functools.partial(soap_kernel, slots, replicas, per_step),
        grid=(slots // per_step,),
        out_shape=[jax.ShapeDtypeStruct(shape, F32)] * 4
        + [jax.ShapeDtypeStruct(shape, BF16), jax.ShapeDtypeStruct(shape, F32)],
        in_specs=[SMEM, SMEM, ANY] + [spec] * 6,
        out_specs=[spec] * 6,
        scratch_shapes=[
            pltpu.VMEM(shape, BF16),
            pltpu.SMEM((owner_row.shape[0],), jnp.int32),
            pltpu.SemaphoreType.DMA,
        ],
        compiler_params=pltpu.CompilerParams(vmem_limit_bytes=60 << 20),
        cost_estimate=pl.CostEstimate(
            flops=24 * slots * 2 * TILE**3, bytes_accessed=20 << 20, transcendentals=0
        ),
        name="soap",
    )(place, owner_row, slab, *state)


def finish_kernel(tokens, cot, mine, across, bias, result, grad_tokens):
    value = tokens[...]
    out = mine[0].astype(F32) + across[0].astype(F32)
    result[...] = value + (out + (bias[7:8, :] + bias[8:9, :]))
    value = value - jnp.mean(value, axis=-1, keepdims=True)
    inverse = lax.rsqrt(jnp.mean(value * value, axis=-1, keepdims=True) + eps_norm)
    hat = value * inverse
    grad = mine[1].astype(F32) + across[1].astype(F32)
    grad_tokens[...] = cot[...] + inverse * (
        grad
        - jnp.mean(grad, axis=-1, keepdims=True)
        - hat * jnp.mean(grad * hat, axis=-1, keepdims=True)
    )


def finish(tokens, cot, mine, across, vectors):
    length, width = tokens.shape
    rows = 128
    one = pl.BlockSpec((rows, width), lambda i: (i, 0))
    two = pl.BlockSpec((2, rows, width), lambda i: (0, i, 0))
    whole = pl.BlockSpec(vectors.shape, lambda i: (0, 0))
    return pl.pallas_call(
        finish_kernel,
        grid=(length // rows,),
        out_shape=[jax.ShapeDtypeStruct((length, width), F32)] * 2,
        in_specs=[one, one, two, two, whole],
        out_specs=[one, one],
        compiler_params=pltpu.CompilerParams(vmem_limit_bytes=60 << 20),
        cost_estimate=pl.CostEstimate(flops=0, bytes_accessed=12 << 20, transcendentals=0),
        name="finish",
    )(tokens, cot, mine, across, vectors)


def adam_step(grad, first, second, param):
    bias_fix = 1.0 - 0.5**STEP
    first_new = 0.5 * first + 0.5 * grad
    second_new = 0.5 * second + 0.5 * grad * grad
    return (
        first_new,
        second_new,
        param - lr_vector * (first_new / bias_fix) / (jnp.sqrt(second_new / bias_fix) + eps_adam),
    )


def local(
    tokens,
    cotangent,
    positions,
    owners,
    masters,
    basis_left,
    basis_right,
    moment1,
    moment2,
    ema,
    vectors,
    vector_moment1,
    vector_moment2,
    hidden_bias,
    hidden_moment1,
    hidden_moment2,
):
    length, width = tokens.shape
    slots = masters.shape[1]
    me = lax.axis_index("dp")
    column = lax.axis_index("mlp")
    replicas = lax.axis_size("dp") // 2
    place = jnp.stack([me, column, me // 2]).astype(jnp.int32)
    owner_row = owners[0]

    inverse_freq = 10000.0 ** (-(jnp.arange(ROT // 2, dtype=F32) * 2.0) / ROT)
    angles = inverse_freq[:, None] * positions.astype(F32)[None, :]
    table = jnp.concatenate([jnp.cos(angles), jnp.sin(angles)], axis=0)
    hats, cots, tables, attn_parts, own_attn, own_ff, send_ff = front(
        tokens, cotangent, table, masters[0], (owner_row // slots ^ me) * slots + owner_row % slots
    )

    mine, across, slab, reduced = middle(
        vectors,
        hidden_bias.reshape(2 * GROUP, -1),
        tables,
        hats,
        cots,
        own_attn,
        attn_parts,
        own_ff,
        send_ff,
        slots,
    )
    state = [item[0] for item in (basis_left, basis_right, moment1, moment2, masters, ema)]
    own_grad, first_new, second_new, master_new, weight_copy, ema_new = soap(
        place, owner_row, slab, state, replicas
    )
    result, grad_tokens = finish(tokens, cotangent, mine, across, vectors)
    vector_grad = jnp.concatenate([reduced[:8], reduced[7:8]], axis=0)
    hidden_grad = reduced[8:].reshape(FF)
    vec_first, vec_second, vectors_new = adam_step(
        vector_grad, vector_moment1, vector_moment2, vectors
    )
    hid_first, hid_second, hidden_new = adam_step(
        hidden_grad, hidden_moment1, hidden_moment2, hidden_bias
    )
    return (
        result,
        grad_tokens,
        own_grad[None],
        first_new[None],
        second_new[None],
        master_new[None],
        weight_copy[None],
        ema_new[None],
        vector_grad,
        vec_first,
        vec_second,
        vectors_new,
        hidden_grad,
        hid_first,
        hid_second,
        hidden_new,
    )


def solution(mesh):
    split = P(("dp", "mlp"), None)
    tiled = P("mlp", "dp", None, None)
    return jax.shard_map(
        local,
        mesh=mesh,
        in_specs=(split, split, P(("dp", "mlp")), P("mlp", None)) + (tiled,) * 6 + (P(),) * 6,
        out_specs=(split, split) + (tiled,) * 6 + (P(),) * 8,
        check_vma=False,
    )
```

```python
import functools

import jax
import jax.numpy as jnp
from jax import lax
from jax.experimental import pallas as pl
from jax.experimental.pallas import tpu as pltpu
from jax.sharding import PartitionSpec as P

HEADS = 16
HDIM = 64
ROT = 16
FF = 4096
STEP = 5
TILE = 128
LANES = 128
GROUP = 4

PRECISE = lax.Precision.HIGHEST
eps_norm = 1e-05
eps_adam = 1e-08
lr_matrix = 0.05
lr_vector = 0.5
ema_keep = 0.8

F32 = jnp.float32
BF16 = jnp.bfloat16
ANY = pl.BlockSpec(memory_space=pl.ANY)
VMEM = pl.BlockSpec(memory_space=pltpu.VMEM)
SMEM = pl.BlockSpec(memory_space=pltpu.SMEM)


def dot_nn(left, right):
    return jnp.dot(left, right, preferred_element_type=F32)


def dot_nt(left, right):
    return lax.dot_general(left, right, (((1,), (1,)), ((), ())), preferred_element_type=F32)


def dot_tn(left, right):
    return lax.dot_general(left, right, (((0,), (0,)), ((), ())), preferred_element_type=F32)


def precise(left, right, left_dim, right_dim):
    return lax.dot_general(
        left,
        right,
        (((left_dim,), (right_dim,)), ((), ())),
        precision=PRECISE,
        preferred_element_type=F32,
    )


MESH = pl.DeviceIdType.MESH


def flip(index, mask):
    bit = 1
    while bit <= mask:
        if mask & bit:
            index = index + bit - 2 * bit * ((index // bit) % 2)
        bit *= 2
    return index


def differ(left, right, count):
    total, bit = 0, 1
    while bit < count:
        one, two = (left // bit) % 2, (right // bit) % 2
        total = total + bit * (one + two - 2 * one * two)
        bit *= 2
    return total


class Links:
    def __init__(self, send_sems, recv_sems):
        self.send_sems, self.recv_sems = send_sems, recv_sems
        self.number = 0
        self.all = []

    def send(self, source, target, device):
        copy = pltpu.make_async_remote_copy(
            src_ref=source,
            dst_ref=target,
            send_sem=self.send_sems.at[self.number],
            recv_sem=self.recv_sems.at[self.number],
            device_id=device,
            device_id_type=MESH,
        )
        self.number += 1
        copy.start()
        entry = [copy, False, False]
        self.all.append(entry)
        return entry

    def arrived(self, entry):
        if not entry[1]:
            entry[0].wait_recv()
            entry[1] = True

    def left(self, entry):
        if not entry[2]:
            entry[0].wait_send()
            entry[2] = True

    def finish(self):
        for entry in self.all:
            self.arrived(entry)
            self.left(entry)


def greet(me, column, masks_dp, masks_z):
    barrier = pltpu.get_barrier_semaphore()
    for mask in masks_dp:
        pl.semaphore_signal(barrier, inc=1, device_id={"dp": flip(me, mask)}, device_id_type=MESH)
    for mask in masks_z:
        pl.semaphore_signal(
            barrier, inc=1, device_id={"mlp": flip(column, mask)}, device_id_type=MESH
        )
    pl.semaphore_wait(barrier, len(masks_dp) + len(masks_z))


class Spread:
    def __init__(self, links, slab, me, count, rows, first, size, backward, pairs=True):
        self.links, self.slab, self.me, self.pairs = links, slab, me, pairs
        self.rows, self.first, self.size = rows, first, size
        self.bits = [1 << i for i in range(1, count.bit_length() - 1)]
        if backward:
            self.bits = self.bits[::-1]
        self.came = {}
        self.order = []

    def part(self, at):
        place = at if self.pairs else at // 2
        return self.slab.at[pl.ds(place * self.rows + self.first, self.size)]

    def forward(self, at, step, source=None):
        source = self.part(at) if source is None else source
        for later in range(step, len(self.bits)):
            bit = self.bits[later]
            entry = self.links.send(source, self.part(at ^ bit), {"dp": flip(self.me, bit)})
            self.came[at ^ bit] = (entry, later + 1)
            self.order.append(at ^ bit)
        if self.pairs:
            self.links.send(source, self.part(at ^ 1), {"dp": flip(self.me, 1)})

    def relay(self):
        while self.order:
            at = min(self.order, key=lambda index: (self.came[index][1], index.bit_count()))
            self.order.remove(at)
            entry, step = self.came[at]
            self.links.arrived(entry)
            self.forward(at, step)


def attn_unit(column, rank, place):
    by_columns = (place // 2) * 8 + 2 * rank + place % 2
    by_rows = (2 * rank + place // 8) * 8 + place % 8
    return jnp.where(column == 3, by_rows, by_columns)


def ff_unit(core, place):
    later = place - 32
    up = 64 + (place // 4) * 8 + core * 4 + place % 4
    down = 128 + (core * 4 + later // 8) * 8 + later % 8
    return jnp.where(place < 32, up, down)


def erf_f32(value):
    value = jnp.clip(value, -3.832506856900711, 3.832506856900711)
    square = value * value
    top = jnp.full_like(square, 0.00022905065861350646)
    for coeff in (
        0.0034082910107109506,
        0.050955695062380861,
        0.18520832239976145,
        1.128379143519084,
    ):
        top = top * square + coeff
    low = jnp.full_like(square, -1.1791602954361697e-7)
    for coeff in (
        0.000023547966471313185,
        0.0010179625278914885,
        0.014070470171167667,
        0.11098505178285362,
        0.49746925110067538,
        1.0,
    ):
        low = low * square + coeff
    return value * top / low


def row_sum(value):
    return dot_nn(jnp.ones((16, value.shape[0]), BF16), value)[0:1, :]


def transpose_tile(value):
    return jnp.swapaxes(value, 0, 1)


def layer_kernel(slots, devices, *refs):
    refs = list(refs)
    take = lambda number: [refs.pop(0) for _ in range(number)]
    norm_ref, hidden_ref, table, tokens, cot_ref, masters, tile_ref = take(7)
    mine, across, slab, attn_parts, z_ff, reduced = take(6)
    weights, table_ref, own_attn, send_attn, send_ff = take(5)
    h_all, c_all, out_acc, back_acc = take(4)
    tiles, weight_a, weight_b, acc_a, acc_b = take(5)
    q_all, k_all, v_all, g_all, o_all, dq_all, dk_all, dv_all = take(8)
    dw, own_land, attn_land, core_land = take(4)
    own_sum, attn_keep, attn_send, attn_back, z_send, z_land, block_all = take(7)
    vec, vec_land, vec_sum = take(3)
    local_sems, tile_sems, slot_sems, send_sems, recv_sems = take(5)
    me, column = lax.axis_index("dp"), lax.axis_index("mlp")
    replicas = devices // 2
    core, quarter = me % 2, me // 2
    rank = 2 * (column % 2) + core
    length, width = h_all.shape[1:]
    hidden = 4 * TILE
    wide = 4 * HDIM
    up, up_acc = weight_a.at[:, 0:hidden], acc_a.at[:, 0:hidden]
    down, down_acc = weight_b, acc_b
    w_in, in_acc = weight_a, acc_a
    w_out, proj_acc = weight_b.at[0:wide, :], acc_b.at[0:wide, :]
    rows_ff, rows_attn = 64 * TILE // replicas, 16 * TILE // replicas
    links = Links(send_sems, recv_sems)
    greet(me, column, [1] + [at << 1 for at in range(1, replicas)], [1, 2, 3])

    stage = [pltpu.make_async_copy(tokens, acc_b, local_sems.at[8])]
    places = []
    for slot in range(slots):
        place = acc_a.at[pl.ds(slot // 6 * TILE, TILE), pl.ds(slot % 6 * TILE, TILE)]
        places.append(place)
        stage.append(pltpu.make_async_copy(masters.at[slot], place, slot_sems.at[slot]))
    for copy in stage[1:] + stage[:1]:
        copy.start()
    for slot in range(slots):
        stage[1 + slot].wait()
        weights[slot] = places[slot][...].astype(BF16)
    cut = slots // 2
    spreads = [
        Spread(links, weights, me, devices, slots, 0, cut, False),
        Spread(links, weights, me, devices, slots, cut, slots - cut, True),
    ]
    for spread in spreads:
        spread.forward(0, 0)
    gathered = list(links.all)

    def normalize(step, carry):
        where = pl.ds(pl.multiple_of(step * TILE, TILE), TILE)
        value = acc_b[where, :]
        value = value - jnp.mean(value, axis=-1, keepdims=True)
        value = value * lax.rsqrt(jnp.mean(value * value, axis=-1, keepdims=True) + eps_norm)
        h_all[0, where, :] = value.astype(BF16)
        return carry

    stage[0].wait()
    lax.fori_loop(0, length // TILE, normalize, 0)
    copy = pltpu.make_async_copy(cot_ref, acc_b, local_sems.at[7])
    copy.start()
    along = []

    def send_along(target, where):
        entry = links.send(
            target.at[0, where, :], target.at[2, where, :], {"mlp": flip(column, 1)}
        )
        along.append((target, where, entry))

    table_ref[0] = table[...]
    early = length * 5 // 8
    send_along(h_all, pl.ds(0, length))
    send_along(table_ref, pl.ds(0, ROT))
    copy.wait()
    c_all[0] = acc_b[...].astype(BF16)
    send_along(c_all, pl.ds(0, early))
    core_blocks = [
        links.send(target.at[0], target.at[1], {"dp": flip(me, 1)})
        for target in (h_all, table_ref, c_all)
    ]
    number = len(links.all)
    for spread in spreads:
        spread.relay()
    gathered += links.all[number:]
    for entry in gathered:
        links.arrived(entry)

    def fill(out_ref, base, rows_out, first_row, unit_of):
        size = min(TILE, rows_out)

        def body(step, carry):
            row = first_row + step * size
            tile = tile_ref[unit_of(row // TILE)]
            where = pl.ds(pl.multiple_of(base + step * size, size), size)
            if size == TILE:
                out_ref[where, :] = weights[tile]
            else:
                out_ref[where, :] = weights[tile, pl.ds(pl.multiple_of(row % TILE, size), size), :]
            return carry

        lax.fori_loop(0, rows_out // size, body, 0)

    low = column % 2
    attn_came_z = []
    for bit in (3, 2, 1):
        fill(
            send_attn,
            (bit - 1) * rows_attn,
            rows_attn,
            quarter * rows_attn,
            functools.partial(attn_unit, column, 2 * (flip(low, 1) if bit & 1 else low) + core),
        )
        piece = pl.ds((bit - 1) * rows_attn, rows_attn)
        attn_came_z.append(
            links.send(
                send_attn.at[piece, :], attn_parts.at[piece, :], {"mlp": flip(column, bit)}
            )
        )
    send_along(c_all, pl.ds(early, length - early))
    fill(send_ff, 0, rows_ff, quarter * rows_ff, functools.partial(ff_unit, core))
    came_ff = [links.send(send_ff, z_ff.at[0], {"mlp": flip(column, 2)})]
    fill(tiles, 0, 64 * TILE, 0, functools.partial(ff_unit, core))
    fill(own_attn, 0, 16 * TILE, 0, functools.partial(attn_unit, column, rank))
    vec[...] = jnp.zeros_like(vec)

    def set_ff_weights():
        for at in range(32):
            up[
                (at // 4) * TILE : (at // 4 + 1) * TILE, (at % 4) * TILE : (at % 4 + 1) * TILE
            ] = tiles[at * TILE : (at + 1) * TILE, :]
            down[
                (at // 8) * TILE : (at // 8 + 1) * TILE, (at % 8) * TILE : (at % 8 + 1) * TILE
            ] = tiles[(32 + at) * TILE : (33 + at) * TILE, :]
        up_acc[...] = jnp.zeros((width, hidden), F32)
        down_acc[...] = jnp.zeros((hidden, width), F32)

    def ff_block(at, ff_column, first, store):
        hat = h_all[at].astype(F32)
        normed = (hat * norm_ref[2:3, :] + norm_ref[3:4, :]).astype(BF16)
        cot = c_all[at]
        pre = dot_nn(normed, up[...]) + hidden_ref[pl.ds(2 * ff_column + core, 1), :]
        cdf = 0.5 + 0.5 * erf_f32(pre * 0.7071067811865476)
        act = (pre * cdf).astype(BF16)
        grad = dot_nt(cot, down[...])
        grad = grad * (cdf + pre * (jnp.exp(-0.5 * pre * pre) * 0.3989422804014327))
        grad = grad.astype(BF16)
        where = pl.ds(pl.multiple_of(core * hidden, hidden), hidden)
        vec[pl.ds(8 + ff_column, 1), where] += row_sum(grad)
        out = dot_nn(act, down[...])
        back = dot_nt(grad, up[...])
        vec[2:3, :] += jnp.sum(back * hat, axis=0, keepdims=True)
        vec[3:4, :] += jnp.sum(back, axis=0, keepdims=True)
        back = back * norm_ref[2:3, :]
        if not first:
            out = out + out_acc[at].astype(F32)
            back = back + back_acc[at].astype(F32)
        store(out, back)
        up_acc[...] += dot_tn(normed, grad)
        down_acc[...] += dot_tn(act, cot)

    def store_ff(target):
        per = rows_ff // TILE
        for at in range(64):
            if at < 32:
                tile = up_acc[
                    (at // 4) * TILE : (at // 4 + 1) * TILE, (at % 4) * TILE : (at % 4 + 1) * TILE
                ]
            else:
                low = at - 32
                tile = down_acc[
                    (low // 8) * TILE : (low // 8 + 1) * TILE,
                    (low % 8) * TILE : (low % 8 + 1) * TILE,
                ]
            target[
                differ(at // per, quarter, replicas), (at % per) * TILE : (at % per + 1) * TILE, :
            ] = tile.astype(BF16)

    def attn_rows(matrix):
        return pl.multiple_of(matrix * (16 * TILE), TILE)

    def attn_rows(matrix):
        return pl.multiple_of(matrix * (16 * TILE), TILE)

    set_ff_weights()
    vec[7:8, :] = row_sum(c_all[0])

    def own_block(at):
        def store(out, back):
            out_acc[at] = out.astype(BF16)
            back_acc[at] = back.astype(BF16)

        ff_block(at, column, True, store)

    own_block(0)
    spreads = []
    for number, entry in enumerate(attn_came_z[::-1]):
        links.arrived(entry)
        pieces = [(number * rows_attn, rows_attn, number == 1)]
        if number == 2:
            cut = rows_attn // 32 * 16
            pieces = [
                (2 * rows_attn, cut, False),
                (2 * rows_attn + cut, rows_attn - cut, True),
            ]
        for first, size, backward in pieces:
            spreads.append(
                Spread(links, attn_parts, me, devices, 3 * rows_attn, first, size, backward, False)
            )
            spreads[-1].forward(0, 0)
    for entry in core_blocks:
        links.arrived(entry)
    own_block(1)
    for target, where, entry in along:
        links.arrived(entry)
        core_blocks.append(
            links.send(target.at[2, where, :], target.at[3, where, :], {"dp": flip(me, 1)})
        )
    for spread in spreads:
        spread.relay()
    gathered = links.all[:]
    own_block(2)
    for entry in core_blocks:
        links.arrived(entry)
    own_block(3)
    store_ff(dw)
    own_sum[...] = dw[0].astype(F32)
    own_came = [
        links.send(dw.at[at], own_land.at[at - 1], {"dp": flip(me, at << 1)})
        for at in range(1, replicas)
    ]
    links.arrived(came_ff[0])
    for at in range(1, replicas):
        came_ff.append(links.send(z_ff.at[0], z_ff.at[at], {"dp": flip(me, at << 1)}))

    for entry in gathered:
        links.arrived(entry)
    tile_loads = [
        pltpu.make_async_copy(
            own_attn, tiles.at[pl.ds(attn_rows(column), 16 * TILE), :], tile_sems.at[0]
        )
    ]
    for at in range(replicas):
        for bit in (1, 2, 3):
            first = attn_rows(flip(column, bit)) + differ(at, quarter, replicas) * rows_attn
            tile_loads.append(
                pltpu.make_async_copy(
                    attn_parts.at[pl.ds((3 * at + bit - 1) * rows_attn, rows_attn), :],
                    tiles.at[pl.ds(pl.multiple_of(first, rows_attn), rows_attn), :],
                    tile_sems.at[len(tile_loads)],
                )
            )
    for copy in tile_loads:
        copy.start()
    for copy in tile_loads:
        copy.wait()
    for matrix in range(3):
        for at in range(16):
            row = (16 * matrix + at) * TILE
            w_in[
                (at // 2) * TILE : (at // 2 + 1) * TILE,
                (2 * matrix + at % 2) * TILE : (2 * matrix + at % 2 + 1) * TILE,
            ] = tiles[row : row + TILE, :]
    for at in range(16):
        w_out[(at // 8) * TILE : (at // 8 + 1) * TILE, (at % 8) * TILE : (at % 8 + 1) * TILE] = (
            tiles[(48 + at) * TILE : (49 + at) * TILE, :]
        )
    in_acc[...] = jnp.zeros((width, 3 * wide), F32)
    proj_acc[...] = jnp.zeros((wide, width), F32)
    half = ROT // 2
    block = BLOCK
    scale = HDIM ** (-0.5)
    lane = lax.broadcasted_iota(jnp.int32, (1, LANES), 1)
    within = lane % HDIM
    keep_low = lane < HDIM
    wave = lax.broadcasted_iota(jnp.int32, (ROT, LANES), 0)
    spot = lax.broadcasted_iota(jnp.int32, (ROT, LANES), 1) % HDIM
    pick_cos = ((spot < ROT) & (wave == spot % half)).astype(F32)
    pick_first = ((spot < half) & (wave == half + spot)).astype(F32)
    pick_second = ((spot >= half) & (spot < ROT) & (wave == spot)).astype(F32)
    plain = (within >= ROT).astype(F32)

    def attn_block(at, carry):
        hat = h_all[at].astype(F32)
        normed = (hat * norm_ref[0:1, :] + norm_ref[1:2, :]).astype(BF16)
        cot = c_all[at]
        table = table_ref[at]
        cos_w = precise(table, pick_cos, 0, 0) + plain
        sin_a = precise(table, pick_first, 0, 0)
        sin_b = precise(table, pick_second, 0, 0)
        proj = dot_nn(normed, w_in[...])
        g_all[...] = dot_nt(cot, w_out[...]).astype(BF16)

        def turn(value):
            return (
                value * cos_w
                - pltpu.roll(value, LANES - half, 1) * sin_a
                + pltpu.roll(value, half, 1) * sin_b
            )

        for pair in range(2):
            cols = slice(pair * LANES, (pair + 1) * LANES)
            where = pl.ds(pl.multiple_of(rank * wide + pair * LANES, LANES), LANES)
            query = proj[:, pair * LANES : (pair + 1) * LANES] + norm_ref[4:5, where]
            key = proj[:, wide + pair * LANES : wide + (pair + 1) * LANES] + norm_ref[5:6, where]
            value = proj[:, 2 * wide + pair * LANES : 2 * wide + (pair + 1) * LANES]
            q_all[:, cols] = (turn(query).astype(BF16) * scale).astype(BF16)
            k_all[:, cols] = turn(key).astype(BF16)
            v_all[:, cols] = (value + norm_ref[6:7, where]).astype(BF16)
        zero = jnp.zeros((), BF16)
        for pair in range(2):
            cols = slice(pair * LANES, (pair + 1) * LANES)
            query, key = q_all[:, cols], k_all[:, cols]
            value, grad = v_all[:, cols], g_all[:, cols]
            key_t, value_t = transpose_tile(key), transpose_tile(value)
            out_t, dq_t = [], []
            dk_all[:, cols] = jnp.zeros((length, LANES), F32)
            dv_all[:, cols] = jnp.zeros((length, LANES), F32)
            for head in range(2):
                mask = keep_low if head == 0 else jnp.logical_not(keep_low)
                key_m, value_m = jnp.where(mask, key, zero), jnp.where(mask, value, zero)
                query_m, grad_m = jnp.where(mask, query, zero), jnp.where(mask, grad, zero)
                part = slice(head * HDIM, (head + 1) * HDIM)
                out_row, dq_row = [], []
                for first in range(0, length, block):
                    last = first + block
                    scores = dot_nt(key_m[:last], query[first:last])
                    key_at = lax.broadcasted_iota(jnp.int32, scores.shape, 0)
                    query_at = first + lax.broadcasted_iota(jnp.int32, scores.shape, 1)
                    scores = jnp.where(key_at <= query_at, scores, -1e30)
                    peak = jnp.max(scores, axis=0, keepdims=True)
                    raised = jnp.exp(scores - peak)
                    prob = raised * (1.0 / jnp.sum(raised, axis=0, keepdims=True))
                    prob_low = prob.astype(BF16)
                    grad_prob = dot_nt(value_m[:last], grad[first:last])
                    delta = jnp.sum(prob * grad_prob, axis=0, keepdims=True)
                    grad_scores = (prob * (grad_prob - delta)).astype(BF16)
                    out_row.append(dot_nn(value_t[part, :last], prob_low))
                    dq_row.append(dot_nn(key_t[part, :last], grad_scores))
                    dv_all[:last, cols] += dot_nn(prob_low, grad_m[first:last])
                    dk_all[:last, cols] += dot_nn(grad_scores, query_m[first:last])
                out_t.append(jnp.concatenate(out_row, axis=1))
                dq_t.append(jnp.concatenate(dq_row, axis=1))
            o_all[:, cols] = transpose_tile(jnp.concatenate(out_t, axis=0)).astype(BF16)
            dq_all[:, cols] = transpose_tile(jnp.concatenate(dq_t, axis=0)) * scale

        def turn_back(value):
            return (
                value * cos_w
                + pltpu.roll(value, LANES - half, 1) * sin_a
                - pltpu.roll(value, half, 1) * sin_b
            ).astype(BF16)

        pieces = [turn_back(dq_all[:, 0:LANES]), turn_back(dq_all[:, LANES : 2 * LANES])]
        pieces += [turn_back(dk_all[:, 0:LANES]), turn_back(dk_all[:, LANES : 2 * LANES])]
        pieces += [dv_all[...].astype(BF16)]
        grads = jnp.concatenate(pieces, axis=1)
        sums = row_sum(grads)
        where = pl.ds(pl.multiple_of(rank * wide, LANES), wide)
        for matrix in range(3):
            vec[4 + matrix : 5 + matrix, where] += sums[:, matrix * wide : (matrix + 1) * wide]
        out = dot_nn(o_all[...], w_out[...])
        out_acc[at] = (out_acc[at].astype(F32) + out).astype(BF16)
        back = dot_nt(grads, w_in[...])
        vec[0:1, :] += jnp.sum(back * hat, axis=0, keepdims=True)
        vec[1:2, :] += jnp.sum(back, axis=0, keepdims=True)
        back_acc[at] = (back_acc[at].astype(F32) + back * norm_ref[0:1, :]).astype(BF16)
        in_acc[...] += dot_tn(normed, grads)
        proj_acc[...] += dot_tn(o_all[...], cot)
        return carry

    lax.fori_loop(0, 4, attn_block, 0)
    for entry in own_came:
        links.arrived(entry)
        links.left(entry)
    for at in range(1, replicas):
        own_sum[...] += own_land[at - 1].astype(F32)
    size = min(TILE, rows_attn)
    for matrix in range(4):
        for at in range(16):
            for piece in range(TILE // size):
                row = at * TILE + piece * size
                if matrix < 3:
                    top, left = (at // 2) * TILE, (2 * matrix + at % 2) * TILE
                    tile = in_acc[top + piece * size : top + (piece + 1) * size, left : left + TILE]
                else:
                    top, left = (at // 8) * TILE, (at % 8) * TILE
                    tile = proj_acc[
                        top + piece * size : top + (piece + 1) * size, left : left + TILE
                    ]
                inner = row % rows_attn
                dw[
                    differ(row // rows_attn, quarter, replicas),
                    pl.ds(
                        pl.multiple_of(flip(column, matrix) * rows_attn + inner, size), size
                    ),
                    :,
                ] = tile.astype(BF16)
    attn_came = [
        links.send(dw.at[at], attn_land.at[at - 1], {"dp": flip(me, at << 1)})
        for at in range(1, replicas)
    ]
    attn_keep[...] = dw[0, 0:rows_attn, :].astype(F32)
    attn_send[...] = dw[0, rows_attn : 4 * rows_attn, :]

    other = flip(column, 2)
    for entry in came_ff:
        links.arrived(entry)
    tile_loads = []
    for at in range(replicas):
        first = pl.multiple_of(differ(at, quarter, replicas) * rows_ff, TILE)
        tile_loads.append(
            pltpu.make_async_copy(
                z_ff.at[at], tiles.at[pl.ds(first, rows_ff), :], tile_sems.at[at]
            )
        )
    for copy in tile_loads:
        copy.start()
    for copy in tile_loads:
        copy.wait()
    set_ff_weights()
    core_came = {}
    outs = []
    waiting = []

    def pump(count):
        for number, source, where in waiting[:count]:
            links.send(
                source.at[2, where, :], across.at[number, where, :], {"mlp": flip(column, 1)}
            )
        del waiting[:count]

    def send_core(at):
        def store(out, back):
            out_acc[at] = out.astype(BF16)
            back_acc[at] = back.astype(BF16)
            for number, source in ((0, out_acc), (1, back_acc)):
                core_came[number, at // 2] = links.send(
                    source.at[at], core_land.at[number, at // 2], {"dp": flip(me, 1)}
                )

        return store

    def keep(at):
        def store(out, back):
            for number, value, source in ((0, out, out_acc), (1, back, back_acc)):
                links.arrived(core_came[number, at // 2])
                value = value + core_land[number, at // 2].astype(F32)
                source[at] = value.astype(BF16)
                if at == 0:
                    copy = pltpu.make_async_copy(
                        source.at[at], mine.at[number], local_sems.at[number]
                    )
                    copy.start()
                    outs.append(copy)
                else:
                    for first in range(0, length, length // 4):
                        waiting.append((number, source, pl.ds(first, length // 4)))

        return store

    for at in (3, 2, 1, 0):
        ff_block(at, other, False, send_core(at) if at % 2 else keep(at))
        pump(1)
    for entry in attn_came:
        links.arrived(entry)
        links.left(entry)

    store_ff(dw)
    chunks = 4
    size = rows_ff // chunks
    dw_came = []
    for chunk in range(chunks):
        piece = pl.ds(chunk * size, size)
        dw_came.append(
            [
                links.send(
                    dw.at[at, piece, :], own_land.at[at - 1, piece, :], {"dp": flip(me, at << 1)}
                )
                for at in range(1, replicas)
            ]
        )
    vec_came = [
        links.send(vec, vec_land.at[bit], {"mlp": flip(column, bit)}) for bit in (1, 2, 3)
    ]
    for at in range(1, replicas):
        attn_keep[...] += attn_land[at - 1, 0:rows_attn, :].astype(F32)
    total = attn_send[...].astype(F32)
    for at in range(1, replicas):
        total = total + attn_land[at - 1, rows_attn : 4 * rows_attn, :].astype(F32)
    attn_send[...] = total.astype(BF16)
    back_came = []
    for bit in (1, 2, 3):
        piece = pl.ds((bit - 1) * rows_attn, rows_attn)
        back_came.append(
            links.send(attn_send.at[piece, :], attn_back.at[bit - 1], {"mlp": flip(column, bit)})
        )
    pump(1)
    rows = slots * TILE
    spreads = []

    def publish(first, count):
        backward = len(spreads) % 2 == 1
        spread = Spread(links, slab, me, devices, rows, first, count, backward)
        source = block_all.at[pl.ds(first, count), :]
        spread.forward(0, 0, source)
        copy = pltpu.make_async_copy(source, spread.part(0), local_sems.at[2 + len(spreads)])
        copy.start()
        outs.append(copy)
        spreads.append(spread)

    def add_chunk(chunk):
        piece = slice(chunk * size, (chunk + 1) * size)
        for entry in dw_came[chunk]:
            links.arrived(entry)
        total = dw[0, piece, :].astype(F32)
        for at in range(1, replicas):
            total = total + own_land[at - 1, piece, :].astype(F32)
        z_send[piece, :] = total.astype(BF16)
        where = pl.ds(chunk * size, size)
        return links.send(z_send.at[where, :], z_land.at[where, :], {"mlp": flip(column, 2)})

    for entry in vec_came:
        links.arrived(entry)
    vec_sum[0] = (vec[...] + vec_land[1]) + (vec_land[2] + vec_land[3])
    vec_core = links.send(vec_sum.at[0], vec_land.at[0], {"dp": flip(me, 1)})
    z_came = [add_chunk(0)]
    pump(1)
    for entry in back_came:
        links.arrived(entry)
    block_all[rows_ff : rows_ff + rows_attn, :] = (
        attn_keep[...] + attn_back[1].astype(F32)
    ).astype(BF16)
    publish(rows_ff, rows_attn)
    block_all[rows_ff + rows_attn : rows, :] = (
        attn_back[0].astype(F32) + attn_back[2].astype(F32)
    ).astype(BF16)
    publish(rows_ff + rows_attn, rows_attn)
    links.arrived(vec_core)
    vec_sum[1] = vec_sum[0] + vec_land[0]
    vec_came = [
        links.send(vec_sum.at[1], vec_land.at[3 + at], {"dp": flip(me, at << 1)})
        for at in range(1, replicas)
    ]
    for chunk in range(1, chunks):
        z_came.append(add_chunk(chunk))
        pump(1)
    for spread in spreads[:2]:
        spread.relay()
    for chunk in range(chunks):
        links.arrived(z_came[chunk])
        piece = slice(chunk * size, (chunk + 1) * size)
        block_all[piece, :] = (own_sum[piece, :] + z_land[piece, :].astype(F32)).astype(BF16)
        publish(chunk * size, size)
        pump(1)
        if chunk > 0:
            spreads[1 + chunk].relay()
    pump(len(waiting))
    spreads[1 + chunks].relay()
    for entry in vec_came:
        links.arrived(entry)
    values = [vec_sum[1]] + [vec_land[3 + at] for at in range(1, replicas)]
    while len(values) > 1:
        values = [values[i] + values[i + 1] for i in range(0, len(values), 2)]
    reduced[...] = values[0]
    for copy in outs:
        copy.wait()
    links.finish()


BLOCK = 256


def layer(vectors, hidden_bias, table, tokens, cot, masters, tile_row):
    length, width = tokens.shape
    slots = masters.shape[0]
    devices = lax.axis_size("dp")
    replicas = devices // 2
    hidden = 4 * TILE
    wide = 4 * HDIM
    rows = slots * TILE
    rows_ff, rows_attn = 64 * TILE // replicas, 16 * TILE // replicas
    count = 2 * (2 * replicas - 1) + 11 + 3 + 4 * (replicas - 1)
    count += 1 + 3 * (replicas - 1) + 4 + 8 + 4 * (replicas - 1) + 3 + 3 + 4 + 1 + replicas - 1
    count += 6 * (2 * replicas - 1)
    vmem = lambda *shape: pltpu.VMEM(shape, BF16)
    vmem32 = lambda *shape: pltpu.VMEM(shape, F32)
    return pl.pallas_call(
        functools.partial(layer_kernel, slots, devices),
        out_shape=[
            jax.ShapeDtypeStruct((2, length, width), BF16),
            jax.ShapeDtypeStruct((2, length, width), BF16),
            jax.ShapeDtypeStruct((devices * rows, LANES), BF16),
            jax.ShapeDtypeStruct((replicas * 3 * rows_attn, LANES), BF16),
            jax.ShapeDtypeStruct((replicas, rows_ff, LANES), BF16),
            jax.ShapeDtypeStruct((12, width), F32),
        ],
        in_specs=[VMEM] * 3 + [ANY] * 3 + [SMEM],
        out_specs=[ANY] * 5 + [VMEM],
        scratch_shapes=[
            vmem(devices * slots, TILE, LANES),
            vmem32(4, ROT, length),
            vmem(16 * TILE, LANES),
            vmem(3 * rows_attn, LANES),
            vmem(rows_ff, LANES),
            vmem(4, length, width),
            vmem(4, length, width),
            vmem(4, length, width),
            vmem(4, length, width),
            vmem(64 * TILE, LANES),
            vmem(width, 3 * wide),
            vmem(hidden, width),
            vmem32(width, 3 * wide),
            vmem32(hidden, width),
            vmem(length, wide),
            vmem(length, wide),
            vmem(length, wide),
            vmem(length, wide),
            vmem(length, wide),
            vmem32(length, wide),
            vmem32(length, wide),
            vmem32(length, wide),
            vmem(replicas, rows_ff, LANES),
            vmem(replicas - 1, rows_ff, LANES),
            vmem(replicas - 1, 4 * rows_attn, LANES),
            vmem(2, 2, length, width),
            vmem32(rows_ff, LANES),
            vmem32(rows_attn, LANES),
            vmem(3 * rows_attn, LANES),
            vmem(3, rows_attn, LANES),
            vmem(rows_ff, LANES),
            vmem(rows_ff, LANES),
            vmem(rows, LANES),
            vmem32(12, width),
            vmem32(3 + replicas, 12, width),
            vmem32(2, 12, width),
            pltpu.SemaphoreType.DMA((9,)),
            pltpu.SemaphoreType.DMA((3 * replicas + 1,)),
            pltpu.SemaphoreType.DMA((slots,)),
            pltpu.SemaphoreType.DMA((count,)),
            pltpu.SemaphoreType.DMA((count,)),
        ],
        compiler_params=pltpu.CompilerParams(
            vmem_limit_bytes=63 << 20, collective_id=2, has_side_effects=True
        ),
        cost_estimate=pl.CostEstimate(
            flops=60 * 10**9, bytes_accessed=40 << 20, transcendentals=0
        ),
        name="layer",
    )(vectors, hidden_bias, table, tokens, cot, masters, tile_row)


def split(value):
    high = value.astype(BF16)
    return high, (value - high.astype(F32)).astype(BF16)


def soap_kernel(slots, replicas, per_step, *refs):
    refs = list(refs)
    take = lambda number: [refs.pop(0) for _ in range(number)]
    place_ref, owner_ref, slab = take(3)
    left_ref, right_ref, first_ref, second_ref, master_ref, ema_ref = take(6)
    grad_ref, first_out, second_out, master_out, copy_out, ema_out = take(6)
    mine, inverse, sem = take(3)
    me, column = place_ref[0], place_ref[1]
    step = pl.program_id(0)
    bias_fix = 1.0 - 0.5**STEP
    rows_ff = 64 * TILE // replicas
    rows_attn = 16 * TILE // replicas
    rows_all = slots * TILE
    size = min(TILE, rows_attn)

    @pl.when(step == 0)
    def _():
        def note(unit, carry):
            inverse[owner_ref[unit]] = unit
            return carry

        lax.fori_loop(0, owner_ref.shape[0], note, 0)

        def fetch(number, carry):
            unit = inverse[me * slots + number]
            row, col = (unit % 64) // 8, unit % 8
            by_rows = column == 3
            rank = jnp.where(by_rows, row // 2, col // 2)
            attn_place = jnp.where(by_rows, (row % 2) * 8 + col, row * 2 + col % 2)
            up_place = row * 4 + col % 4
            down_place = 32 + (row % 4) * 8 + col
            is_attn, is_up = unit < 64, unit < 128
            core = jnp.where(is_attn, rank % 2, jnp.where(is_up, col // 4, row // 4))
            other = ((rank // 2) != (column % 2)).astype(jnp.int32)
            for piece in range(TILE // size):
                attn_row = attn_place * TILE + piece * size
                ff_row = jnp.where(is_up, up_place, down_place) * TILE + piece * size
                holder = jnp.where(is_attn, attn_row // rows_attn, ff_row // rows_ff)
                inner = jnp.where(
                    is_attn, rows_ff + other * rows_attn + attn_row % rows_attn, ff_row % rows_ff
                )
                start = ((holder * 2 + core) ^ me) * rows_all + inner
                pltpu.make_async_copy(
                    slab.at[pl.ds(pl.multiple_of(start, size), size), :],
                    mine.at[number, pl.ds(piece * size, size), :],
                    sem,
                ).start()
            return carry

        lax.fori_loop(0, slots, fetch, 0)
        pltpu.make_async_copy(mine, mine, sem).wait()

    every = range(per_step)
    grads = [mine[step * per_step + number] for number in every]
    left = [split(left_ref[number]) for number in every]
    right = [split(right_ref[number]) for number in every]
    twice = lambda value, axis: jnp.concatenate([value, value], axis=axis)
    both = lambda pair, axis: jnp.concatenate(pair, axis=axis)
    turned = [dot_tn(both(left[n], 0), twice(grads[n], 0)) for n in every]
    parts = [split(turned[n]) for n in every]
    turned = [
        dot_nn(parts[n][0], right[n][1]) + dot_nn(both(parts[n], 1), twice(right[n][0], 0))
        for n in every
    ]
    scaled = []
    for n in every:
        grad_ref[n] = grads[n].astype(F32)
        first = 0.5 * first_ref[n] + 0.5 * turned[n]
        second = 0.5 * second_ref[n] + 0.5 * turned[n] * turned[n]
        first_out[n] = first
        second_out[n] = second
        scaled.append(first / bias_fix / (jnp.sqrt(second / bias_fix) + eps_adam))
    parts = [split(scaled[n]) for n in every]
    back = [
        dot_nn(left[n][0], parts[n][1]) + dot_nn(both(left[n], 1), twice(parts[n][0], 0))
        for n in every
    ]
    parts = [split(back[n]) for n in every]
    back = [
        dot_nt(parts[n][0], right[n][1]) + dot_nt(both(parts[n], 1), twice(right[n][0], 1))
        for n in every
    ]
    for n in every:
        master = master_ref[n] - lr_matrix * back[n]
        master_out[n] = master
        copy_out[n] = master.astype(BF16)
        ema_out[n] = ema_keep * ema_ref[n] + (1.0 - ema_keep) * master


def soap(place, owner_row, slab, state, replicas):
    slots = state[0].shape[0]
    per_step = 4 if slots % 4 == 0 else 1
    spec = pl.BlockSpec((per_step, TILE, TILE), lambda i: (i, 0, 0))
    shape = (slots, TILE, TILE)
    return pl.pallas_call(
        functools.partial(soap_kernel, slots, replicas, per_step),
        grid=(slots // per_step,),
        out_shape=[jax.ShapeDtypeStruct(shape, F32)] * 4
        + [jax.ShapeDtypeStruct(shape, BF16), jax.ShapeDtypeStruct(shape, F32)],
        in_specs=[SMEM, SMEM, ANY] + [spec] * 6,
        out_specs=[spec] * 6,
        scratch_shapes=[
            pltpu.VMEM(shape, BF16),
            pltpu.SMEM((owner_row.shape[0],), jnp.int32),
            pltpu.SemaphoreType.DMA,
        ],
        compiler_params=pltpu.CompilerParams(vmem_limit_bytes=60 << 20),
        cost_estimate=pl.CostEstimate(
            flops=24 * slots * 2 * TILE**3, bytes_accessed=20 << 20, transcendentals=0
        ),
        name="soap",
    )(place, owner_row, slab, *state)


def finish_kernel(tokens, cot, mine, across, bias, result, grad_tokens):
    value = tokens[...]
    out = mine[0].astype(F32) + across[0].astype(F32)
    result[...] = value + (out + (bias[7:8, :] + bias[8:9, :]))
    value = value - jnp.mean(value, axis=-1, keepdims=True)
    inverse = lax.rsqrt(jnp.mean(value * value, axis=-1, keepdims=True) + eps_norm)
    hat = value * inverse
    grad = mine[1].astype(F32) + across[1].astype(F32)
    grad_tokens[...] = cot[...] + inverse * (
        grad
        - jnp.mean(grad, axis=-1, keepdims=True)
        - hat * jnp.mean(grad * hat, axis=-1, keepdims=True)
    )


def finish(tokens, cot, mine, across, vectors):
    length, width = tokens.shape
    rows = 128
    one = pl.BlockSpec((rows, width), lambda i: (i, 0))
    two = pl.BlockSpec((2, rows, width), lambda i: (0, i, 0))
    whole = pl.BlockSpec(vectors.shape, lambda i: (0, 0))
    return pl.pallas_call(
        finish_kernel,
        grid=(length // rows,),
        out_shape=[jax.ShapeDtypeStruct((length, width), F32)] * 2,
        in_specs=[one, one, two, two, whole],
        out_specs=[one, one],
        compiler_params=pltpu.CompilerParams(vmem_limit_bytes=60 << 20),
        cost_estimate=pl.CostEstimate(flops=0, bytes_accessed=12 << 20, transcendentals=0),
        name="finish",
    )(tokens, cot, mine, across, vectors)


def adam_step(grad, first, second, param):
    bias_fix = 1.0 - 0.5**STEP
    first_new = 0.5 * first + 0.5 * grad
    second_new = 0.5 * second + 0.5 * grad * grad
    return (
        first_new,
        second_new,
        param - lr_vector * (first_new / bias_fix) / (jnp.sqrt(second_new / bias_fix) + eps_adam),
    )


def local(
    tokens,
    cotangent,
    positions,
    owners,
    masters,
    basis_left,
    basis_right,
    moment1,
    moment2,
    ema,
    vectors,
    vector_moment1,
    vector_moment2,
    hidden_bias,
    hidden_moment1,
    hidden_moment2,
):
    length, width = tokens.shape
    slots = masters.shape[1]
    me = lax.axis_index("dp")
    column = lax.axis_index("mlp")
    replicas = lax.axis_size("dp") // 2
    place = jnp.stack([me, column, me // 2]).astype(jnp.int32)
    owner_row = owners[0]

    inverse_freq = 10000.0 ** (-(jnp.arange(ROT // 2, dtype=F32) * 2.0) / ROT)
    angles = inverse_freq[:, None] * positions.astype(F32)[None, :]
    table = jnp.concatenate([jnp.cos(angles), jnp.sin(angles)], axis=0)
    mine, across, slab, _, _, reduced = layer(
        vectors,
        hidden_bias.reshape(2 * GROUP, -1),
        table,
        tokens,
        cotangent,
        masters[0],
        (owner_row // slots ^ me) * slots + owner_row % slots,
    )
    state = [item[0] for item in (basis_left, basis_right, moment1, moment2, masters, ema)]
    own_grad, first_new, second_new, master_new, weight_copy, ema_new = soap(
        place, owner_row, slab, state, replicas
    )
    result, grad_tokens = finish(tokens, cotangent, mine, across, vectors)
    vector_grad = jnp.concatenate([reduced[:8], reduced[7:8]], axis=0)
    hidden_grad = reduced[8:].reshape(FF)
    vec_first, vec_second, vectors_new = adam_step(
        vector_grad, vector_moment1, vector_moment2, vectors
    )
    hid_first, hid_second, hidden_new = adam_step(
        hidden_grad, hidden_moment1, hidden_moment2, hidden_bias
    )
    return (
        result,
        grad_tokens,
        own_grad[None],
        first_new[None],
        second_new[None],
        master_new[None],
        weight_copy[None],
        ema_new[None],
        vector_grad,
        vec_first,
        vec_second,
        vectors_new,
        hidden_grad,
        hid_first,
        hid_second,
        hidden_new,
    )


def solution(mesh):
    split = P(("dp", "mlp"), None)
    tiled = P("mlp", "dp", None, None)
    return jax.shard_map(
        local,
        mesh=mesh,
        in_specs=(split, split, P(("dp", "mlp")), P("mlp", None)) + (tiled,) * 6 + (P(),) * 6,
        out_specs=(split, split) + (tiled,) * 6 + (P(),) * 8,
        check_vma=False,
    )
```

```python
import functools

import jax
import jax.numpy as jnp
from jax import lax
from jax.experimental import pallas as pl
from jax.experimental.pallas import tpu as pltpu
from jax.sharding import PartitionSpec as P

HEADS = 16
HDIM = 64
ROT = 16
FF = 4096
STEP = 5
TILE = 128
LANES = 128
GROUP = 4

PRECISE = lax.Precision.HIGHEST
eps_norm = 1e-05
eps_adam = 1e-08
lr_matrix = 0.05
lr_vector = 0.5
ema_keep = 0.8

F32 = jnp.float32
BF16 = jnp.bfloat16
ANY = pl.BlockSpec(memory_space=pl.ANY)
VMEM = pl.BlockSpec(memory_space=pltpu.VMEM)
SMEM = pl.BlockSpec(memory_space=pltpu.SMEM)


def dot_nn(left, right):
    return jnp.dot(left, right, preferred_element_type=F32)


def dot_nt(left, right):
    return lax.dot_general(left, right, (((1,), (1,)), ((), ())), preferred_element_type=F32)


def dot_tn(left, right):
    return lax.dot_general(left, right, (((0,), (0,)), ((), ())), preferred_element_type=F32)


def precise(left, right, left_dim, right_dim):
    return lax.dot_general(
        left,
        right,
        (((left_dim,), (right_dim,)), ((), ())),
        precision=PRECISE,
        preferred_element_type=F32,
    )


MESH = pl.DeviceIdType.MESH


def flip(index, mask):
    bit = 1
    while bit <= mask:
        if mask & bit:
            index = index + bit - 2 * bit * ((index // bit) % 2)
        bit *= 2
    return index


def differ(left, right, count):
    total, bit = 0, 1
    while bit < count:
        one, two = (left // bit) % 2, (right // bit) % 2
        total = total + bit * (one + two - 2 * one * two)
        bit *= 2
    return total


class Links:
    def __init__(self, send_sems, recv_sems):
        self.send_sems, self.recv_sems = send_sems, recv_sems
        self.number = 0
        self.all = []

    def plan(self, source, target, device):
        copy = pltpu.make_async_remote_copy(
            src_ref=source,
            dst_ref=target,
            send_sem=self.send_sems.at[self.number],
            recv_sem=self.recv_sems.at[self.number],
            device_id=device,
            device_id_type=MESH,
        )
        self.number += 1
        entry = [copy, False, False]
        self.all.append(entry)
        return entry

    def send(self, source, target, device):
        entry = self.plan(source, target, device)
        entry[0].start()
        return entry

    def arrived(self, entry):
        if not entry[1]:
            entry[0].wait_recv()
            entry[1] = True

    def left(self, entry):
        if not entry[2]:
            entry[0].wait_send()
            entry[2] = True

    def finish(self):
        for entry in self.all:
            self.arrived(entry)
            self.left(entry)


def greet(me, column, masks_dp, masks_z):
    barrier = pltpu.get_barrier_semaphore()
    for mask in masks_dp:
        pl.semaphore_signal(barrier, inc=1, device_id={"dp": flip(me, mask)}, device_id_type=MESH)
    for mask in masks_z:
        pl.semaphore_signal(
            barrier, inc=1, device_id={"mlp": flip(column, mask)}, device_id_type=MESH
        )
    pl.semaphore_wait(barrier, len(masks_dp) + len(masks_z))


class Reduce:
    def __init__(self, links, own, land, me, replicas, pieces):
        self.links, self.own, self.land = links, own, land
        self.me, self.replicas, self.pieces = me, replicas, pieces
        self.first, self.second = [], []

    def start(self):
        for number, (first, size) in enumerate(self.pieces):
            where = pl.ds(first, size)
            device = lambda at: {"dp": flip(self.me, at << 1)}
            near, far = (1, 2) if number % 2 == 0 else (2, 1)
            if self.replicas == 4:
                moves = [(near, 0, near), (3, 1, near)]
            else:
                moves = [(at, at - 1, at) for at in range(1, self.replicas)]
            self.first.append(
                [
                    self.links.send(
                        self.own.at[at, where, :], self.land.at[to, where, :], device(over)
                    )
                    for at, to, over in moves
                ]
            )
            if self.replicas == 4:
                self.second.append(
                    self.links.plan(
                        self.own.at[far, where, :], self.land.at[2, where, :], device(far)
                    )
                )

    def middle(self, number):
        if self.replicas != 4:
            return
        first, size = self.pieces[number]
        rows = slice(first, first + size)
        far = 2 if number % 2 == 0 else 1
        for entry in self.first[number]:
            self.links.arrived(entry)
        self.own[far, rows, :] = (
            self.own[far, rows, :].astype(F32) + self.land[1, rows, :].astype(F32)
        ).astype(BF16)
        self.second[number][0].start()

    def total(self, number):
        first, size = self.pieces[number]
        rows = slice(first, first + size)
        for entry in self.first[number] + (self.second[number : number + 1]):
            self.links.arrived(entry)
        value = self.own[0, rows, :].astype(F32)
        for at in range(self.replicas - 1):
            if self.replicas != 4 or at != 1:
                value = value + self.land[at, rows, :].astype(F32)
        return value

    def left(self):
        for entry in sum(self.first, []) + self.second:
            self.links.left(entry)


class Spread:
    def __init__(self, links, slab, me, count, rows, first, size, backward, pairs=True):
        self.links, self.slab, self.me, self.pairs = links, slab, me, pairs
        self.rows, self.first, self.size = rows, first, size
        self.bits = [1 << i for i in range(1, count.bit_length() - 1)]
        if backward:
            self.bits = self.bits[::-1]
        self.came = {}
        self.order = []

    def part(self, at):
        place = at if self.pairs else at // 2
        return self.slab.at[pl.ds(place * self.rows + self.first, self.size)]

    def forward(self, at, step, source=None):
        source = self.part(at) if source is None else source
        for later in range(step, len(self.bits)):
            bit = self.bits[later]
            entry = self.links.send(source, self.part(at ^ bit), {"dp": flip(self.me, bit)})
            self.came[at ^ bit] = (entry, later + 1)
            self.order.append(at ^ bit)
        if self.pairs:
            self.links.send(source, self.part(at ^ 1), {"dp": flip(self.me, 1)})

    def relay(self):
        while self.order:
            at = min(self.order, key=lambda index: (self.came[index][1], index.bit_count()))
            self.order.remove(at)
            entry, step = self.came[at]
            self.links.arrived(entry)
            self.forward(at, step)


def attn_unit(column, rank, place):
    by_columns = (place // 2) * 8 + 2 * rank + place % 2
    by_rows = (2 * rank + place // 8) * 8 + place % 8
    return jnp.where(column == 3, by_rows, by_columns)


def ff_unit(core, place):
    later = place - 32
    up = 64 + (place // 4) * 8 + core * 4 + place % 4
    down = 128 + (core * 4 + later // 8) * 8 + later % 8
    return jnp.where(place < 32, up, down)


def erf_f32(value):
    value = jnp.clip(value, -3.832506856900711, 3.832506856900711)
    square = value * value
    top = jnp.full_like(square, 0.00022905065861350646)
    for coeff in (
        0.0034082910107109506,
        0.050955695062380861,
        0.18520832239976145,
        1.128379143519084,
    ):
        top = top * square + coeff
    low = jnp.full_like(square, -1.1791602954361697e-7)
    for coeff in (
        0.000023547966471313185,
        0.0010179625278914885,
        0.014070470171167667,
        0.11098505178285362,
        0.49746925110067538,
        1.0,
    ):
        low = low * square + coeff
    return value * top / low


def row_sum(value):
    return dot_nn(jnp.ones((16, value.shape[0]), BF16), value)[0:1, :]


def transpose_tile(value):
    return jnp.swapaxes(value, 0, 1)


def layer_kernel(slots, devices, *refs):
    refs = list(refs)
    take = lambda number: [refs.pop(0) for _ in range(number)]
    norm_ref, hidden_ref, table, tokens, cot_ref, masters, tile_ref = take(7)
    mine, across, slab, attn_parts, z_ff, reduced = take(6)
    weights, table_ref, own_attn, send_attn, send_ff = take(5)
    h_all, c_all, out_acc, back_acc = take(4)
    tiles, weight_a, weight_b, acc_a, acc_b = take(5)
    q_all, k_all, v_all, g_all, o_all, dq_all, dk_all, dv_all = take(8)
    dw, own_land, attn_land, core_land = take(4)
    own_sum, attn_keep, attn_send, attn_back, z_send, z_land, block_all = take(7)
    vec, vec_land, vec_sum = take(3)
    local_sems, tile_sems, slot_sems, send_sems, recv_sems = take(5)
    me, column = lax.axis_index("dp"), lax.axis_index("mlp")
    replicas = devices // 2
    core, quarter = me % 2, me // 2
    rank = 2 * (column % 2) + core
    length, width = h_all.shape[1:]
    hidden = 4 * TILE
    wide = 4 * HDIM
    up, up_acc = weight_a.at[:, 0:hidden], acc_a.at[:, 0:hidden]
    down, down_acc = weight_b, acc_b
    w_in, in_acc = weight_a, acc_a
    w_out, proj_acc = weight_b.at[0:wide, :], acc_b.at[0:wide, :]
    rows_ff, rows_attn = 64 * TILE // replicas, 16 * TILE // replicas
    links = Links(send_sems, recv_sems)
    greet(me, column, [1] + [at << 1 for at in range(1, replicas)], [1, 2, 3])

    stage = [pltpu.make_async_copy(tokens, acc_b, local_sems.at[8])]
    places = []
    for slot in range(slots):
        place = acc_a.at[pl.ds(slot // 6 * TILE, TILE), pl.ds(slot % 6 * TILE, TILE)]
        places.append(place)
        stage.append(pltpu.make_async_copy(masters.at[slot], place, slot_sems.at[slot]))
    for copy in stage[1:] + stage[:1]:
        copy.start()
    for slot in range(slots):
        stage[1 + slot].wait()
        weights[slot] = places[slot][...].astype(BF16)
    cut = slots // 2
    spreads = [
        Spread(links, weights, me, devices, slots, 0, cut, False),
        Spread(links, weights, me, devices, slots, cut, slots - cut, True),
    ]
    for spread in spreads:
        spread.forward(0, 0)
    gathered = list(links.all)

    def normalize(step, carry):
        where = pl.ds(pl.multiple_of(step * TILE, TILE), TILE)
        value = acc_b[where, :]
        value = value - jnp.mean(value, axis=-1, keepdims=True)
        value = value * lax.rsqrt(jnp.mean(value * value, axis=-1, keepdims=True) + eps_norm)
        h_all[0, where, :] = value.astype(BF16)
        return carry

    stage[0].wait()
    lax.fori_loop(0, length // TILE, normalize, 0)
    copy = pltpu.make_async_copy(cot_ref, acc_b, local_sems.at[7])
    copy.start()
    along = []

    def send_along(target, where):
        entry = links.send(
            target.at[0, where, :], target.at[2, where, :], {"mlp": flip(column, 1)}
        )
        along.append((target, where, entry))

    table_ref[0] = table[...]
    early = length * 5 // 8
    send_along(h_all, pl.ds(0, length))
    send_along(table_ref, pl.ds(0, ROT))
    copy.wait()
    c_all[0] = acc_b[...].astype(BF16)
    send_along(c_all, pl.ds(0, early))
    core_blocks = [
        links.send(target.at[0], target.at[1], {"dp": flip(me, 1)})
        for target in (h_all, table_ref, c_all)
    ]
    number = len(links.all)
    for spread in spreads:
        spread.relay()
    gathered += links.all[number:]
    for entry in gathered:
        links.arrived(entry)

    def fill(out_ref, base, rows_out, first_row, unit_of):
        size = min(TILE, rows_out)

        def body(step, carry):
            row = first_row + step * size
            tile = tile_ref[unit_of(row // TILE)]
            where = pl.ds(pl.multiple_of(base + step * size, size), size)
            if size == TILE:
                out_ref[where, :] = weights[tile]
            else:
                out_ref[where, :] = weights[tile, pl.ds(pl.multiple_of(row % TILE, size), size), :]
            return carry

        lax.fori_loop(0, rows_out // size, body, 0)

    low = column % 2
    attn_came_z = []
    for bit in (3, 2, 1):
        fill(
            send_attn,
            (bit - 1) * rows_attn,
            rows_attn,
            quarter * rows_attn,
            functools.partial(attn_unit, column, 2 * (flip(low, 1) if bit & 1 else low) + core),
        )
        piece = pl.ds((bit - 1) * rows_attn, rows_attn)
        attn_came_z.append(
            links.send(
                send_attn.at[piece, :], attn_parts.at[piece, :], {"mlp": flip(column, bit)}
            )
        )
    send_along(c_all, pl.ds(early, length - early))
    fill(send_ff, 0, rows_ff, quarter * rows_ff, functools.partial(ff_unit, core))
    came_ff = [links.send(send_ff, z_ff.at[0], {"mlp": flip(column, 2)})]
    fill(tiles, 0, 64 * TILE, 0, functools.partial(ff_unit, core))
    fill(own_attn, 0, 16 * TILE, 0, functools.partial(attn_unit, column, rank))
    vec[...] = jnp.zeros_like(vec)

    def set_ff_weights():
        for at in range(32):
            up[
                (at // 4) * TILE : (at // 4 + 1) * TILE, (at % 4) * TILE : (at % 4 + 1) * TILE
            ] = tiles[at * TILE : (at + 1) * TILE, :]
            down[
                (at // 8) * TILE : (at // 8 + 1) * TILE, (at % 8) * TILE : (at % 8 + 1) * TILE
            ] = tiles[(32 + at) * TILE : (33 + at) * TILE, :]
        up_acc[...] = jnp.zeros((width, hidden), F32)
        down_acc[...] = jnp.zeros((hidden, width), F32)

    def ff_block(at, ff_column, first, store):
        hat = h_all[at].astype(F32)
        normed = (hat * norm_ref[2:3, :] + norm_ref[3:4, :]).astype(BF16)
        cot = c_all[at]
        pre = dot_nn(normed, up[...]) + hidden_ref[pl.ds(2 * ff_column + core, 1), :]
        cdf = 0.5 + 0.5 * erf_f32(pre * 0.7071067811865476)
        act = (pre * cdf).astype(BF16)
        grad = dot_nt(cot, down[...])
        grad = grad * (cdf + pre * (jnp.exp(-0.5 * pre * pre) * 0.3989422804014327))
        grad = grad.astype(BF16)
        where = pl.ds(pl.multiple_of(core * hidden, hidden), hidden)
        vec[pl.ds(8 + ff_column, 1), where] += row_sum(grad)
        out = dot_nn(act, down[...])
        back = dot_nt(grad, up[...])
        vec[2:3, :] += jnp.sum(back * hat, axis=0, keepdims=True)
        vec[3:4, :] += jnp.sum(back, axis=0, keepdims=True)
        back = back * norm_ref[2:3, :]
        if not first:
            out = out + out_acc[at].astype(F32)
            back = back + back_acc[at].astype(F32)
        store(out, back)
        up_acc[...] += dot_tn(normed, grad)
        down_acc[...] += dot_tn(act, cot)

    def store_ff(target):
        per = rows_ff // TILE
        for at in range(64):
            if at < 32:
                tile = up_acc[
                    (at // 4) * TILE : (at // 4 + 1) * TILE, (at % 4) * TILE : (at % 4 + 1) * TILE
                ]
            else:
                low = at - 32
                tile = down_acc[
                    (low // 8) * TILE : (low // 8 + 1) * TILE,
                    (low % 8) * TILE : (low % 8 + 1) * TILE,
                ]
            target[
                differ(at // per, quarter, replicas), (at % per) * TILE : (at % per + 1) * TILE, :
            ] = tile.astype(BF16)

    def attn_rows(matrix):
        return pl.multiple_of(matrix * (16 * TILE), TILE)

    def attn_rows(matrix):
        return pl.multiple_of(matrix * (16 * TILE), TILE)

    set_ff_weights()
    vec[7:8, :] = row_sum(c_all[0])

    def own_block(at):
        def store(out, back):
            out_acc[at] = out.astype(BF16)
            back_acc[at] = back.astype(BF16)

        ff_block(at, column, True, store)

    own_block(0)
    spreads = []
    for number, entry in enumerate(attn_came_z[::-1]):
        links.arrived(entry)
        pieces = [(number * rows_attn, rows_attn, number == 1)]
        if number == 2:
            cut = rows_attn // 32 * 16
            pieces = [
                (2 * rows_attn, cut, False),
                (2 * rows_attn + cut, rows_attn - cut, True),
            ]
        for first, size, backward in pieces:
            spreads.append(
                Spread(links, attn_parts, me, devices, 3 * rows_attn, first, size, backward, False)
            )
            spreads[-1].forward(0, 0)
    for entry in core_blocks:
        links.arrived(entry)
    own_block(1)
    for target, where, entry in along:
        links.arrived(entry)
        core_blocks.append(
            links.send(target.at[2, where, :], target.at[3, where, :], {"dp": flip(me, 1)})
        )
    for spread in spreads:
        spread.relay()
    gathered = links.all[:]
    own_block(2)
    for entry in core_blocks:
        links.arrived(entry)
    own_block(3)
    store_ff(dw)
    own_reduce = Reduce(
        links, dw, own_land, me, replicas, [(0, rows_ff // 2), (rows_ff // 2, rows_ff // 2)]
    )
    own_reduce.start()
    links.arrived(came_ff[0])
    relays = []
    if replicas == 4:
        for near, far, first in ((1, 2, 0), (2, 1, rows_ff // 2)):
            where = pl.ds(first, rows_ff // 2)
            for at in (near, far):
                came_ff.append(
                    links.send(
                        z_ff.at[0, where, :], z_ff.at[at, where, :], {"dp": flip(me, at << 1)}
                    )
                )
            relays.append(
                (
                    came_ff[-2],
                    links.plan(
                        z_ff.at[near, where, :], z_ff.at[3, where, :], {"dp": flip(me, far << 1)}
                    ),
                )
            )
            came_ff.append(relays[-1][1])
    else:
        for at in range(1, replicas):
            came_ff.append(links.send(z_ff.at[0], z_ff.at[at], {"dp": flip(me, at << 1)}))

    def between(at):
        @pl.when(at == 1)
        def _():
            for number in range(2):
                own_reduce.middle(number)

        @pl.when(at == 2)
        def _():
            for entry, copy in relays:
                links.arrived(entry)
                copy[0].start()

    for entry in gathered:
        links.arrived(entry)
    tile_loads = [
        pltpu.make_async_copy(
            own_attn, tiles.at[pl.ds(attn_rows(column), 16 * TILE), :], tile_sems.at[0]
        )
    ]
    for at in range(replicas):
        for bit in (1, 2, 3):
            first = attn_rows(flip(column, bit)) + differ(at, quarter, replicas) * rows_attn
            tile_loads.append(
                pltpu.make_async_copy(
                    attn_parts.at[pl.ds((3 * at + bit - 1) * rows_attn, rows_attn), :],
                    tiles.at[pl.ds(pl.multiple_of(first, rows_attn), rows_attn), :],
                    tile_sems.at[len(tile_loads)],
                )
            )
    for copy in tile_loads:
        copy.start()
    for copy in tile_loads:
        copy.wait()
    for matrix in range(3):
        for at in range(16):
            row = (16 * matrix + at) * TILE
            w_in[
                (at // 2) * TILE : (at // 2 + 1) * TILE,
                (2 * matrix + at % 2) * TILE : (2 * matrix + at % 2 + 1) * TILE,
            ] = tiles[row : row + TILE, :]
    for at in range(16):
        w_out[(at // 8) * TILE : (at // 8 + 1) * TILE, (at % 8) * TILE : (at % 8 + 1) * TILE] = (
            tiles[(48 + at) * TILE : (49 + at) * TILE, :]
        )
    in_acc[...] = jnp.zeros((width, 3 * wide), F32)
    proj_acc[...] = jnp.zeros((wide, width), F32)
    half = ROT // 2
    block = BLOCK
    scale = HDIM ** (-0.5)
    lane = lax.broadcasted_iota(jnp.int32, (1, LANES), 1)
    within = lane % HDIM
    keep_low = lane < HDIM
    wave = lax.broadcasted_iota(jnp.int32, (ROT, LANES), 0)
    spot = lax.broadcasted_iota(jnp.int32, (ROT, LANES), 1) % HDIM
    pick_cos = ((spot < ROT) & (wave == spot % half)).astype(F32)
    pick_first = ((spot < half) & (wave == half + spot)).astype(F32)
    pick_second = ((spot >= half) & (spot < ROT) & (wave == spot)).astype(F32)
    plain = (within >= ROT).astype(F32)

    def attn_block(at, carry):
        hat = h_all[at].astype(F32)
        normed = (hat * norm_ref[0:1, :] + norm_ref[1:2, :]).astype(BF16)
        cot = c_all[at]
        table = table_ref[at]
        cos_w = precise(table, pick_cos, 0, 0) + plain
        sin_a = precise(table, pick_first, 0, 0)
        sin_b = precise(table, pick_second, 0, 0)
        proj = dot_nn(normed, w_in[...])
        g_all[...] = dot_nt(cot, w_out[...]).astype(BF16)

        def turn(value):
            return (
                value * cos_w
                - pltpu.roll(value, LANES - half, 1) * sin_a
                + pltpu.roll(value, half, 1) * sin_b
            )

        for pair in range(2):
            cols = slice(pair * LANES, (pair + 1) * LANES)
            where = pl.ds(pl.multiple_of(rank * wide + pair * LANES, LANES), LANES)
            query = proj[:, pair * LANES : (pair + 1) * LANES] + norm_ref[4:5, where]
            key = proj[:, wide + pair * LANES : wide + (pair + 1) * LANES] + norm_ref[5:6, where]
            value = proj[:, 2 * wide + pair * LANES : 2 * wide + (pair + 1) * LANES]
            q_all[:, cols] = (turn(query).astype(BF16) * scale).astype(BF16)
            k_all[:, cols] = turn(key).astype(BF16)
            v_all[:, cols] = (value + norm_ref[6:7, where]).astype(BF16)
        zero = jnp.zeros((), BF16)
        for pair in range(2):
            cols = slice(pair * LANES, (pair + 1) * LANES)
            query, key = q_all[:, cols], k_all[:, cols]
            value, grad = v_all[:, cols], g_all[:, cols]
            key_t, value_t = transpose_tile(key), transpose_tile(value)
            out_t, dq_t = [], []
            dk_all[:, cols] = jnp.zeros((length, LANES), F32)
            dv_all[:, cols] = jnp.zeros((length, LANES), F32)
            for head in range(2):
                mask = keep_low if head == 0 else jnp.logical_not(keep_low)
                key_m, value_m = jnp.where(mask, key, zero), jnp.where(mask, value, zero)
                query_m, grad_m = jnp.where(mask, query, zero), jnp.where(mask, grad, zero)
                part = slice(head * HDIM, (head + 1) * HDIM)
                out_row, dq_row = [], []
                for first in range(0, length, block):
                    last = first + block
                    scores = dot_nt(key_m[:last], query[first:last])
                    key_at = lax.broadcasted_iota(jnp.int32, scores.shape, 0)
                    query_at = first + lax.broadcasted_iota(jnp.int32, scores.shape, 1)
                    scores = jnp.where(key_at <= query_at, scores, -1e30)
                    peak = jnp.max(scores, axis=0, keepdims=True)
                    raised = jnp.exp(scores - peak)
                    prob = raised * (1.0 / jnp.sum(raised, axis=0, keepdims=True))
                    prob_low = prob.astype(BF16)
                    grad_prob = dot_nt(value_m[:last], grad[first:last])
                    delta = jnp.sum(prob * grad_prob, axis=0, keepdims=True)
                    grad_scores = (prob * (grad_prob - delta)).astype(BF16)
                    out_row.append(dot_nn(value_t[part, :last], prob_low))
                    dq_row.append(dot_nn(key_t[part, :last], grad_scores))
                    dv_all[:last, cols] += dot_nn(prob_low, grad_m[first:last])
                    dk_all[:last, cols] += dot_nn(grad_scores, query_m[first:last])
                out_t.append(jnp.concatenate(out_row, axis=1))
                dq_t.append(jnp.concatenate(dq_row, axis=1))
            o_all[:, cols] = transpose_tile(jnp.concatenate(out_t, axis=0)).astype(BF16)
            dq_all[:, cols] = transpose_tile(jnp.concatenate(dq_t, axis=0)) * scale

        def turn_back(value):
            return (
                value * cos_w
                + pltpu.roll(value, LANES - half, 1) * sin_a
                - pltpu.roll(value, half, 1) * sin_b
            ).astype(BF16)

        pieces = [turn_back(dq_all[:, 0:LANES]), turn_back(dq_all[:, LANES : 2 * LANES])]
        pieces += [turn_back(dk_all[:, 0:LANES]), turn_back(dk_all[:, LANES : 2 * LANES])]
        pieces += [dv_all[...].astype(BF16)]
        grads = jnp.concatenate(pieces, axis=1)
        sums = row_sum(grads)
        where = pl.ds(pl.multiple_of(rank * wide, LANES), wide)
        for matrix in range(3):
            vec[4 + matrix : 5 + matrix, where] += sums[:, matrix * wide : (matrix + 1) * wide]
        out = dot_nn(o_all[...], w_out[...])
        out_acc[at] = (out_acc[at].astype(F32) + out).astype(BF16)
        back = dot_nt(grads, w_in[...])
        vec[0:1, :] += jnp.sum(back * hat, axis=0, keepdims=True)
        vec[1:2, :] += jnp.sum(back, axis=0, keepdims=True)
        back_acc[at] = (back_acc[at].astype(F32) + back * norm_ref[0:1, :]).astype(BF16)
        in_acc[...] += dot_tn(normed, grads)
        proj_acc[...] += dot_tn(o_all[...], cot)
        between(at)
        return carry

    lax.fori_loop(0, 4, attn_block, 0)
    for number, (first, count) in enumerate(own_reduce.pieces):
        own_sum[first : first + count, :] = own_reduce.total(number)
    own_reduce.left()
    size = min(TILE, rows_attn)
    for matrix in range(4):
        for at in range(16):
            for piece in range(TILE // size):
                row = at * TILE + piece * size
                if matrix < 3:
                    top, left = (at // 2) * TILE, (2 * matrix + at % 2) * TILE
                    tile = in_acc[top + piece * size : top + (piece + 1) * size, left : left + TILE]
                else:
                    top, left = (at // 8) * TILE, (at % 8) * TILE
                    tile = proj_acc[
                        top + piece * size : top + (piece + 1) * size, left : left + TILE
                    ]
                inner = row % rows_attn
                dw[
                    differ(row // rows_attn, quarter, replicas),
                    pl.ds(
                        pl.multiple_of(flip(column, matrix) * rows_attn + inner, size), size
                    ),
                    :,
                ] = tile.astype(BF16)
    attn_reduce = Reduce(
        links, dw, attn_land, me, replicas, [(0, 2 * rows_attn), (2 * rows_attn, 2 * rows_attn)]
    )
    attn_reduce.start()

    other = flip(column, 2)
    for entry in came_ff:
        links.arrived(entry)
    tile_loads = []
    for at in range(replicas):
        first = pl.multiple_of(differ(at, quarter, replicas) * rows_ff, TILE)
        tile_loads.append(
            pltpu.make_async_copy(
                z_ff.at[at], tiles.at[pl.ds(first, rows_ff), :], tile_sems.at[at]
            )
        )
    for copy in tile_loads:
        copy.start()
    for copy in tile_loads:
        copy.wait()
    set_ff_weights()
    core_came = {}
    outs = []
    waiting = []

    def pump(count):
        for number, source, where in waiting[:count]:
            links.send(
                source.at[2, where, :], across.at[number, where, :], {"mlp": flip(column, 1)}
            )
        del waiting[:count]

    def send_core(at):
        def store(out, back):
            out_acc[at] = out.astype(BF16)
            back_acc[at] = back.astype(BF16)
            for number, source in ((0, out_acc), (1, back_acc)):
                core_came[number, at // 2] = links.send(
                    source.at[at], core_land.at[number, at // 2], {"dp": flip(me, 1)}
                )

        return store

    def keep(at):
        def store(out, back):
            for number, value, source in ((0, out, out_acc), (1, back, back_acc)):
                links.arrived(core_came[number, at // 2])
                value = value + core_land[number, at // 2].astype(F32)
                source[at] = value.astype(BF16)
                if at == 0:
                    copy = pltpu.make_async_copy(
                        source.at[at], mine.at[number], local_sems.at[number]
                    )
                    copy.start()
                    outs.append(copy)
                else:
                    for first in range(0, length, length // 4):
                        waiting.append((number, source, pl.ds(first, length // 4)))

        return store

    for at in (3, 2, 1, 0):
        ff_block(at, other, False, send_core(at) if at % 2 else keep(at))
        pump(1)
        if at == 2:
            for number in range(2):
                attn_reduce.middle(number)
    attn_total = [attn_reduce.total(number) for number in range(2)]
    attn_keep[...] = attn_total[0][0:rows_attn]
    attn_send[0:rows_attn, :] = attn_total[0][rows_attn : 2 * rows_attn].astype(BF16)
    attn_send[rows_attn : 3 * rows_attn, :] = attn_total[1].astype(BF16)
    attn_reduce.left()

    store_ff(dw)
    chunks = 4
    size = rows_ff // chunks
    other_reduce = Reduce(
        links, dw, own_land, me, replicas, [(chunk * size, size) for chunk in range(chunks)]
    )
    other_reduce.start()
    vec_came = [
        links.send(vec, vec_land.at[bit], {"mlp": flip(column, bit)}) for bit in (1, 2, 3)
    ]
    back_came = []
    for bit in (1, 2, 3):
        piece = pl.ds((bit - 1) * rows_attn, rows_attn)
        back_came.append(
            links.send(attn_send.at[piece, :], attn_back.at[bit - 1], {"mlp": flip(column, bit)})
        )
    pump(1)
    rows = slots * TILE
    spreads = []

    def publish(first, count):
        backward = len(spreads) % 2 == 1
        spread = Spread(links, slab, me, devices, rows, first, count, backward)
        source = block_all.at[pl.ds(first, count), :]
        spread.forward(0, 0, source)
        copy = pltpu.make_async_copy(source, spread.part(0), local_sems.at[2 + len(spreads)])
        copy.start()
        outs.append(copy)
        spreads.append(spread)

    def add_chunk(chunk):
        piece = slice(chunk * size, (chunk + 1) * size)
        z_send[piece, :] = other_reduce.total(chunk).astype(BF16)
        where = pl.ds(chunk * size, size)
        return links.send(z_send.at[where, :], z_land.at[where, :], {"mlp": flip(column, 2)})

    for entry in vec_came:
        links.arrived(entry)
    vec_sum[0] = (vec[...] + vec_land[1]) + (vec_land[2] + vec_land[3])
    vec_core = links.send(vec_sum.at[0], vec_land.at[0], {"dp": flip(me, 1)})
    other_reduce.middle(0)
    pump(1)
    for entry in back_came:
        links.arrived(entry)
    block_all[rows_ff : rows_ff + rows_attn, :] = (
        attn_keep[...] + attn_back[1].astype(F32)
    ).astype(BF16)
    publish(rows_ff, rows_attn)
    block_all[rows_ff + rows_attn : rows, :] = (
        attn_back[0].astype(F32) + attn_back[2].astype(F32)
    ).astype(BF16)
    publish(rows_ff + rows_attn, rows_attn)
    links.arrived(vec_core)
    vec_sum[1] = vec_sum[0] + vec_land[0]
    vec_came = [
        links.send(vec_sum.at[1], vec_land.at[3 + at], {"dp": flip(me, at << 1)})
        for at in range(1, replicas)
    ]
    for chunk in range(1, chunks):
        other_reduce.middle(chunk)
    z_came = []
    for chunk in range(chunks):
        z_came.append(add_chunk(chunk))
        pump(1)
    for spread in spreads[:2]:
        spread.relay()
    for chunk in range(chunks):
        links.arrived(z_came[chunk])
        piece = slice(chunk * size, (chunk + 1) * size)
        block_all[piece, :] = (own_sum[piece, :] + z_land[piece, :].astype(F32)).astype(BF16)
        publish(chunk * size, size)
        pump(1)
        if chunk > 0:
            spreads[1 + chunk].relay()
    pump(len(waiting))
    spreads[1 + chunks].relay()
    for entry in vec_came:
        links.arrived(entry)
    values = [vec_sum[1]] + [vec_land[3 + at] for at in range(1, replicas)]
    while len(values) > 1:
        values = [values[i] + values[i + 1] for i in range(0, len(values), 2)]
    reduced[...] = values[0]
    for copy in outs:
        copy.wait()
    links.finish()


BLOCK = 256


def layer(vectors, hidden_bias, table, tokens, cot, masters, tile_row):
    length, width = tokens.shape
    slots = masters.shape[0]
    devices = lax.axis_size("dp")
    replicas = devices // 2
    hidden = 4 * TILE
    wide = 4 * HDIM
    rows = slots * TILE
    rows_ff, rows_attn = 64 * TILE // replicas, 16 * TILE // replicas
    count = 2 * (2 * replicas - 1) + 11 + 3 + 4 * (replicas - 1)
    count += 1 + 2 * (replicas - 1) + 4 + 8 + 8 * (replicas - 1) + 3 + 3 + 4 + 1 + replicas - 1
    count += 6 * (2 * replicas - 1)
    vmem = lambda *shape: pltpu.VMEM(shape, BF16)
    vmem32 = lambda *shape: pltpu.VMEM(shape, F32)
    return pl.pallas_call(
        functools.partial(layer_kernel, slots, devices),
        out_shape=[
            jax.ShapeDtypeStruct((2, length, width), BF16),
            jax.ShapeDtypeStruct((2, length, width), BF16),
            jax.ShapeDtypeStruct((devices * rows, LANES), BF16),
            jax.ShapeDtypeStruct((replicas * 3 * rows_attn, LANES), BF16),
            jax.ShapeDtypeStruct((replicas, rows_ff, LANES), BF16),
            jax.ShapeDtypeStruct((12, width), F32),
        ],
        in_specs=[VMEM] * 3 + [ANY] * 3 + [SMEM],
        out_specs=[ANY] * 5 + [VMEM],
        scratch_shapes=[
            vmem(devices * slots, TILE, LANES),
            vmem32(4, ROT, length),
            vmem(16 * TILE, LANES),
            vmem(3 * rows_attn, LANES),
            vmem(rows_ff, LANES),
            vmem(4, length, width),
            vmem(4, length, width),
            vmem(4, length, width),
            vmem(4, length, width),
            vmem(64 * TILE, LANES),
            vmem(width, 3 * wide),
            vmem(hidden, width),
            vmem32(width, 3 * wide),
            vmem32(hidden, width),
            vmem(length, wide),
            vmem(length, wide),
            vmem(length, wide),
            vmem(length, wide),
            vmem(length, wide),
            vmem32(length, wide),
            vmem32(length, wide),
            vmem32(length, wide),
            vmem(replicas, rows_ff, LANES),
            vmem(replicas - 1, rows_ff, LANES),
            vmem(replicas - 1, 4 * rows_attn, LANES),
            vmem(2, 2, length, width),
            vmem32(rows_ff, LANES),
            vmem32(rows_attn, LANES),
            vmem(3 * rows_attn, LANES),
            vmem(3, rows_attn, LANES),
            vmem(rows_ff, LANES),
            vmem(rows_ff, LANES),
            vmem(rows, LANES),
            vmem32(12, width),
            vmem32(3 + replicas, 12, width),
            vmem32(2, 12, width),
            pltpu.SemaphoreType.DMA((9,)),
            pltpu.SemaphoreType.DMA((3 * replicas + 1,)),
            pltpu.SemaphoreType.DMA((slots,)),
            pltpu.SemaphoreType.DMA((count,)),
            pltpu.SemaphoreType.DMA((count,)),
        ],
        compiler_params=pltpu.CompilerParams(
            vmem_limit_bytes=63 << 20, collective_id=2, has_side_effects=True
        ),
        cost_estimate=pl.CostEstimate(
            flops=60 * 10**9, bytes_accessed=40 << 20, transcendentals=0
        ),
        name="layer",
    )(vectors, hidden_bias, table, tokens, cot, masters, tile_row)


def split(value):
    high = value.astype(BF16)
    return high, (value - high.astype(F32)).astype(BF16)


def soap_kernel(slots, replicas, per_step, *refs):
    refs = list(refs)
    take = lambda number: [refs.pop(0) for _ in range(number)]
    place_ref, owner_ref, slab = take(3)
    left_ref, right_ref, first_ref, second_ref, master_ref, ema_ref = take(6)
    token_refs = take(5)
    grad_ref, first_out, second_out, master_out, copy_out, ema_out = take(6)
    finish_block(*token_refs, *take(2))
    mine, inverse, sem = take(3)
    me, column = place_ref[0], place_ref[1]
    step = pl.program_id(0)
    bias_fix = 1.0 - 0.5**STEP
    rows_ff = 64 * TILE // replicas
    rows_attn = 16 * TILE // replicas
    rows_all = slots * TILE
    size = min(TILE, rows_attn)

    @pl.when(step == 0)
    def _():
        def note(unit, carry):
            inverse[owner_ref[unit]] = unit
            return carry

        lax.fori_loop(0, owner_ref.shape[0], note, 0)

        def fetch(number, carry):
            unit = inverse[me * slots + number]
            row, col = (unit % 64) // 8, unit % 8
            by_rows = column == 3
            rank = jnp.where(by_rows, row // 2, col // 2)
            attn_place = jnp.where(by_rows, (row % 2) * 8 + col, row * 2 + col % 2)
            up_place = row * 4 + col % 4
            down_place = 32 + (row % 4) * 8 + col
            is_attn, is_up = unit < 64, unit < 128
            core = jnp.where(is_attn, rank % 2, jnp.where(is_up, col // 4, row // 4))
            other = ((rank // 2) != (column % 2)).astype(jnp.int32)
            for piece in range(TILE // size):
                attn_row = attn_place * TILE + piece * size
                ff_row = jnp.where(is_up, up_place, down_place) * TILE + piece * size
                holder = jnp.where(is_attn, attn_row // rows_attn, ff_row // rows_ff)
                inner = jnp.where(
                    is_attn, rows_ff + other * rows_attn + attn_row % rows_attn, ff_row % rows_ff
                )
                start = ((holder * 2 + core) ^ me) * rows_all + inner
                pltpu.make_async_copy(
                    slab.at[pl.ds(pl.multiple_of(start, size), size), :],
                    mine.at[number, pl.ds(piece * size, size), :],
                    sem,
                ).start()
            return carry

        lax.fori_loop(0, slots, fetch, 0)
        pltpu.make_async_copy(mine, mine, sem).wait()

    every = range(per_step)
    grads = [mine[step * per_step + number] for number in every]
    left = [split(left_ref[number]) for number in every]
    right = [split(right_ref[number]) for number in every]
    twice = lambda value, axis: jnp.concatenate([value, value], axis=axis)
    both = lambda pair, axis: jnp.concatenate(pair, axis=axis)
    turned = [dot_tn(both(left[n], 0), twice(grads[n], 0)) for n in every]
    parts = [split(turned[n]) for n in every]
    turned = [
        dot_nn(parts[n][0], right[n][1]) + dot_nn(both(parts[n], 1), twice(right[n][0], 0))
        for n in every
    ]
    scaled = []
    for n in every:
        grad_ref[n] = grads[n].astype(F32)
        first = 0.5 * first_ref[n] + 0.5 * turned[n]
        second = 0.5 * second_ref[n] + 0.5 * turned[n] * turned[n]
        first_out[n] = first
        second_out[n] = second
        scaled.append(first / bias_fix / (jnp.sqrt(second / bias_fix) + eps_adam))
    parts = [split(scaled[n]) for n in every]
    back = [
        dot_nn(left[n][0], parts[n][1]) + dot_nn(both(left[n], 1), twice(parts[n][0], 0))
        for n in every
    ]
    parts = [split(back[n]) for n in every]
    back = [
        dot_nt(parts[n][0], right[n][1]) + dot_nt(both(parts[n], 1), twice(right[n][0], 1))
        for n in every
    ]
    for n in every:
        master = master_ref[n] - lr_matrix * back[n]
        master_out[n] = master
        copy_out[n] = master.astype(BF16)
        ema_out[n] = ema_keep * ema_ref[n] + (1.0 - ema_keep) * master


def soap(place, owner_row, slab, state, token_state, replicas):
    slots = state[0].shape[0]
    steps = STEPS if slots % STEPS == 0 else 1
    per_step = slots // steps
    length, width = token_state[0].shape
    one = pl.BlockSpec((length // steps, width), lambda i: (i, 0))
    two = pl.BlockSpec((2, length // steps, width), lambda i: (0, i, 0))
    whole = pl.BlockSpec(token_state[4].shape, lambda i: (0, 0))
    spec = pl.BlockSpec((per_step, TILE, TILE), lambda i: (i, 0, 0))
    shape = (slots, TILE, TILE)
    return pl.pallas_call(
        functools.partial(soap_kernel, slots, replicas, per_step),
        grid=(steps,),
        out_shape=[jax.ShapeDtypeStruct(shape, F32)] * 4
        + [jax.ShapeDtypeStruct(shape, BF16), jax.ShapeDtypeStruct(shape, F32)]
        + [jax.ShapeDtypeStruct((length, width), F32)] * 2,
        in_specs=[SMEM, SMEM, ANY] + [spec] * 6 + [one, one, two, two, whole],
        out_specs=[spec] * 6 + [one, one],
        scratch_shapes=[
            pltpu.VMEM(shape, BF16),
            pltpu.SMEM((owner_row.shape[0],), jnp.int32),
            pltpu.SemaphoreType.DMA,
        ],
        compiler_params=pltpu.CompilerParams(vmem_limit_bytes=60 << 20),
        cost_estimate=pl.CostEstimate(
            flops=24 * slots * 2 * TILE**3, bytes_accessed=20 << 20, transcendentals=0
        ),
        name="soap",
    )(place, owner_row, slab, *state, *token_state)


def finish_block(tokens, cot, mine, across, bias, result, grad_tokens):
    value = tokens[...]
    out = mine[0].astype(F32) + across[0].astype(F32)
    result[...] = value + (out + (bias[7:8, :] + bias[8:9, :]))
    value = value - jnp.mean(value, axis=-1, keepdims=True)
    inverse = lax.rsqrt(jnp.mean(value * value, axis=-1, keepdims=True) + eps_norm)
    hat = value * inverse
    grad = mine[1].astype(F32) + across[1].astype(F32)
    grad_tokens[...] = cot[...] + inverse * (
        grad
        - jnp.mean(grad, axis=-1, keepdims=True)
        - hat * jnp.mean(grad * hat, axis=-1, keepdims=True)
    )


STEPS = 4


def adam_step(grad, first, second, param):
    bias_fix = 1.0 - 0.5**STEP
    first_new = 0.5 * first + 0.5 * grad
    second_new = 0.5 * second + 0.5 * grad * grad
    return (
        first_new,
        second_new,
        param - lr_vector * (first_new / bias_fix) / (jnp.sqrt(second_new / bias_fix) + eps_adam),
    )


def local(
    tokens,
    cotangent,
    positions,
    owners,
    masters,
    basis_left,
    basis_right,
    moment1,
    moment2,
    ema,
    vectors,
    vector_moment1,
    vector_moment2,
    hidden_bias,
    hidden_moment1,
    hidden_moment2,
):
    length, width = tokens.shape
    slots = masters.shape[1]
    me = lax.axis_index("dp")
    column = lax.axis_index("mlp")
    replicas = lax.axis_size("dp") // 2
    place = jnp.stack([me, column, me // 2]).astype(jnp.int32)
    owner_row = owners[0]

    inverse_freq = 10000.0 ** (-(jnp.arange(ROT // 2, dtype=F32) * 2.0) / ROT)
    angles = inverse_freq[:, None] * positions.astype(F32)[None, :]
    table = jnp.concatenate([jnp.cos(angles), jnp.sin(angles)], axis=0)
    mine, across, slab, _, _, reduced = layer(
        vectors,
        hidden_bias.reshape(2 * GROUP, -1),
        table,
        tokens,
        cotangent,
        masters[0],
        (owner_row // slots ^ me) * slots + owner_row % slots,
    )
    state = [item[0] for item in (basis_left, basis_right, moment1, moment2, masters, ema)]
    token_state = [tokens, cotangent, mine, across, vectors]
    own_grad, first_new, second_new, master_new, weight_copy, ema_new, result, grad_tokens = soap(
        place, owner_row, slab, state, token_state, replicas
    )
    vector_grad = jnp.concatenate([reduced[:8], reduced[7:8]], axis=0)
    hidden_grad = reduced[8:].reshape(FF)
    vec_first, vec_second, vectors_new = adam_step(
        vector_grad, vector_moment1, vector_moment2, vectors
    )
    hid_first, hid_second, hidden_new = adam_step(
        hidden_grad, hidden_moment1, hidden_moment2, hidden_bias
    )
    return (
        result,
        grad_tokens,
        own_grad[None],
        first_new[None],
        second_new[None],
        master_new[None],
        weight_copy[None],
        ema_new[None],
        vector_grad,
        vec_first,
        vec_second,
        vectors_new,
        hidden_grad,
        hid_first,
        hid_second,
        hidden_new,
    )


def solution(mesh):
    split = P(("dp", "mlp"), None)
    tiled = P("mlp", "dp", None, None)
    return jax.shard_map(
        local,
        mesh=mesh,
        in_specs=(split, split, P(("dp", "mlp")), P("mlp", None)) + (tiled,) * 6 + (P(),) * 6,
        out_specs=(split, split) + (tiled,) * 6 + (P(),) * 8,
        check_vma=False,
    )
```

```python
import functools

import jax
import jax.numpy as jnp
from jax import lax
from jax.experimental import pallas as pl
from jax.experimental.pallas import tpu as pltpu
from jax.sharding import PartitionSpec as P

HEADS = 16
HDIM = 64
ROT = 16
FF = 4096
STEP = 5
TILE = 128
LANES = 128
GROUP = 4

PRECISE = lax.Precision.HIGHEST
eps_norm = 1e-05
eps_adam = 1e-08
lr_matrix = 0.05
lr_vector = 0.5
ema_keep = 0.8

F32 = jnp.float32
BF16 = jnp.bfloat16
ANY = pl.BlockSpec(memory_space=pl.ANY)
VMEM = pl.BlockSpec(memory_space=pltpu.VMEM)
SMEM = pl.BlockSpec(memory_space=pltpu.SMEM)


def dot_nn(left, right):
    return jnp.dot(left, right, preferred_element_type=F32)


def dot_nt(left, right):
    return lax.dot_general(left, right, (((1,), (1,)), ((), ())), preferred_element_type=F32)


def dot_tn(left, right):
    return lax.dot_general(left, right, (((0,), (0,)), ((), ())), preferred_element_type=F32)


def precise(left, right, left_dim, right_dim):
    return lax.dot_general(
        left,
        right,
        (((left_dim,), (right_dim,)), ((), ())),
        precision=PRECISE,
        preferred_element_type=F32,
    )


MESH = pl.DeviceIdType.MESH


def flip(index, mask):
    bit = 1
    while bit <= mask:
        if mask & bit:
            index = index + bit - 2 * bit * ((index // bit) % 2)
        bit *= 2
    return index


def differ(left, right, count):
    total, bit = 0, 1
    while bit < count:
        one, two = (left // bit) % 2, (right // bit) % 2
        total = total + bit * (one + two - 2 * one * two)
        bit *= 2
    return total


class Links:
    def __init__(self, send_sems, recv_sems):
        self.send_sems, self.recv_sems = send_sems, recv_sems
        self.number = 0
        self.all = []

    def plan(self, source, target, device):
        copy = pltpu.make_async_remote_copy(
            src_ref=source,
            dst_ref=target,
            send_sem=self.send_sems.at[self.number],
            recv_sem=self.recv_sems.at[self.number],
            device_id=device,
            device_id_type=MESH,
        )
        self.number += 1
        entry = [copy, False, False]
        self.all.append(entry)
        return entry

    def send(self, source, target, device):
        entry = self.plan(source, target, device)
        entry[0].start()
        return entry

    def arrived(self, entry):
        if not entry[1]:
            entry[0].wait_recv()
            entry[1] = True

    def left(self, entry):
        if not entry[2]:
            entry[0].wait_send()
            entry[2] = True

    def finish(self):
        for entry in self.all:
            self.arrived(entry)
            self.left(entry)


def greet(me, column, masks_dp, masks_z):
    barrier = pltpu.get_barrier_semaphore()
    for mask in masks_dp:
        pl.semaphore_signal(barrier, inc=1, device_id={"dp": flip(me, mask)}, device_id_type=MESH)
    for mask in masks_z:
        pl.semaphore_signal(
            barrier, inc=1, device_id={"mlp": flip(column, mask)}, device_id_type=MESH
        )
    pl.semaphore_wait(barrier, len(masks_dp) + len(masks_z))


class Reduce:
    def __init__(self, links, own, land, me, replicas, pieces):
        self.links, self.own, self.land = links, own, land
        self.me, self.replicas, self.pieces = me, replicas, pieces
        self.first, self.second = [], []

    def start(self):
        for number, (first, size) in enumerate(self.pieces):
            where = pl.ds(first, size)
            device = lambda at: {"dp": flip(self.me, at << 1)}
            near, far = (1, 2) if number % 2 == 0 else (2, 1)
            if self.replicas == 4:
                moves = [(near, 0, near), (3, 1, near)]
            else:
                moves = [(at, at - 1, at) for at in range(1, self.replicas)]
            self.first.append(
                [
                    self.links.send(
                        self.own.at[at, where, :], self.land.at[to, where, :], device(over)
                    )
                    for at, to, over in moves
                ]
            )
            if self.replicas == 4:
                self.second.append(
                    self.links.plan(
                        self.own.at[far, where, :], self.land.at[2, where, :], device(far)
                    )
                )

    def middle(self, number):
        if self.replicas != 4:
            return
        first, size = self.pieces[number]
        rows = slice(first, first + size)
        far = 2 if number % 2 == 0 else 1
        for entry in self.first[number]:
            self.links.arrived(entry)
        self.own[far, rows, :] = (
            self.own[far, rows, :].astype(F32) + self.land[1, rows, :].astype(F32)
        ).astype(BF16)
        self.second[number][0].start()

    def total(self, number):
        first, size = self.pieces[number]
        rows = slice(first, first + size)
        for entry in self.first[number] + (self.second[number : number + 1]):
            self.links.arrived(entry)
        value = self.own[0, rows, :].astype(F32)
        for at in range(self.replicas - 1):
            if self.replicas != 4 or at != 1:
                value = value + self.land[at, rows, :].astype(F32)
        return value

    def left(self):
        for entry in sum(self.first, []) + self.second:
            self.links.left(entry)


class Spread:
    def __init__(self, links, slab, me, count, rows, first, size, backward, pairs=True):
        self.links, self.slab, self.me, self.pairs = links, slab, me, pairs
        self.rows, self.first, self.size = rows, first, size
        self.bits = [1 << i for i in range(1, count.bit_length() - 1)]
        if backward:
            self.bits = self.bits[::-1]
        self.came = {}
        self.order = []

    def part(self, at):
        place = at if self.pairs else at // 2
        return self.slab.at[pl.ds(place * self.rows + self.first, self.size)]

    def forward(self, at, step, source=None):
        source = self.part(at) if source is None else source
        for later in range(step, len(self.bits)):
            bit = self.bits[later]
            entry = self.links.send(source, self.part(at ^ bit), {"dp": flip(self.me, bit)})
            self.came[at ^ bit] = (entry, later + 1)
            self.order.append(at ^ bit)
        if self.pairs:
            self.links.send(source, self.part(at ^ 1), {"dp": flip(self.me, 1)})

    def relay(self):
        while self.order:
            at = min(self.order, key=lambda index: (self.came[index][1], index.bit_count()))
            self.order.remove(at)
            entry, step = self.came[at]
            self.links.arrived(entry)
            self.forward(at, step)


def attn_unit(column, rank, place):
    by_columns = (place // 2) * 8 + 2 * rank + place % 2
    by_rows = (2 * rank + place // 8) * 8 + place % 8
    return jnp.where(column == 3, by_rows, by_columns)


def ff_unit(core, place):
    later = place - 32
    up = 64 + (place // 4) * 8 + core * 4 + place % 4
    down = 128 + (core * 4 + later // 8) * 8 + later % 8
    return jnp.where(place < 32, up, down)


def erf_f32(value):
    value = jnp.clip(value, -3.832506856900711, 3.832506856900711)
    square = value * value
    top = jnp.full_like(square, 0.00022905065861350646)
    for coeff in (
        0.0034082910107109506,
        0.050955695062380861,
        0.18520832239976145,
        1.128379143519084,
    ):
        top = top * square + coeff
    low = jnp.full_like(square, -1.1791602954361697e-7)
    for coeff in (
        0.000023547966471313185,
        0.0010179625278914885,
        0.014070470171167667,
        0.11098505178285362,
        0.49746925110067538,
        1.0,
    ):
        low = low * square + coeff
    return value * top / low


def row_sum(value):
    return dot_nn(jnp.ones((16, value.shape[0]), BF16), value)[0:1, :]


def transpose_tile(value):
    return jnp.swapaxes(value, 0, 1)


def layer_kernel(slots, devices, *refs):
    refs = list(refs)
    take = lambda number: [refs.pop(0) for _ in range(number)]
    norm_ref, hidden_ref, table, tokens, cot_ref, masters, tile_ref = take(7)
    mine, across, slab, attn_parts, z_ff, reduced = take(6)
    weights, table_ref, own_attn, send_attn, send_ff = take(5)
    h_all, c_all, out_acc, back_acc = take(4)
    tiles, weight_a, weight_b, acc_a, acc_b = take(5)
    q_all, k_all, v_all, g_all, o_all, dq_all, dk_all, dv_all = take(8)
    dw, own_land, attn_land, core_land = take(4)
    own_sum, attn_keep, attn_send, attn_back, z_send, z_land, block_all = take(7)
    vec, vec_land, vec_sum = take(3)
    local_sems, tile_sems, slot_sems, send_sems, recv_sems = take(5)
    me, column = lax.axis_index("dp"), lax.axis_index("mlp")
    replicas = devices // 2
    core, quarter = me % 2, me // 2
    rank = 2 * (column % 2) + core
    length, width = h_all.shape[1:]
    hidden = 4 * TILE
    wide = 4 * HDIM
    up, up_acc = weight_a.at[:, 0:hidden], acc_a.at[:, 0:hidden]
    down, down_acc = weight_b, acc_b
    w_in, in_acc = weight_a, acc_a
    w_out, proj_acc = weight_b.at[0:wide, :], acc_b.at[0:wide, :]
    rows_ff, rows_attn = 64 * TILE // replicas, 16 * TILE // replicas
    links = Links(send_sems, recv_sems)
    greet(me, column, [1] + [at << 1 for at in range(1, replicas)], [1, 2, 3])

    stage = [pltpu.make_async_copy(tokens, acc_b, local_sems.at[8])]
    places = []
    for slot in range(slots):
        place = acc_a.at[pl.ds(slot // 6 * TILE, TILE), pl.ds(slot % 6 * TILE, TILE)]
        places.append(place)
        stage.append(pltpu.make_async_copy(masters.at[slot], place, slot_sems.at[slot]))
    for copy in stage[1:] + stage[:1]:
        copy.start()
    for slot in range(slots):
        stage[1 + slot].wait()
        weights[slot] = places[slot][...].astype(BF16)
    cut = slots // 2
    spreads = [
        Spread(links, weights, me, devices, slots, 0, cut, False),
        Spread(links, weights, me, devices, slots, cut, slots - cut, True),
    ]
    for spread in spreads:
        spread.forward(0, 0)
    gathered = list(links.all)

    def normalize(step, carry):
        where = pl.ds(pl.multiple_of(step * TILE, TILE), TILE)
        value = acc_b[where, :]
        value = value - jnp.mean(value, axis=-1, keepdims=True)
        value = value * lax.rsqrt(jnp.mean(value * value, axis=-1, keepdims=True) + eps_norm)
        h_all[0, where, :] = value.astype(BF16)
        return carry

    stage[0].wait()
    lax.fori_loop(0, length // TILE, normalize, 0)
    copy = pltpu.make_async_copy(cot_ref, acc_b, local_sems.at[7])
    copy.start()
    along = []

    def send_along(target, where):
        entry = links.send(
            target.at[0, where, :], target.at[2, where, :], {"mlp": flip(column, 1)}
        )
        along.append((target, where, entry))

    table_ref[0] = table[...]
    early = length * 5 // 8
    send_along(h_all, pl.ds(0, length))
    send_along(table_ref, pl.ds(0, ROT))
    copy.wait()
    c_all[0] = acc_b[...].astype(BF16)
    send_along(c_all, pl.ds(0, early))
    core_blocks = [
        links.send(target.at[0], target.at[1], {"dp": flip(me, 1)})
        for target in (h_all, table_ref, c_all)
    ]
    number = len(links.all)
    for spread in spreads:
        spread.relay()
    gathered += links.all[number:]
    for entry in gathered:
        links.arrived(entry)

    def fill(out_ref, base, rows_out, first_row, unit_of):
        size = min(TILE, rows_out)

        def body(step, carry):
            row = first_row + step * size
            tile = tile_ref[unit_of(row // TILE)]
            where = pl.ds(pl.multiple_of(base + step * size, size), size)
            if size == TILE:
                out_ref[where, :] = weights[tile]
            else:
                out_ref[where, :] = weights[tile, pl.ds(pl.multiple_of(row % TILE, size), size), :]
            return carry

        lax.fori_loop(0, rows_out // size, body, 0)

    low = column % 2
    attn_came_z = []
    for bit in (3, 2, 1):
        fill(
            send_attn,
            (bit - 1) * rows_attn,
            rows_attn,
            quarter * rows_attn,
            functools.partial(attn_unit, column, 2 * (flip(low, 1) if bit & 1 else low) + core),
        )
        piece = pl.ds((bit - 1) * rows_attn, rows_attn)
        attn_came_z.append(
            links.send(
                send_attn.at[piece, :], attn_parts.at[piece, :], {"mlp": flip(column, bit)}
            )
        )
    send_along(c_all, pl.ds(early, length - early))
    fill(send_ff, 0, rows_ff, quarter * rows_ff, functools.partial(ff_unit, core))
    came_ff = [links.send(send_ff, z_ff.at[0], {"mlp": flip(column, 2)})]
    fill(tiles, 0, 64 * TILE, 0, functools.partial(ff_unit, core))
    fill(own_attn, 0, 16 * TILE, 0, functools.partial(attn_unit, column, rank))
    vec[...] = jnp.zeros_like(vec)

    def set_ff_weights():
        for at in range(32):
            up[
                (at // 4) * TILE : (at // 4 + 1) * TILE, (at % 4) * TILE : (at % 4 + 1) * TILE
            ] = tiles[at * TILE : (at + 1) * TILE, :]
            down[
                (at // 8) * TILE : (at // 8 + 1) * TILE, (at % 8) * TILE : (at % 8 + 1) * TILE
            ] = tiles[(32 + at) * TILE : (33 + at) * TILE, :]
        up_acc[...] = jnp.zeros((width, hidden), F32)
        down_acc[...] = jnp.zeros((hidden, width), F32)

    def ff_block(at, ff_column, first, store):
        hat = h_all[at].astype(F32)
        normed = (hat * norm_ref[2:3, :] + norm_ref[3:4, :]).astype(BF16)
        cot = c_all[at]
        pre = dot_nn(normed, up[...]) + hidden_ref[pl.ds(2 * ff_column + core, 1), :]
        cdf = 0.5 + 0.5 * erf_f32(pre * 0.7071067811865476)
        act = (pre * cdf).astype(BF16)
        grad = dot_nt(cot, down[...])
        grad = grad * (cdf + pre * (jnp.exp(-0.5 * pre * pre) * 0.3989422804014327))
        grad = grad.astype(BF16)
        where = pl.ds(pl.multiple_of(core * hidden, hidden), hidden)
        vec[pl.ds(8 + ff_column, 1), where] += row_sum(grad)
        out = dot_nn(act, down[...])
        back = dot_nt(grad, up[...])
        vec[2:3, :] += jnp.sum(back * hat, axis=0, keepdims=True)
        vec[3:4, :] += jnp.sum(back, axis=0, keepdims=True)
        back = back * norm_ref[2:3, :]
        if not first:
            out = out + out_acc[at].astype(F32)
            back = back + back_acc[at].astype(F32)
        store(out, back)
        up_acc[...] += dot_tn(normed, grad)
        down_acc[...] += dot_tn(act, cot)

    def store_ff(target):
        per = rows_ff // TILE
        for at in range(64):
            if at < 32:
                tile = up_acc[
                    (at // 4) * TILE : (at // 4 + 1) * TILE, (at % 4) * TILE : (at % 4 + 1) * TILE
                ]
            else:
                low = at - 32
                tile = down_acc[
                    (low // 8) * TILE : (low // 8 + 1) * TILE,
                    (low % 8) * TILE : (low % 8 + 1) * TILE,
                ]
            target[
                differ(at // per, quarter, replicas), (at % per) * TILE : (at % per + 1) * TILE, :
            ] = tile.astype(BF16)

    def attn_rows(matrix):
        return pl.multiple_of(matrix * (16 * TILE), TILE)

    def attn_rows(matrix):
        return pl.multiple_of(matrix * (16 * TILE), TILE)

    set_ff_weights()
    vec[7:8, :] = row_sum(c_all[0])

    def own_block(at):
        def store(out, back):
            out_acc[at] = out.astype(BF16)
            back_acc[at] = back.astype(BF16)

        ff_block(at, column, True, store)

    own_block(0)
    spreads = []
    for number, entry in enumerate(attn_came_z[::-1]):
        links.arrived(entry)
        pieces = [(number * rows_attn, rows_attn, number == 1)]
        if number == 2:
            cut = rows_attn // 32 * 16
            pieces = [
                (2 * rows_attn, cut, False),
                (2 * rows_attn + cut, rows_attn - cut, True),
            ]
        for first, size, backward in pieces:
            spreads.append(
                Spread(links, attn_parts, me, devices, 3 * rows_attn, first, size, backward, False)
            )
            spreads[-1].forward(0, 0)
    for entry in core_blocks:
        links.arrived(entry)
    own_block(1)
    for target, where, entry in along:
        links.arrived(entry)
        core_blocks.append(
            links.send(target.at[2, where, :], target.at[3, where, :], {"dp": flip(me, 1)})
        )
    for spread in spreads:
        spread.relay()
    gathered = links.all[:]
    own_block(2)
    for entry in core_blocks:
        links.arrived(entry)
    own_block(3)
    store_ff(dw)
    own_reduce = Reduce(
        links, dw, own_land, me, replicas, [(0, rows_ff // 2), (rows_ff // 2, rows_ff // 2)]
    )
    own_reduce.start()
    links.arrived(came_ff[0])
    relays = []
    if replicas == 4:
        for near, far, first in ((1, 2, 0), (2, 1, rows_ff // 2)):
            where = pl.ds(first, rows_ff // 2)
            for at in (near, far):
                came_ff.append(
                    links.send(
                        z_ff.at[0, where, :], z_ff.at[at, where, :], {"dp": flip(me, at << 1)}
                    )
                )
            relays.append(
                (
                    came_ff[-2],
                    links.plan(
                        z_ff.at[near, where, :], z_ff.at[3, where, :], {"dp": flip(me, far << 1)}
                    ),
                )
            )
            came_ff.append(relays[-1][1])
    else:
        for at in range(1, replicas):
            came_ff.append(links.send(z_ff.at[0], z_ff.at[at], {"dp": flip(me, at << 1)}))

    def between(at):
        @pl.when(at == 1)
        def _():
            for number in range(2):
                own_reduce.middle(number)

        @pl.when(at == 2)
        def _():
            for entry, copy in relays:
                links.arrived(entry)
                copy[0].start()

    for entry in gathered:
        links.arrived(entry)
    tile_loads = [
        pltpu.make_async_copy(
            own_attn, tiles.at[pl.ds(attn_rows(column), 16 * TILE), :], tile_sems.at[0]
        )
    ]
    for at in range(replicas):
        for bit in (1, 2, 3):
            first = attn_rows(flip(column, bit)) + differ(at, quarter, replicas) * rows_attn
            tile_loads.append(
                pltpu.make_async_copy(
                    attn_parts.at[pl.ds((3 * at + bit - 1) * rows_attn, rows_attn), :],
                    tiles.at[pl.ds(pl.multiple_of(first, rows_attn), rows_attn), :],
                    tile_sems.at[len(tile_loads)],
                )
            )
    for copy in tile_loads:
        copy.start()
    for copy in tile_loads:
        copy.wait()
    for matrix in range(3):
        for at in range(16):
            row = (16 * matrix + at) * TILE
            w_in[
                (at // 2) * TILE : (at // 2 + 1) * TILE,
                (2 * matrix + at % 2) * TILE : (2 * matrix + at % 2 + 1) * TILE,
            ] = tiles[row : row + TILE, :]
    for at in range(16):
        w_out[(at // 8) * TILE : (at // 8 + 1) * TILE, (at % 8) * TILE : (at % 8 + 1) * TILE] = (
            tiles[(48 + at) * TILE : (49 + at) * TILE, :]
        )
    in_acc[...] = jnp.zeros((width, 3 * wide), F32)
    proj_acc[...] = jnp.zeros((wide, width), F32)
    half = ROT // 2
    block = BLOCK
    scale = HDIM ** (-0.5)
    lane = lax.broadcasted_iota(jnp.int32, (1, LANES), 1)
    within = lane % HDIM
    keep_low = lane < HDIM
    wave = lax.broadcasted_iota(jnp.int32, (ROT, LANES), 0)
    spot = lax.broadcasted_iota(jnp.int32, (ROT, LANES), 1) % HDIM
    pick_cos = ((spot < ROT) & (wave == spot % half)).astype(F32)
    pick_first = ((spot < half) & (wave == half + spot)).astype(F32)
    pick_second = ((spot >= half) & (spot < ROT) & (wave == spot)).astype(F32)
    plain = (within >= ROT).astype(F32)

    def attn_block(at, carry):
        hat = h_all[at].astype(F32)
        normed = (hat * norm_ref[0:1, :] + norm_ref[1:2, :]).astype(BF16)
        cot = c_all[at]
        table = table_ref[at]
        cos_w = precise(table, pick_cos, 0, 0) + plain
        sin_a = precise(table, pick_first, 0, 0)
        sin_b = precise(table, pick_second, 0, 0)
        proj = dot_nn(normed, w_in[...])
        g_all[...] = dot_nt(cot, w_out[...]).astype(BF16)

        def turn(value):
            return (
                value * cos_w
                - pltpu.roll(value, LANES - half, 1) * sin_a
                + pltpu.roll(value, half, 1) * sin_b
            )

        for pair in range(2):
            cols = slice(pair * LANES, (pair + 1) * LANES)
            where = pl.ds(pl.multiple_of(rank * wide + pair * LANES, LANES), LANES)
            query = proj[:, pair * LANES : (pair + 1) * LANES] + norm_ref[4:5, where]
            key = proj[:, wide + pair * LANES : wide + (pair + 1) * LANES] + norm_ref[5:6, where]
            value = proj[:, 2 * wide + pair * LANES : 2 * wide + (pair + 1) * LANES]
            q_all[:, cols] = (turn(query).astype(BF16) * scale).astype(BF16)
            k_all[:, cols] = turn(key).astype(BF16)
            v_all[:, cols] = (value + norm_ref[6:7, where]).astype(BF16)
        zero = jnp.zeros((), BF16)
        for pair in range(2):
            cols = slice(pair * LANES, (pair + 1) * LANES)
            query, key = q_all[:, cols], k_all[:, cols]
            value, grad = v_all[:, cols], g_all[:, cols]
            key_t, value_t = transpose_tile(key), transpose_tile(value)
            out_t, dq_t = [], []
            dk_all[:, cols] = jnp.zeros((length, LANES), F32)
            dv_all[:, cols] = jnp.zeros((length, LANES), F32)
            for head in range(2):
                mask = keep_low if head == 0 else jnp.logical_not(keep_low)
                key_m, value_m = jnp.where(mask, key, zero), jnp.where(mask, value, zero)
                query_m, grad_m = jnp.where(mask, query, zero), jnp.where(mask, grad, zero)
                part = slice(head * HDIM, (head + 1) * HDIM)
                out_row, dq_row = [], []
                for first in range(0, length, block):
                    last = first + block
                    scores = dot_nt(key_m[:last], query[first:last])
                    key_at = lax.broadcasted_iota(jnp.int32, scores.shape, 0)
                    query_at = first + lax.broadcasted_iota(jnp.int32, scores.shape, 1)
                    scores = jnp.where(key_at <= query_at, scores, -1e30)
                    peak = jnp.max(scores, axis=0, keepdims=True)
                    raised = jnp.exp(scores - peak)
                    prob = raised * (1.0 / jnp.sum(raised, axis=0, keepdims=True))
                    prob_low = prob.astype(BF16)
                    grad_prob = dot_nt(value_m[:last], grad[first:last])
                    delta = jnp.sum(prob * grad_prob, axis=0, keepdims=True)
                    grad_scores = (prob * (grad_prob - delta)).astype(BF16)
                    out_row.append(dot_nn(value_t[part, :last], prob_low))
                    dq_row.append(dot_nn(key_t[part, :last], grad_scores))
                    dv_all[:last, cols] += dot_nn(prob_low, grad_m[first:last])
                    dk_all[:last, cols] += dot_nn(grad_scores, query_m[first:last])
                out_t.append(jnp.concatenate(out_row, axis=1))
                dq_t.append(jnp.concatenate(dq_row, axis=1))
            o_all[:, cols] = transpose_tile(jnp.concatenate(out_t, axis=0)).astype(BF16)
            dq_all[:, cols] = transpose_tile(jnp.concatenate(dq_t, axis=0)) * scale

        def turn_back(value):
            return (
                value * cos_w
                + pltpu.roll(value, LANES - half, 1) * sin_a
                - pltpu.roll(value, half, 1) * sin_b
            ).astype(BF16)

        pieces = [turn_back(dq_all[:, 0:LANES]), turn_back(dq_all[:, LANES : 2 * LANES])]
        pieces += [turn_back(dk_all[:, 0:LANES]), turn_back(dk_all[:, LANES : 2 * LANES])]
        pieces += [dv_all[...].astype(BF16)]
        grads = jnp.concatenate(pieces, axis=1)
        sums = row_sum(grads)
        where = pl.ds(pl.multiple_of(rank * wide, LANES), wide)
        for matrix in range(3):
            vec[4 + matrix : 5 + matrix, where] += sums[:, matrix * wide : (matrix + 1) * wide]
        out = dot_nn(o_all[...], w_out[...])
        out_acc[at] = (out_acc[at].astype(F32) + out).astype(BF16)
        back = dot_nt(grads, w_in[...])
        vec[0:1, :] += jnp.sum(back * hat, axis=0, keepdims=True)
        vec[1:2, :] += jnp.sum(back, axis=0, keepdims=True)
        back_acc[at] = (back_acc[at].astype(F32) + back * norm_ref[0:1, :]).astype(BF16)
        in_acc[...] += dot_tn(normed, grads)
        proj_acc[...] += dot_tn(o_all[...], cot)
        between(at)
        return carry

    lax.fori_loop(0, 4, attn_block, 0)
    for number, (first, count) in enumerate(own_reduce.pieces):
        own_sum[first : first + count, :] = own_reduce.total(number)
    own_reduce.left()
    size = min(TILE, rows_attn)
    for matrix in range(4):
        for at in range(16):
            for piece in range(TILE // size):
                row = at * TILE + piece * size
                if matrix < 3:
                    top, left = (at // 2) * TILE, (2 * matrix + at % 2) * TILE
                    tile = in_acc[top + piece * size : top + (piece + 1) * size, left : left + TILE]
                else:
                    top, left = (at // 8) * TILE, (at % 8) * TILE
                    tile = proj_acc[
                        top + piece * size : top + (piece + 1) * size, left : left + TILE
                    ]
                inner = row % rows_attn
                dw[
                    differ(row // rows_attn, quarter, replicas),
                    pl.ds(
                        pl.multiple_of(flip(column, matrix) * rows_attn + inner, size), size
                    ),
                    :,
                ] = tile.astype(BF16)
    attn_reduce = Reduce(
        links, dw, attn_land, me, replicas, [(0, 2 * rows_attn), (2 * rows_attn, 2 * rows_attn)]
    )
    attn_reduce.start()

    other = flip(column, 2)
    for entry in came_ff:
        links.arrived(entry)
    tile_loads = []
    for at in range(replicas):
        first = pl.multiple_of(differ(at, quarter, replicas) * rows_ff, TILE)
        tile_loads.append(
            pltpu.make_async_copy(
                z_ff.at[at], tiles.at[pl.ds(first, rows_ff), :], tile_sems.at[at]
            )
        )
    for copy in tile_loads:
        copy.start()
    for copy in tile_loads:
        copy.wait()
    set_ff_weights()
    core_came = {}
    outs = []
    waiting = []

    def pump(count):
        for number, source, where in waiting[:count]:
            links.send(
                source.at[2, where, :], across.at[number, where, :], {"mlp": flip(column, 1)}
            )
        del waiting[:count]

    def send_core(at):
        def store(out, back):
            out_acc[at] = out.astype(BF16)
            back_acc[at] = back.astype(BF16)
            for number, source in ((0, out_acc), (1, back_acc)):
                core_came[number, at // 2] = links.send(
                    source.at[at], core_land.at[number, at // 2], {"dp": flip(me, 1)}
                )

        return store

    def keep(at):
        def store(out, back):
            for number, value, source in ((0, out, out_acc), (1, back, back_acc)):
                links.arrived(core_came[number, at // 2])
                value = value + core_land[number, at // 2].astype(F32)
                source[at] = value.astype(BF16)
                if at == 0:
                    copy = pltpu.make_async_copy(
                        source.at[at], mine.at[number], local_sems.at[number]
                    )
                    copy.start()
                    outs.append(copy)
                else:
                    for first in range(0, length, length // 4):
                        waiting.append((number, source, pl.ds(first, length // 4)))

        return store

    for at in (3, 2, 1, 0):
        ff_block(at, other, False, send_core(at) if at % 2 else keep(at))
        pump(1)
        if at == 2:
            for number in range(2):
                attn_reduce.middle(number)
    attn_total = [attn_reduce.total(number) for number in range(2)]
    attn_keep[...] = attn_total[0][0:rows_attn]
    attn_send[0:rows_attn, :] = attn_total[0][rows_attn : 2 * rows_attn].astype(BF16)
    attn_send[rows_attn : 3 * rows_attn, :] = attn_total[1].astype(BF16)
    attn_reduce.left()

    store_ff(dw)
    chunks = 4
    size = rows_ff // chunks
    other_reduce = Reduce(
        links, dw, own_land, me, replicas, [(chunk * size, size) for chunk in range(chunks)]
    )
    other_reduce.start()
    vec_came = [
        links.send(vec, vec_land.at[bit], {"mlp": flip(column, bit)}) for bit in (1, 2, 3)
    ]
    back_came = []
    for bit in (1, 2, 3):
        piece = pl.ds((bit - 1) * rows_attn, rows_attn)
        back_came.append(
            links.send(attn_send.at[piece, :], attn_back.at[bit - 1], {"mlp": flip(column, bit)})
        )
    pump(1)
    rows = slots * TILE
    spreads = []

    def publish(first, count):
        backward = len(spreads) % 2 == 1
        spread = Spread(links, slab, me, devices, rows, first, count, backward)
        source = block_all.at[pl.ds(first, count), :]
        spread.forward(0, 0, source)
        copy = pltpu.make_async_copy(source, spread.part(0), local_sems.at[2 + len(spreads)])
        copy.start()
        outs.append(copy)
        spreads.append(spread)

    def add_chunk(chunk):
        piece = slice(chunk * size, (chunk + 1) * size)
        z_send[piece, :] = other_reduce.total(chunk).astype(BF16)
        where = pl.ds(chunk * size, size)
        return links.send(z_send.at[where, :], z_land.at[where, :], {"mlp": flip(column, 2)})

    for entry in vec_came:
        links.arrived(entry)
    vec_sum[0] = (vec[...] + vec_land[1]) + (vec_land[2] + vec_land[3])
    vec_core = links.send(vec_sum.at[0], vec_land.at[0], {"dp": flip(me, 1)})
    other_reduce.middle(0)
    pump(1)
    for entry in back_came:
        links.arrived(entry)
    block_all[rows_ff : rows_ff + rows_attn, :] = (
        attn_keep[...] + attn_back[1].astype(F32)
    ).astype(BF16)
    publish(rows_ff, rows_attn)
    block_all[rows_ff + rows_attn : rows, :] = (
        attn_back[0].astype(F32) + attn_back[2].astype(F32)
    ).astype(BF16)
    publish(rows_ff + rows_attn, rows_attn)
    links.arrived(vec_core)
    vec_sum[1] = vec_sum[0] + vec_land[0]
    vec_came = [
        links.send(vec_sum.at[1], vec_land.at[3 + at], {"dp": flip(me, at << 1)})
        for at in range(1, replicas)
    ]
    for chunk in range(1, chunks):
        other_reduce.middle(chunk)
    z_came = []
    for chunk in range(chunks):
        z_came.append(add_chunk(chunk))
        pump(1)
    for spread in spreads[:2]:
        spread.relay()
    for chunk in range(chunks):
        links.arrived(z_came[chunk])
        piece = slice(chunk * size, (chunk + 1) * size)
        block_all[piece, :] = (own_sum[piece, :] + z_land[piece, :].astype(F32)).astype(BF16)
        publish(chunk * size, size)
        pump(1)
        if chunk > 0:
            spreads[1 + chunk].relay()
    pump(len(waiting))
    spreads[1 + chunks].relay()
    for entry in vec_came:
        links.arrived(entry)
    values = [vec_sum[1]] + [vec_land[3 + at] for at in range(1, replicas)]
    while len(values) > 1:
        values = [values[i] + values[i + 1] for i in range(0, len(values), 2)]
    reduced[...] = values[0]
    for copy in outs:
        copy.wait()
    links.finish()


BLOCK = 512


def layer(vectors, hidden_bias, table, tokens, cot, masters, tile_row):
    length, width = tokens.shape
    slots = masters.shape[0]
    devices = lax.axis_size("dp")
    replicas = devices // 2
    hidden = 4 * TILE
    wide = 4 * HDIM
    rows = slots * TILE
    rows_ff, rows_attn = 64 * TILE // replicas, 16 * TILE // replicas
    count = 2 * (2 * replicas - 1) + 11 + 3 + 4 * (replicas - 1)
    count += 1 + 2 * (replicas - 1) + 4 + 8 + 8 * (replicas - 1) + 3 + 3 + 4 + 1 + replicas - 1
    count += 6 * (2 * replicas - 1)
    vmem = lambda *shape: pltpu.VMEM(shape, BF16)
    vmem32 = lambda *shape: pltpu.VMEM(shape, F32)
    return pl.pallas_call(
        functools.partial(layer_kernel, slots, devices),
        out_shape=[
            jax.ShapeDtypeStruct((2, length, width), BF16),
            jax.ShapeDtypeStruct((2, length, width), BF16),
            jax.ShapeDtypeStruct((devices * rows, LANES), BF16),
            jax.ShapeDtypeStruct((replicas * 3 * rows_attn, LANES), BF16),
            jax.ShapeDtypeStruct((replicas, rows_ff, LANES), BF16),
            jax.ShapeDtypeStruct((12, width), F32),
        ],
        in_specs=[VMEM] * 3 + [ANY] * 3 + [SMEM],
        out_specs=[ANY] * 5 + [VMEM],
        scratch_shapes=[
            vmem(devices * slots, TILE, LANES),
            vmem32(4, ROT, length),
            vmem(16 * TILE, LANES),
            vmem(3 * rows_attn, LANES),
            vmem(rows_ff, LANES),
            vmem(4, length, width),
            vmem(4, length, width),
            vmem(4, length, width),
            vmem(4, length, width),
            vmem(64 * TILE, LANES),
            vmem(width, 3 * wide),
            vmem(hidden, width),
            vmem32(width, 3 * wide),
            vmem32(hidden, width),
            vmem(length, wide),
            vmem(length, wide),
            vmem(length, wide),
            vmem(length, wide),
            vmem(length, wide),
            vmem32(length, wide),
            vmem32(length, wide),
            vmem32(length, wide),
            vmem(replicas, rows_ff, LANES),
            vmem(replicas - 1, rows_ff, LANES),
            vmem(replicas - 1, 4 * rows_attn, LANES),
            vmem(2, 2, length, width),
            vmem32(rows_ff, LANES),
            vmem32(rows_attn, LANES),
            vmem(3 * rows_attn, LANES),
            vmem(3, rows_attn, LANES),
            vmem(rows_ff, LANES),
            vmem(rows_ff, LANES),
            vmem(rows, LANES),
            vmem32(12, width),
            vmem32(3 + replicas, 12, width),
            vmem32(2, 12, width),
            pltpu.SemaphoreType.DMA((9,)),
            pltpu.SemaphoreType.DMA((3 * replicas + 1,)),
            pltpu.SemaphoreType.DMA((slots,)),
            pltpu.SemaphoreType.DMA((count,)),
            pltpu.SemaphoreType.DMA((count,)),
        ],
        compiler_params=pltpu.CompilerParams(
            vmem_limit_bytes=63 << 20, collective_id=2, has_side_effects=True
        ),
        cost_estimate=pl.CostEstimate(
            flops=60 * 10**9, bytes_accessed=40 << 20, transcendentals=0
        ),
        name="layer",
    )(vectors, hidden_bias, table, tokens, cot, masters, tile_row)


def split(value):
    high = value.astype(BF16)
    return high, (value - high.astype(F32)).astype(BF16)


def soap_kernel(slots, replicas, per_step, *refs):
    refs = list(refs)
    take = lambda number: [refs.pop(0) for _ in range(number)]
    place_ref, owner_ref, slab = take(3)
    left_ref, right_ref, first_ref, second_ref, master_ref, ema_ref = take(6)
    token_refs = take(5)
    grad_ref, first_out, second_out, master_out, copy_out, ema_out = take(6)
    finish_block(*token_refs, *take(2))
    mine, inverse, sem = take(3)
    me, column = place_ref[0], place_ref[1]
    step = pl.program_id(0)
    bias_fix = 1.0 - 0.5**STEP
    rows_ff = 64 * TILE // replicas
    rows_attn = 16 * TILE // replicas
    rows_all = slots * TILE
    size = min(TILE, rows_attn)

    @pl.when(step == 0)
    def _():
        def note(unit, carry):
            inverse[owner_ref[unit]] = unit
            return carry

        lax.fori_loop(0, owner_ref.shape[0], note, 0)

        def fetch(number, carry):
            unit = inverse[me * slots + number]
            row, col = (unit % 64) // 8, unit % 8
            by_rows = column == 3
            rank = jnp.where(by_rows, row // 2, col // 2)
            attn_place = jnp.where(by_rows, (row % 2) * 8 + col, row * 2 + col % 2)
            up_place = row * 4 + col % 4
            down_place = 32 + (row % 4) * 8 + col
            is_attn, is_up = unit < 64, unit < 128
            core = jnp.where(is_attn, rank % 2, jnp.where(is_up, col // 4, row // 4))
            other = ((rank // 2) != (column % 2)).astype(jnp.int32)
            for piece in range(TILE // size):
                attn_row = attn_place * TILE + piece * size
                ff_row = jnp.where(is_up, up_place, down_place) * TILE + piece * size
                holder = jnp.where(is_attn, attn_row // rows_attn, ff_row // rows_ff)
                inner = jnp.where(
                    is_attn, rows_ff + other * rows_attn + attn_row % rows_attn, ff_row % rows_ff
                )
                start = ((holder * 2 + core) ^ me) * rows_all + inner
                pltpu.make_async_copy(
                    slab.at[pl.ds(pl.multiple_of(start, size), size), :],
                    mine.at[number, pl.ds(piece * size, size), :],
                    sem,
                ).start()
            return carry

        lax.fori_loop(0, slots, fetch, 0)
        pltpu.make_async_copy(mine, mine, sem).wait()

    every = range(per_step)
    grads = [mine[step * per_step + number] for number in every]
    left = [split(left_ref[number]) for number in every]
    right = [split(right_ref[number]) for number in every]
    twice = lambda value, axis: jnp.concatenate([value, value], axis=axis)
    both = lambda pair, axis: jnp.concatenate(pair, axis=axis)
    turned = [dot_tn(both(left[n], 0), twice(grads[n], 0)) for n in every]
    parts = [split(turned[n]) for n in every]
    turned = [
        dot_nn(parts[n][0], right[n][1]) + dot_nn(both(parts[n], 1), twice(right[n][0], 0))
        for n in every
    ]
    scaled = []
    for n in every:
        grad_ref[n] = grads[n].astype(F32)
        first = 0.5 * first_ref[n] + 0.5 * turned[n]
        second = 0.5 * second_ref[n] + 0.5 * turned[n] * turned[n]
        first_out[n] = first
        second_out[n] = second
        scaled.append(first / bias_fix / (jnp.sqrt(second / bias_fix) + eps_adam))
    parts = [split(scaled[n]) for n in every]
    back = [
        dot_nn(left[n][0], parts[n][1]) + dot_nn(both(left[n], 1), twice(parts[n][0], 0))
        for n in every
    ]
    parts = [split(back[n]) for n in every]
    back = [
        dot_nt(parts[n][0], right[n][1]) + dot_nt(both(parts[n], 1), twice(right[n][0], 1))
        for n in every
    ]
    for n in every:
        master = master_ref[n] - lr_matrix * back[n]
        master_out[n] = master
        copy_out[n] = master.astype(BF16)
        ema_out[n] = ema_keep * ema_ref[n] + (1.0 - ema_keep) * master


def soap(place, owner_row, slab, state, token_state, replicas):
    slots = state[0].shape[0]
    steps = STEPS if slots % STEPS == 0 else 1
    per_step = slots // steps
    length, width = token_state[0].shape
    one = pl.BlockSpec((length // steps, width), lambda i: (i, 0))
    two = pl.BlockSpec((2, length // steps, width), lambda i: (0, i, 0))
    whole = pl.BlockSpec(token_state[4].shape, lambda i: (0, 0))
    spec = pl.BlockSpec((per_step, TILE, TILE), lambda i: (i, 0, 0))
    shape = (slots, TILE, TILE)
    return pl.pallas_call(
        functools.partial(soap_kernel, slots, replicas, per_step),
        grid=(steps,),
        out_shape=[jax.ShapeDtypeStruct(shape, F32)] * 4
        + [jax.ShapeDtypeStruct(shape, BF16), jax.ShapeDtypeStruct(shape, F32)]
        + [jax.ShapeDtypeStruct((length, width), F32)] * 2,
        in_specs=[SMEM, SMEM, ANY] + [spec] * 6 + [one, one, two, two, whole],
        out_specs=[spec] * 6 + [one, one],
        scratch_shapes=[
            pltpu.VMEM(shape, BF16),
            pltpu.SMEM((owner_row.shape[0],), jnp.int32),
            pltpu.SemaphoreType.DMA,
        ],
        compiler_params=pltpu.CompilerParams(vmem_limit_bytes=60 << 20),
        cost_estimate=pl.CostEstimate(
            flops=24 * slots * 2 * TILE**3, bytes_accessed=20 << 20, transcendentals=0
        ),
        name="soap",
    )(place, owner_row, slab, *state, *token_state)


def finish_block(tokens, cot, mine, across, bias, result, grad_tokens):
    value = tokens[...]
    out = mine[0].astype(F32) + across[0].astype(F32)
    result[...] = value + (out + (bias[7:8, :] + bias[8:9, :]))
    value = value - jnp.mean(value, axis=-1, keepdims=True)
    inverse = lax.rsqrt(jnp.mean(value * value, axis=-1, keepdims=True) + eps_norm)
    hat = value * inverse
    grad = mine[1].astype(F32) + across[1].astype(F32)
    grad_tokens[...] = cot[...] + inverse * (
        grad
        - jnp.mean(grad, axis=-1, keepdims=True)
        - hat * jnp.mean(grad * hat, axis=-1, keepdims=True)
    )


STEPS = 4


def adam_step(grad, first, second, param):
    bias_fix = 1.0 - 0.5**STEP
    first_new = 0.5 * first + 0.5 * grad
    second_new = 0.5 * second + 0.5 * grad * grad
    return (
        first_new,
        second_new,
        param - lr_vector * (first_new / bias_fix) / (jnp.sqrt(second_new / bias_fix) + eps_adam),
    )


def local(
    tokens,
    cotangent,
    positions,
    owners,
    masters,
    basis_left,
    basis_right,
    moment1,
    moment2,
    ema,
    vectors,
    vector_moment1,
    vector_moment2,
    hidden_bias,
    hidden_moment1,
    hidden_moment2,
):
    length, width = tokens.shape
    slots = masters.shape[1]
    me = lax.axis_index("dp")
    column = lax.axis_index("mlp")
    replicas = lax.axis_size("dp") // 2
    place = jnp.stack([me, column, me // 2]).astype(jnp.int32)
    owner_row = owners[0]

    inverse_freq = 10000.0 ** (-(jnp.arange(ROT // 2, dtype=F32) * 2.0) / ROT)
    angles = inverse_freq[:, None] * positions.astype(F32)[None, :]
    table = jnp.concatenate([jnp.cos(angles), jnp.sin(angles)], axis=0)
    mine, across, slab, _, _, reduced = layer(
        vectors,
        hidden_bias.reshape(2 * GROUP, -1),
        table,
        tokens,
        cotangent,
        masters[0],
        (owner_row // slots ^ me) * slots + owner_row % slots,
    )
    state = [item[0] for item in (basis_left, basis_right, moment1, moment2, masters, ema)]
    token_state = [tokens, cotangent, mine, across, vectors]
    own_grad, first_new, second_new, master_new, weight_copy, ema_new, result, grad_tokens = soap(
        place, owner_row, slab, state, token_state, replicas
    )
    vector_grad = jnp.concatenate([reduced[:8], reduced[7:8]], axis=0)
    hidden_grad = reduced[8:].reshape(FF)
    vec_first, vec_second, vectors_new = adam_step(
        vector_grad, vector_moment1, vector_moment2, vectors
    )
    hid_first, hid_second, hidden_new = adam_step(
        hidden_grad, hidden_moment1, hidden_moment2, hidden_bias
    )
    return (
        result,
        grad_tokens,
        own_grad[None],
        first_new[None],
        second_new[None],
        master_new[None],
        weight_copy[None],
        ema_new[None],
        vector_grad,
        vec_first,
        vec_second,
        vectors_new,
        hidden_grad,
        hid_first,
        hid_second,
        hidden_new,
    )


def solution(mesh):
    split = P(("dp", "mlp"), None)
    tiled = P("mlp", "dp", None, None)
    return jax.shard_map(
        local,
        mesh=mesh,
        in_specs=(split, split, P(("dp", "mlp")), P("mlp", None)) + (tiled,) * 6 + (P(),) * 6,
        out_specs=(split, split) + (tiled,) * 6 + (P(),) * 8,
        check_vma=False,
    )
```
